128 devices in a mesh: row: 8 (over x, core), seq: 16 (over z, y).
Axes of the slice: x: 4, y: 4, z: 4, core: 2. Of those that a mesh axis runs over, the one named last changes fastest.
Arguments:
- tokens: bfloat16 [8, 2304, 512], P('row', 'seq'), may hold values from -6 to 6
- segment: int32 [8, 2304], P('row', 'seq'), may hold values from 0 to 2303, as said below
- w_qkv: bfloat16 [2, 512, 1536], replicated, may hold values from -0.25 to 0.25
- w_out: bfloat16 [2, 512, 512], replicated, may hold values from -1 to 1
- w_up: bfloat16 [2, 512, 2048], replicated, may hold values from -0.25 to 0.25
- w_down: bfloat16 [2, 2048, 512], replicated, may hold values from -0.125 to 0.125
- gains: bfloat16 [2, 2, 512], replicated, may hold values from 0.5 to 1.5
- cotangent: bfloat16 [8, 2304, 512], P('row', 'seq'), may hold values from -6 to 6
Outputs:
- output: bfloat16 [8, 2304, 512], P('row', 'seq')
- tokens_grad: float32 [8, 2304, 512], P('row', 'seq')
- w_qkv_grad: float32 [2, 512, 1536], replicated
- w_out_grad: float32 [2, 512, 512], replicated
- w_up_grad: float32 [2, 512, 2048], replicated
- w_down_grad: float32 [2, 2048, 512], replicated
- gains_grad: float32 [2, 2, 512], replicated
The draws below stay inside these ranges and needn't reach their ends.
Inputs may be any that keep to these rules, and one draw needn't show every extreme that they name: `segment`: along a row the document numbers never fall, so each document is a contiguous run of bytes; in one row drawn from the seed a document starts within the first 72 bytes and ends within the last 72.
All inputs are finite; a program needn't handle non-finite values.
Results may differ from the reference program's by a relative error of at most 0.017.
Values may be sent and summed in bfloat16 or wider, within the bound.
A program may use at most 192 MiB of HBM per device.

```python
import math
import jax
import jax.numpy as jnp
from jax import lax

D = 512
HEAD = 64
FF = 2048
STRETCH = 144
ROWS = 8
LENGTH = 2304
SHORT = 768


def draw_segment(key, part):
    key = jax.random.fold_in(key, 11)
    keys = jax.random.split(key, 5)
    picked = jax.random.randint(keys[0], (), 0, ROWS)
    shifts = jax.random.randint(keys[1], (ROWS, 1), 4, 11)
    period = jnp.left_shift(jnp.ones((ROWS, 1), jnp.int32), shifts)
    rolls = jax.random.randint(keys[2], (ROWS, LENGTH), 0, 1 << 20)
    boundary = (rolls % period == 0).astype(jnp.int32)
    boundary = boundary.at[:, 0].set(0)
    total = jnp.sum(boundary, axis=1, keepdims=True).astype(jnp.int32)
    ragged = (LENGTH - 1 - total + jnp.cumsum(boundary, axis=1)).astype(jnp.int32)
    start = jax.random.randint(keys[3], (), 1, STRETCH // 2 + 1)
    finish = jax.random.randint(keys[4], (), 1, STRETCH // 2 + 1)
    places = jnp.arange(LENGTH, dtype=jnp.int32)
    spanning = jnp.where(places < start, 0, jnp.where(places < LENGTH - finish, 1, 2)).astype(jnp.int32)
    row_ids = jnp.arange(ROWS, dtype=jnp.int32)[:, None]
    return jnp.where(row_ids == picked, spanning[None, :], ragged).astype(jnp.int32)


def levels(rng, extent, shards, low, high):
    def one(axis_at, shards_of):
        draws = jax.random.uniform(jax.random.fold_in(jax.random.fold_in(rng, 6), axis_at), (shards_of,), jnp.float32, low / len(shards), high / len(shards))
        return jnp.repeat(jnp.exp(draws), extent[axis_at] // shards_of).reshape((-1,) + (1,) * (len(extent) - axis_at - 1))

    level = one(*shards[0])
    for cut in shards[1:]:
        level = level * one(*cut)
    return level


def normal_values(rng, dims, scale, limit, cuts=(), kind=jnp.bfloat16):
    drawn = scale * jax.random.normal(rng, dims, jnp.float32)
    if cuts:
        drawn = drawn * levels(rng, dims, cuts, -0.22, 0.18)
    return jnp.clip(drawn, -limit, limit).astype(kind)


def setup_inputs(seed: int = 0) -> dict:
    arg_keys = jax.random.split(jax.random.key(seed), 9)
    return {
        "tokens": normal_values(arg_keys[0], (ROWS, LENGTH, D), 1.0, 6.0, ((0, 8), (1, 16))),
        "segment": draw_segment(jax.random.fold_in(arg_keys[8], 71), 0),
        "w_qkv": normal_values(arg_keys[2], (2, D, 3 * D), D ** -0.5, 0.25),
        "w_out": normal_values(arg_keys[3], (2, D, D), (D // 16) ** -0.5, 1.0),
        "w_up": normal_values(arg_keys[4], (2, D, FF), D ** -0.5, 0.25),
        "w_down": normal_values(arg_keys[5], (2, FF, D), FF ** -0.5, 0.125),
        "gains": jnp.clip(1.0 + 0.1 * jax.random.normal(arg_keys[6], (2, 2, D), jnp.float32), 0.5, 1.5).astype(jnp.bfloat16),
        "cotangent": normal_values(arg_keys[7], (ROWS, LENGTH, D), 1.0, 6.0, ((0, 8), (1, 16))),
    }


@jax.custom_vjp
def low(v):
    return lax.optimization_barrier(v.astype(jnp.bfloat16)).astype(jnp.float32)

@jax.custom_vjp
def low_back(v):
    return v

def low_keep(v):
    return (low(v), None)

def low_pass(kept, grad):
    return (grad,)

def back_keep(v):
    return (v, None)

def back_low(kept, grad):
    return (low(grad),)
low.defvjp(low_keep, low_pass)
low_back.defvjp(back_keep, back_low)

def product(left, right, form):
    return jnp.einsum(form, left, right, precision=lax.Precision.HIGHEST)

def layer_norm(values, gain):
    center = values - lax.optimization_barrier(jnp.mean(values, -1, keepdims=True))
    spread = lax.optimization_barrier(jnp.mean(center * center, -1, keepdims=True))
    return center * lax.rsqrt(spread + 1e-05) * gain

def rotate(tensor, positions, sign):
    row_count, length, width = tensor.shape
    split = tensor.reshape(row_count, length, width // HEAD, HEAD)
    half = HEAD // 2
    freq = 10000.0 ** (-jnp.arange(half, dtype=jnp.float32) / half)
    angle = positions.astype(jnp.float32)[:, None] * freq[None, :]
    cosine = jnp.cos(angle)[None, :, None, :]
    sine = jnp.sin(angle)[None, :, None, :]
    first = split[..., :half]
    second = split[..., half:]
    joined = jnp.concatenate([first * cosine - sign * second * sine, sign * first * sine + second * cosine], -1)
    return joined.reshape(row_count, length, width)

def attend_row(query, key, value, segment, positions):
    length, width = query.shape
    heads = width // HEAD
    block = math.gcd(length, 512)
    count = length // block
    key_heads = key.reshape(length, heads, HEAD)
    value_heads = value.reshape(length, heads, HEAD)

    def one_block(pieces):
        query_block, segment_block, position_block = pieces
        raw = low_back(product(query_block.reshape(block, heads, HEAD), key_heads, 'qhe,khe->hqk'))
        allowed = (positions[None, :] <= position_block[:, None]) & (segment[None, :] == segment_block[:, None])
        score = jnp.where(allowed[None], HEAD ** (-0.5) * raw, -1000000000.0)
        top = lax.optimization_barrier(jnp.max(score, -1, keepdims=True))
        expo = jnp.exp(score - top)
        prob = expo / lax.optimization_barrier(jnp.sum(expo, -1, keepdims=True))
        mixed = product(low(prob), value_heads, 'hqk,khe->qhe')
        return mixed.reshape(block, width)
    mixed = lax.map(jax.checkpoint(one_block), (query.reshape(count, block, width), segment.reshape(count, block), positions.reshape(count, block)))
    return mixed.reshape(length, width)

def block(values, segment, positions, w_qkv, w_out, w_up, w_down, gains):
    width = values.shape[2]
    normed = low(layer_norm(values, gains[0]))
    proj = low_back(product(normed, w_qkv, 'rsd,de->rse'))
    query = low(rotate(proj[..., :width], positions, 1.0))
    key = low(rotate(proj[..., width:2 * width], positions, 1.0))
    value = low(proj[..., 2 * width:])
    mixed = lax.map(lambda parts: attend_row(parts[0], parts[1], parts[2], parts[3], positions), (query, key, value, segment))
    mixed = low_back(low(mixed))
    first = values + low_back(product(mixed, w_out, 'rsd,de->rse'))
    normed_two = low(layer_norm(first, gains[1]))
    hidden = low_back(product(normed_two, w_up, 'rsd,df->rsf'))
    active = low(jax.nn.gelu(hidden, approximate=True))
    return first + low_back(product(active, w_down, 'rsf,fd->rsd'))

def reference(tokens, segment, w_qkv, w_out, w_up, w_down, gains, cotangent):
    row_count = tokens.shape[0]
    width = tokens.shape[2]

    def forward(inputs, qkv_all, out_all, up_all, down_all, gain_all):
        full_pos = jnp.arange(LENGTH, dtype=jnp.int32)
        second = block(inputs, segment, full_pos, qkv_all[0], out_all[0], up_all[0], down_all[0], gain_all[0])
        shifted = jnp.concatenate([jnp.zeros((row_count, 2, width), jnp.float32), second[:, :LENGTH - 2]], 1)
        pooled = lax.optimization_barrier(jnp.mean(shifted.reshape(row_count, SHORT, 3, width), 2))
        short_pos = jnp.arange(SHORT, dtype=jnp.int32)
        short = block(pooled, segment[:, ::3], short_pos, qkv_all[1], out_all[1], up_all[1], down_all[1], gain_all[1])
        return second + jnp.repeat(short, 3, axis=1)
    floats = (tokens.astype(jnp.float32), w_qkv.astype(jnp.float32), w_out.astype(jnp.float32), w_up.astype(jnp.float32), w_down.astype(jnp.float32), gains.astype(jnp.float32))
    result, pull = jax.vjp(forward, *floats)
    grads = pull(cotangent.astype(jnp.float32))
    return (result.astype(jnp.bfloat16), grads[0], grads[1], grads[2], grads[3], grads[4], grads[5])
```

```python
import types

import jax
import jax.numpy as jnp
import numpy as np
from jax import lax
from jax.experimental import pallas as pl
from jax.experimental.pallas import tpu as pltpu
from jax.sharding import PartitionSpec as P

MESH = pl.DeviceIdType.MESH
F32 = jnp.float32
BF16 = jnp.bfloat16

SEQ = 16
LONG = 144
SHORT = 48
D = 512
FF = 2048
GROUPS = 4
NOTE = 16
KV, Q, DM, MIX, DKV, DQ = range(6)
X, Y, Z = range(3)
ORDERS = ((X, Y, Z), (Y, Z, X), (Z, X, Y))


def dot(left, right):
    return jnp.dot(left, right, preferred_element_type=F32)


def dot_nt(left, right):
    return lax.dot_general(left, right, (((1,), (1,)), ((), ())), preferred_element_type=F32)


def dot_tn(left, right):
    return lax.dot_general(left, right, (((0,), (0,)), ((), ())), preferred_element_type=F32)


def lanes(shape):
    return lax.broadcasted_iota(jnp.int32, shape, len(shape) - 1)


def sublanes(shape):
    return lax.broadcasted_iota(jnp.int32, shape, len(shape) - 2)


def normalize(values):
    center = values - jnp.mean(values, -1, keepdims=True)
    scale = lax.rsqrt(jnp.mean(center * center, -1, keepdims=True) + 1e-05)
    return center * scale, scale


def normalize_back(grad, normal, scale, gain):
    inner = grad * gain
    return scale * (
        inner
        - jnp.mean(inner, -1, keepdims=True)
        - normal * jnp.mean(inner * normal, -1, keepdims=True)
    )


def half_turn(tensor):
    up = pltpu.roll(tensor, 96, 1)
    down = pltpu.roll(tensor, 32, 1)
    return jnp.where(lanes(tensor.shape) % 64 < 32, -up, down)


def padded(rows):
    return -(-rows // 32) * 16


def seal(packed):
    rows = packed.shape[0]
    return jnp.concatenate([packed, jnp.zeros((padded(2 * rows) - rows, 128), F32)], 0).astype(BF16)


def pack_pair(pair):
    rows = pair.shape[0] // 2
    top, bottom = pair[:rows], pltpu.roll(pair[rows:], 64, 1)
    low = lanes(top.shape) < 64
    return seal(jnp.where(low, top, bottom)), seal(jnp.where(low, bottom, top))


def unpack_pair(even, odd, rows):
    even, odd = even.astype(F32)[: rows // 2], odd.astype(F32)[: rows // 2]
    low = lanes(even.shape) < 64
    return jnp.concatenate([jnp.where(low, even, odd), pltpu.roll(jnp.where(low, odd, even), 64, 1)], 0)


def unpack_one(packed, rows):
    packed = packed.astype(F32)[: rows // 2]
    return jnp.concatenate([packed, pltpu.roll(packed, 64, 1)], 0).astype(BF16)


def spill(ref, first, values):
    for group in range(GROUPS):
        ref[group, first : first + values.shape[0], :] = values[:, 128 * group : 128 * group + 128]


def every_third(ref, first, group):
    return ref[group, pl.ds(first, SHORT, 3), :]


def remote(src, dst, send, recv, device):
    return pltpu.make_async_remote_copy(
        src_ref=src, dst_ref=dst, send_sem=send, recv_sem=recv, device_id=device, device_id_type=MESH
    )


class Place:
    def __init__(self):
        self.row = lax.axis_index("row")
        self.seq = lax.axis_index("seq")
        self.core = lax.rem(self.row, 2)
        self.at = (self.row // 2, lax.rem(self.seq, 4), self.seq // 4)
        self.head = lax.rem(self.seq, 8)
        self.same = (self.seq // 8 == self.core) & (lax.rem(self.seq, 2) == self.core)
        self.sending, self.coming = [], {}

    def peer(self, axis, distance):
        to = lax.rem(self.at[axis] + distance, 4)
        if axis == X:
            return (to * 2 + self.core, self.seq)
        if axis == Y:
            return (self.row, self.at[Z] * 4 + to)
        return (self.row, to * 4 + self.at[Y])

    def partner(self):
        return (self.row + 1 - 2 * self.core, self.seq)

    def along(self, distance):
        return (self.row, lax.rem(self.seq + distance, SEQ))

    def holder(self, head):
        device = (2 * self.at[X] + lax.rem(self.seq, 2), 8 * self.core + head)
        return device, self.same & (self.head == head)

    def owner(self, index):
        device = (2 * self.at[X] + self.seq // 8, 2 * index + self.core)
        return device, self.same & (self.seq // 2 == index)

    def start(self, copy, key):
        copy.start()
        self.sending.append(copy.wait_send)
        self.coming[key] = copy.wait_recv

    def finish(self, copy, key):
        self.coming.pop(key)
        copy.wait_recv()

    def greet(self, barrier):
        for make in (self.holder, self.owner):
            for index in range(8):
                device, same = make(index)

                @pl.when(jnp.logical_not(same))
                def _():
                    pl.semaphore_signal(barrier, inc=1, device_id=device, device_id_type=MESH)

        others = [self.partner(), self.along(1), self.along(SEQ - 1)]
        others += [self.peer(axis, distance) for axis in (X, Y, Z) for distance in (1, 2, 3)]
        for device in others:
            pl.semaphore_signal(barrier, inc=1, device_id=device, device_id_type=MESH)
        return 16 + len(others) - 2 * self.same.astype(jnp.int32)


class Layer:
    def __init__(self, at, ref, own, index, rows):
        self.at = at
        self.r = ref
        self.s = own
        self.index = index
        self.rows = rows


    def _buffers(self, kind):
        s = self.s
        return (
            (s.kv_out, s.kv_in), (s.q_out, s.q_in), (s.dm_out, s.dm_in),
            (s.mix_out, s.mix_in), (s.dkv_out, s.dkv_in), (s.dq_out, s.dq_in),
        )[kind]

    def _copy(self, kind, index):
        at = self.at
        out, into = self._buffers(kind)
        if kind in (KV, Q, DM):
            (device, same), slot = at.holder(index), at.seq // 2
            target = at.seq if kind == KV else slot
        else:
            (device, same), slot = at.owner(index), at.head
            target = slot
        send, recv = self.s.sems.at[2 * kind, index], self.s.sems.at[2 * kind + 1, slot]
        return out.at[index], into.at[target], send, recv, device, same

    def send(self, kind):
        def one(index, carry):
            src, dst, send, recv, device, same = self._copy(kind, index)

            @pl.when(same)
            def _():
                pltpu.make_async_copy(src, dst, recv).start()

            @pl.when(jnp.logical_not(same))
            def _():
                remote(src, dst, send, recv, device).start()

            return carry

        lax.fori_loop(0, 8, one, 0)
        self.at.sending.append(lambda: self.sent(kind))
        self.at.coming[(self.index, kind)] = lambda: self.receive(kind)

    def _arrival(self, kind, index):
        out, into = self._buffers(kind)
        device, _ = self.at.owner(0)
        sems = self.s.sems
        return remote(out.at[0], into.at[0], sems.at[2 * kind, 0], sems.at[2 * kind + 1, index], device)

    def receive(self, kind):
        self.at.coming.pop((self.index, kind), None)

        def one(index, carry):
            self._arrival(kind, index).wait_recv()
            return carry

        lax.fori_loop(0, 8, one, 0)

    def sent(self, kind):
        def one(index, carry):
            src, dst, send, recv, device, same = self._copy(kind, index)

            @pl.when(jnp.logical_not(same))
            def _():
                remote(src, dst, send, recv, device).wait_send()

            return carry

        lax.fori_loop(0, 8, one, 0)

    def _relay(self, index):
        place = self.s.kv_in.at[2 * index + self.at.core]
        sems = self.s.sems
        return remote(place, place, sems.at[12, index], sems.at[13, index], self.at.partner())

    def receive_keys(self):
        self.at.coming.pop((self.index, KV), None)

        def one(index, carry):
            self._arrival(KV, index).wait_recv()
            self._relay(index).start()
            return carry

        def other(index, carry):
            self._relay(index).wait_recv()
            return carry

        def done(index, carry):
            self._relay(index).wait_send()
            return carry

        lax.fori_loop(0, 8, one, 0)
        lax.fori_loop(0, 8, other, 0)
        self.at.sending.append(lambda: lax.fori_loop(0, 8, done, 0))


    def angles(self):
        table, first = self.r.offsets, self.r.firsts
        place = self.index * SEQ + self.at.seq
        cos_a, sin_a = first[0, pl.ds(place, 1), :], first[1, pl.ds(place, 1), :]
        cos_b, sin_b = table[0, : self.rows, :], table[1, : self.rows, :]
        return cos_a * cos_b - sin_a * sin_b, sin_a * cos_b + cos_a * sin_b

    def gain(self, which):
        return self.r.gains[self.index, which : which + 1, :].astype(F32)

    def project(self, values):
        s, rows = self.s, self.rows
        normal, scale = normalize(values)
        s.normal[0] = normal
        s.scale[0] = jnp.broadcast_to(scale, (rows, 128))
        normed = (normal * self.gain(0)).astype(BF16)
        s.n1[...] = normed
        cosine, sine = self.angles()
        low = lanes((rows, 128)) < 64
        weight = self.r.wqkv.at[self.index]
        for group in range(GROUPS):
            key = dot(normed, weight[:, 512 + 128 * group : 640 + 128 * group])
            value = dot(normed, weight[:, 1024 + 128 * group : 1152 + 128 * group])
            key = key * cosine + half_turn(key) * sine
            value = pltpu.roll(value, 64, 1)
            s.kv_out[2 * group, :rows] = jnp.where(low, key, value).astype(BF16)
            s.kv_out[2 * group + 1, :rows] = jnp.where(low, value, key).astype(BF16)
            query = dot(normed, weight[:, 128 * group : 128 * group + 128])
            query = (query * cosine + half_turn(query) * sine) * 0.125
            s.q_out[2 * group], s.q_out[2 * group + 1] = pack_pair(query)

    def native(self, shape):
        return (lanes(shape) // 64) == lax.rem(self.at.seq, 2)

    def pack_one(self, values):
        rows = self.rows // 2
        return seal(jnp.where(self.native((rows, 128)), values[:rows], pltpu.roll(values[rows:], 64, 1)))

    def split_heads(self):
        s, length = self.s, SEQ * self.rows
        both = s.kv_in[:, : self.rows, :].reshape(length, 128).astype(F32)
        own = self.native((length, 128))
        s.key[...] = jnp.where(own, both, 0.0).astype(BF16)
        s.value[...] = jnp.where(own, pltpu.roll(both, 64, 1), 0.0).astype(BF16)

    def attend(self):
        s, core = self.s, self.at.core
        for index in range(8):
            s.query[index] = unpack_one(s.q_in[index], self.rows)
        if self.index == 0:
            for pair in range(8):
                count = -(-288 * (pair + 1) // 128) * 128
                score = dot_nt(s.query[pair], s.key[:count])
                first = (288 * pair) // 128 * 128
                column = s.column[pair][:, :1]
                allowed = s.line[0:1, :count] == column
                position = sublanes((LONG, count - first)) + (2 * pair + core) * LONG
                causal = lanes((LONG, count - first)) + first <= position
                if first:
                    head = jnp.where(allowed[:, :first], score[:, :first], -1e9)
                    tail = jnp.where(allowed[:, first:] & causal, score[:, first:], -1e9)
                    score = jnp.concatenate([head, tail], 1)
                else:
                    score = jnp.where(allowed & causal, score, -1e9)
                top = jnp.max(score, -1, keepdims=True)
                expo = jnp.exp(score - top)
                prob = (expo * (1.0 / jnp.sum(expo, -1, keepdims=True))).astype(BF16)
                s.prob[pair, :, :count] = prob
                s.mix_out[pair] = self.pack_one(dot(prob, s.value[:count]))
        else:
            count, length = 8 * SHORT, SEQ * SHORT
            score = dot_nt(s.query[...].reshape(count, 128), s.key[...])
            column = s.column[...].reshape(count, 128)[:, :1]
            row = lax.broadcasted_iota(jnp.int32, (8, SHORT, length), 1)
            block = lax.broadcasted_iota(jnp.int32, (8, SHORT, length), 0)
            position = (row + (2 * block + core) * SHORT).reshape(count, length)
            causal = lanes((count, length)) <= position
            score = jnp.where((s.line[0:1, :] == column) & causal, score, -1e9)
            top = jnp.max(score, -1, keepdims=True)
            expo = jnp.exp(score - top)
            prob = (expo * (1.0 / jnp.sum(expo, -1, keepdims=True))).astype(BF16)
            s.prob[...] = prob
            mixed = dot(prob, s.value[...]).reshape(8, SHORT, 128)
            for index in range(8):
                s.mix_out[index] = self.pack_one(mixed[index])

    def feed_forward(self, values):
        i, s = self.index, self.s
        parts = [unpack_pair(s.mix_in[2 * g], s.mix_in[2 * g + 1], self.rows) for g in range(GROUPS)]
        mixed = jnp.concatenate(parts, 1).astype(BF16)
        s.mixed[...] = mixed
        first = values + dot(mixed, self.r.wout[i])
        normal, scale = normalize(first)
        s.normal[1] = normal
        s.scale[1] = jnp.broadcast_to(scale, (self.rows, 128))
        normed = (normal * self.gain(1)).astype(BF16)
        s.n2[...] = normed
        result = first
        for part in range(4):
            at = slice(512 * part, 512 * part + 512)
            hidden = dot(normed, self.r.wup[i, :, at])
            inner = 0.7978845608028654 * (hidden + 0.044715 * hidden * hidden * hidden)
            bend = jnp.tanh(inner)
            active = (0.5 * hidden * (1.0 + bend)).astype(BF16)
            slope = 0.5 * (1.0 + bend) + 0.5 * hidden * (1.0 - bend * bend) * (
                0.7978845608028654 * (1.0 + 3.0 * 0.044715 * hidden * hidden)
            )
            s.slope[:, at] = slope
            s.act[part // 2, :, 512 * (part % 2) : 512 * (part % 2) + 512] = active
            result = result + dot(active, self.r.wdown[i, at, :])
        return result


    def feed_back(self, grad):
        i, s = self.index, self.s
        low = grad.astype(BF16)
        s.glow[...] = low
        back = jnp.zeros((self.rows, D), F32)
        for part in range(4):
            at = slice(512 * part, 512 * part + 512)
            active = dot_nt(low, self.r.wdown[i, at, :])
            hidden = (s.slope[:, at] * active).astype(BF16)
            s.dhid[part // 2, :, 512 * (part % 2) : 512 * (part % 2) + 512] = hidden
            back = back + dot_nt(hidden, self.r.wup[i, :, at])
        normal, scale = s.normal[1], s.scale[1][:, :1]
        self.r.gsum[2 * i + 1 : 2 * i + 2, :] = jnp.sum(back * normal, 0, keepdims=True)
        first = grad + normalize_back(back, normal, scale, self.gain(1))
        s.dfirst[...] = first
        first_low = first.astype(BF16)
        s.dv1[0] = first_low[:, :256]
        s.dv1[1] = first_low[:, 256:]
        for group in range(GROUPS):
            at = slice(128 * group, 128 * group + 128)
            s.dm_out[2 * group], s.dm_out[2 * group + 1] = pack_pair(dot_nt(first_low, self.r.wout[i, at, :]))

    def attend_back(self):
        s, length = self.s, SEQ * self.rows
        own = self.native((length, 128))
        if self.index == 0:
            self.r.dkey[...] = jnp.zeros((length, 128), F32)
            self.r.dvalue[...] = jnp.zeros((length, 128), F32)
            for pair in range(8):
                count = -(-288 * (pair + 1) // 128) * 128
                grad = unpack_one(s.dm_in[pair], self.rows)
                prob = s.prob[pair, :, :count]
                dprob = dot_nt(grad, s.value[:count])
                weighted = prob * dprob
                inner = jnp.sum(weighted, -1, keepdims=True)
                draw = (weighted - prob * inner).astype(BF16)
                s.dq_out[pair] = self.pack_one(dot(draw, s.key[:count]) * 0.125)
                self.r.dkey[:count] += dot_tn(draw, s.query[pair])
                self.r.dvalue[:count] += dot_tn(prob, grad)
            dkey, dvalue = self.r.dkey[...], self.r.dvalue[...]
        else:
            count = 8 * SHORT
            grad = jnp.concatenate([unpack_one(s.dm_in[index], self.rows) for index in range(8)], 0)
            prob = s.prob[...]
            dprob = dot_nt(grad, s.value[...])
            weighted = prob * dprob
            inner = jnp.sum(weighted, -1, keepdims=True)
            draw = (weighted - prob * inner).astype(BF16)
            dq = (dot(draw, s.key[...]) * 0.125).reshape(8, SHORT, 128)
            for index in range(8):
                s.dq_out[index] = self.pack_one(dq[index])
            dkey = dot_tn(draw, s.query[...].reshape(count, 128))
            dvalue = dot_tn(prob, grad)
        both = jnp.where(own, dkey, pltpu.roll(dvalue, 64, 1)).astype(BF16)
        both = both.reshape(8, 2, self.rows, 128)
        for which in range(2):
            s.dkv_part[which] = both[:, which]

    def _merge(self):
        s = self.s
        return remote(
            s.dkv_part.at[1 - self.at.core], s.dkv_other, s.sems.at[14, 0], s.sems.at[14, 1], self.at.partner()
        )

    def merge_start(self):
        self.at.start(self._merge(), (self.index, 14))

    def merge(self):
        s = self.s
        self.at.finish(self._merge(), (self.index, 14))
        s.dkv_out[...] = (s.dkv_part[self.at.core].astype(F32) + s.dkv_other[...].astype(F32)).astype(BF16)

    def project_back(self):
        i, s, rows = self.index, self.s, self.rows
        cosine, sine = self.angles()
        low = lanes((rows, 128)) < 64
        back = jnp.zeros((rows, D), F32)
        for group in range(GROUPS):
            even, odd = s.dkv_in[2 * group].astype(F32), s.dkv_in[2 * group + 1].astype(F32)
            key = jnp.where(low, even, odd)
            key = key * cosine - half_turn(key) * sine
            value = pltpu.roll(jnp.where(low, odd, even), 64, 1)
            query = unpack_pair(s.dq_in[2 * group], s.dq_in[2 * group + 1], rows)
            query = query * cosine - half_turn(query) * sine
            for which, piece in enumerate((query, key, value)):
                place = 4 * which + group
                column = 128 * (place % 6)
                s.dproj[place // 6, :, column : column + 128] = piece.astype(BF16)
        for part in range(2):
            back = back + dot_nt(s.dproj[part], self.r.wqkv[i, :, 768 * part : 768 * part + 768])
        normal, scale = s.normal[0], s.scale[0][:, :1]
        self.r.gsum[2 * i : 2 * i + 1, :] = jnp.sum(back * normal, 0, keepdims=True)
        return s.dfirst[...] + normalize_back(back, normal, scale, self.gain(0))


    def _swap(self, which):
        s, other = self.s, 1 - self.at.core
        src, dst = (
            (s.glow, s.glow_in), (s.n2, s.n2_in), (s.act.at[other], s.act_in), (s.dhid.at[other], s.dhid_in),
            (s.mixed, s.mixed_in), (s.dv1.at[other], s.dv1_in), (s.n1, s.n1_in), (s.dproj.at[other], s.dproj_in),
        )[which]
        return remote(src, dst, s.sems.at[15, which], s.sems.at[16, which], self.at.partner())

    def swap(self, steps):
        for which in steps:
            self.at.start(self._swap(which), (self.index, 10, which))

    def swapped(self, steps):
        for which in steps:
            self.at.finish(self._swap(which), (self.index, 10, which))

    def grads_feed(self, total):
        s, core = self.s, self.at.core
        for part in range(4):
            at = slice(256 * part, 256 * part + 256)
            total.put_rows(
                part, dot_tn(s.act[core, :, at], s.glow[...]) + dot_tn(s.act_in[:, at], s.glow_in[...])
            )
        for part in range(2):
            at = slice(512 * part, 512 * part + 512)
            up = dot_tn(s.n2[...], s.dhid[core, :, at]) + dot_tn(s.n2_in[...], s.dhid_in[:, at])
            total.put_columns(4 + 2 * part, up[:, :256])
            total.put_columns(5 + 2 * part, up[:, 256:])
        total.put_columns(8, dot_tn(s.mixed[...], s.dv1[core]) + dot_tn(s.mixed_in[...], s.dv1_in[...]))

    def grads_attention(self, total):
        s, core = self.s, self.at.core
        grad = dot_tn(s.n1[...], s.dproj[core]) + dot_tn(s.n1_in[...], s.dproj_in[...])
        for part in range(3):
            total.put_columns(part, grad[:, 256 * part : 256 * part + 256])


class Total:
    def __init__(self, at, own, index, kind, result):
        self.at, self.s, self.index, self.kind, self.result = at, own, index, kind, result
        self.units = own.full.shape[-1] // 128

    def put_rows(self, unit, values):
        part, column = unit // self.units, unit % self.units * 128
        values = values.astype(BF16)
        for group in range(4):
            self.s.grads[part, group, :, :, :, column : column + 128] = values[
                :, 128 * group : 128 * group + 128
            ].reshape(4, 4, 16, 128)

    def put_columns(self, unit, values):
        part, column = unit // self.units, unit % self.units * 128
        values = values.astype(BF16)
        for group in range(2):
            self.s.grads[part, 2 * group : 2 * group + 2, :, :, :, column : column + 128] = values[
                :, 128 * group : 128 * group + 128
            ].reshape(2, 4, 4, 16, 128)

    def _scatter(self, part, stage, distance):
        s, axis = self.s, ORDERS[part][stage]
        to = lax.rem(self.at.at[axis] + distance, 4)
        src = (s.grads, s.sum1, s.sum2)[stage].at[part, to]
        dst = (s.part0, s.part1, s.part2)[stage].at[part, distance - 1]
        slot = 3 * part + distance - 1
        return remote(src, dst, s.sems.at[2 * stage, slot], s.sems.at[2 * stage + 1, slot], self.at.peer(axis, distance))

    def _gather(self, part, stage, distance):
        s, axis = self.s, ORDERS[part][stage]
        place = s.full.at[(part, *[self.at.at[a] for a in ORDERS[part]][: stage + 1])]
        slot = 3 * part + distance - 1
        send, recv = s.sems.at[6 + 2 * stage, slot], s.sems.at[7 + 2 * stage, slot]
        return remote(place, place, send, recv, self.at.peer(axis, distance))

    def _relay(self, part):
        src, dst = self.s.full.at[part], self.result.at[self.index, self.at.core, part]
        return remote(src, dst, self.s.sems.at[12, part], self.s.sems.at[12, 3 + part], self.at.partner())

    def _store(self, part):
        dst = self.result.at[self.index, self.at.core, part]
        return pltpu.make_async_copy(self.s.full.at[part], dst, self.s.sems.at[12, 6 + part])

    def _all(self, make, act, name, stage):
        for part in range(3):
            for distance in (1, 2, 3):
                act(make(part, stage, distance), (self.index, self.kind, name, part, stage, distance))

    def scatter(self, stage):
        self._all(self._scatter, self.at.start, 0, stage)

    def scattered(self, stage):
        s = self.s
        for part in range(3):
            for distance in (1, 2, 3):
                self.at.finish(self._scatter(part, stage, distance), (self.index, self.kind, 0, part, stage, distance))
            mine = [self.at.at[a] for a in ORDERS[part]]
            src = (s.grads, s.sum1, s.sum2)[stage]
            got = (s.part0, s.part1, s.part2)[stage]
            total = src[part, mine[stage]].astype(F32)
            for distance in range(3):
                total = total + got[part, distance].astype(F32)
            total = total.astype(BF16)
            if stage == 0:
                s.sum1[part] = total
            elif stage == 1:
                s.sum2[part] = total
            else:
                s.full[(part, *mine)] = total
            for distance in (1, 2, 3):
                if stage < 2:
                    copy = self._scatter(part, stage + 1, distance)
                    self.at.start(copy, (self.index, self.kind, 0, part, stage + 1, distance))
                else:
                    self.at.start(self._gather(part, 2, distance), (self.index, self.kind, 1, part, 2, distance))

    def gathered(self, stage):
        for part in range(3):
            for distance in (1, 2, 3):
                self.at.finish(self._gather(part, stage, distance), (self.index, self.kind, 1, part, stage, distance))
            if stage:
                for distance in (1, 2, 3):
                    copy = self._gather(part, stage - 1, distance)
                    self.at.start(copy, (self.index, self.kind, 1, part, stage - 1, distance))
            else:
                self.at.start(self._relay(part), (self.index, self.kind, 2, part))
                self._store(part).start()
                self.at.sending.append(self._store(part).wait)


def vmem(**shapes):
    return {name: pltpu.VMEM(shape, kind) for name, (shape, kind) in shapes.items()}


def layer_scratch(index, rows):
    length, half = SEQ * rows, padded(rows)
    message = rows + (NOTE if index == 0 else 0)
    shapes = vmem(
        kv_out=((8, message, 128), BF16), kv_in=((SEQ, message, 128), BF16),
        q_out=((8, half, 128), BF16), q_in=((8, half, 128), BF16),
        dm_out=((8, half, 128), BF16), dm_in=((8, half, 128), BF16),
        mix_out=((8, half, 128), BF16), mix_in=((8, half, 128), BF16),
        dq_out=((8, half, 128), BF16), dq_in=((8, half, 128), BF16),
        dkv_part=((2, 8, rows, 128), BF16), dkv_other=((8, rows, 128), BF16),
        dkv_out=((8, rows, 128), BF16), dkv_in=((8, rows, 128), BF16),
        query=((8, rows, 128), BF16), key=((length, 128), BF16), value=((length, 128), BF16),
        prob=((8, rows, length) if index == 0 else (8 * rows, length), BF16),
        normal=((2, rows, D), F32), scale=((2, rows, 128), F32),
        slope=((rows, FF), F32), dfirst=((rows, D), F32),
        n1=((rows, D), BF16), n2=((rows, D), BF16), mixed=((rows, D), BF16), glow=((rows, D), BF16),
        act=((2, rows, FF // 2), BF16), dhid=((2, rows, FF // 2), BF16),
        dv1=((2, rows, 256), BF16), dproj=((2, rows, 768), BF16),
        n1_in=((rows, D), BF16), n2_in=((rows, D), BF16), mixed_in=((rows, D), BF16), glow_in=((rows, D), BF16),
        act_in=((rows, FF // 2), BF16), dhid_in=((rows, FF // 2), BF16),
        dv1_in=((rows, 256), BF16), dproj_in=((rows, 768), BF16),
        column=((8, rows, 128), F32), line=((8, length), F32),
    )
    shapes.update(sems=pltpu.SemaphoreType.DMA((17, 8)))
    return shapes


def total_scratch(width):
    shapes = vmem(
        grads=((3, 4, 4, 4, 16, width), BF16),
        part0=((3, 3, 4, 4, 16, width), BF16), sum1=((3, 4, 4, 16, width), BF16),
        part1=((3, 3, 4, 16, width), BF16), sum2=((3, 4, 16, width), BF16),
        part2=((3, 3, 16, width), BF16),
        full=((3, 4, 4, 4, 16, width), BF16),
    )
    shapes.update(sems=pltpu.SemaphoreType.DMA((13, 9)))
    return shapes


def common_scratch():
    shapes = vmem(
        tokens=((LONG, D), BF16), cot=((LONG, D), BF16), seg=((1, LONG), jnp.int32), gains=((2, 2, D), BF16),
        offsets=((2, LONG, 128), F32), firsts=((2, 2 * SEQ, 128), F32),
        wqkv=((2, D, 3 * D), BF16), wout=((2, D, D), BF16),
        wup=((2, D, FF), BF16), wdown=((2, FF, D), BF16),
        dkey=((SEQ * LONG, 128), F32), dvalue=((SEQ * LONG, 128), F32),
        second=((4, LONG + 8, 128), F32), share=((4, SHORT + 8, 128), F32),
        work=((4, LONG, 128), F32), spread=((4, LONG, 128), F32),
        tail=((4, 8, 128), F32), ahead=((4, 8, 128), F32),
        output=((LONG, D), BF16), result=((LONG, D), F32),
        gsum=((8, D), F32), gain_in=((4, 4, 8, D), F32), gain_out=((3, 8, D), F32),
    )
    shapes.update(more=pltpu.SemaphoreType.DMA((6, 20)))
    return shapes


SPACES = (
    common_scratch(), layer_scratch(0, LONG), layer_scratch(1, SHORT),
    total_scratch(384), total_scratch(128), total_scratch(384), total_scratch(128),
)


def body(*refs):
    spaces, place = [], 15
    for part in SPACES:
        spaces.append(types.SimpleNamespace(**dict(zip(part, refs[place : place + len(part)]))))
        place += len(part)
    at = Place()
    steps(at, spaces, *refs[:15])
    for wait in at.coming.values():
        wait()
    for wait in at.sending:
        wait()


def steps(
    at, spaces, tokens, seg, wqkv, wout, wup, wdown, gains, cot, offsets, firsts,
    output, tokens_grad, feed_sums, attention_sums, gain_sum,
):
    ref = spaces[0]
    more = ref.more
    full, short = Layer(at, ref, spaces[1], 0, LONG), Layer(at, ref, spaces[2], 1, SHORT)
    full_feed, full_heads = Total(at, spaces[3], 0, 20, feed_sums), Total(at, spaces[4], 0, 21, attention_sums)
    short_feed, short_heads = Total(at, spaces[5], 1, 20, feed_sums), Total(at, spaces[6], 1, 21, attention_sums)

    pairs = [
        (tokens, ref.tokens), (gains, ref.gains), (wqkv.at[0], ref.wqkv.at[0]),
        (offsets, ref.offsets), (firsts, ref.firsts), (seg, ref.seg),
        (wout.at[0], ref.wout.at[0]), (wup.at[0], ref.wup.at[0]), (wdown.at[0], ref.wdown.at[0]),
        (wqkv.at[1], ref.wqkv.at[1]), (cot, ref.cot),
        (wout.at[1], ref.wout.at[1]), (wup.at[1], ref.wup.at[1]), (wdown.at[1], ref.wdown.at[1]),
    ]
    loads = [pltpu.make_async_copy(src, dst, more.at[0, step]) for step, (src, dst) in enumerate(pairs)]
    for load in loads:
        load.start()
    waiting = list(range(len(loads)))

    def loaded(count):
        while waiting and waiting[0] < count:
            loads[waiting.pop(0)].wait()

    at.sending.append(lambda: loaded(len(loads)))
    barrier = pltpu.get_barrier_semaphore()
    greeted = at.greet(barrier)

    loaded(6)
    inputs = ref.tokens[...].astype(F32)
    full.project(inputs)
    line = ref.seg[...].astype(F32)
    high = jnp.floor(line * (1.0 / 64.0))
    rows = jnp.concatenate([high, line - 64.0 * high, jnp.zeros((6, LONG), F32)], 0)
    third = jnp.where(sublanes((LONG, 128)) == 3 * lanes((LONG, 128)), 1.0, 0.0)
    picked = dot(rows, third)
    wide = jnp.concatenate([rows[:, 128:], jnp.zeros((8, 112), F32)], 1)
    note = jnp.concatenate([rows[0:2, :128], wide[0:2], picked[0:2], jnp.zeros((10, 128), F32)], 0).astype(BF16)
    for head in range(8):
        full.s.kv_out[head, LONG:] = note
    pl.semaphore_wait(barrier, greeted)
    full.send(KV)
    full.send(Q)

    def segments():
        notes = [full.s.kv_in[block, LONG:, :].astype(F32) for block in range(SEQ)]
        for block, code in enumerate(notes):
            long = jnp.concatenate([64.0 * code[0:1] + code[1:2], 64.0 * code[2:3, :16] + code[3:4, :16]], 1)
            full.s.line[0:1, LONG * block : LONG * block + LONG] = long
            short.s.line[0:1, SHORT * block : SHORT * block + SHORT] = (64.0 * code[4:5] + code[5:6])[:, :SHORT]
        for layer in (full, short):
            rows = layer.rows
            equal = lanes((rows, rows)) == sublanes((rows, rows))
            for pair in range(8):
                code = full.s.kv_in[2 * pair + at.core, LONG:, :].astype(F32)
                if layer is full:
                    line = jnp.concatenate([64.0 * code[0:1] + code[1:2], 64.0 * code[2:3, :16] + code[3:4, :16]], 1)
                else:
                    line = (64.0 * code[4:5] + code[5:6])[:, :SHORT]
                column = jnp.sum(jnp.where(equal, line, 0.0), 1, keepdims=True)
                layer.s.column[pair] = jnp.broadcast_to(column, (rows, 128))

    def attention(layer):
        layer.receive_keys()
        layer.receive(Q)
        if layer is full:
            segments()
        layer.split_heads()
        layer.attend()
        layer.send(MIX)
        layer.receive(MIX)

    attention(full)
    loaded(9)
    second = ref.second
    spill(second, 8, full.feed_forward(inputs))

    def halo():
        return remote(second.at[:, pl.ds(LONG, 8), :], ref.tail, more.at[1, 0], more.at[1, 1], at.along(1))

    at.start(halo(), (3, 0))
    loaded(11)
    work = ref.work
    spill(work, 0, ref.cot[...].astype(F32))
    grad_short = jnp.concatenate(
        [every_third(work, 0, g) + every_third(work, 1, g) + every_third(work, 2, g) for g in range(GROUPS)], 1
    )
    at.finish(halo(), (3, 0))
    second[:, 0:8, :] = jnp.where(at.seq == 0, 0.0, ref.tail[...])
    pooled = jnp.concatenate(
        [
            (every_third(second, 6, g) + every_third(second, 7, g) + every_third(second, 8, g)) / 3.0
            for g in range(GROUPS)
        ],
        1,
    )
    short.project(pooled)
    short.send(KV)
    short.send(Q)
    loaded(14)
    attention(short)
    result = short.feed_forward(pooled)

    def backward(layer, total, grad, between):
        layer.feed_back(grad)
        layer.send(DM)
        layer.swap((0, 1, 2, 3, 4, 5, 6))
        between(0)
        layer.swapped((0, 1, 2, 3, 4, 5, 6))
        layer.grads_feed(total)
        total.scatter(0)
        between(1)
        layer.receive(DM)
        layer.attend_back()
        layer.merge_start()
        layer.send(DQ)
        layer.merge()
        layer.send(DKV)
        between(2)
        layer.receive(DQ)
        layer.receive(DKV)
        back = layer.project_back()
        layer.swap((7,))
        return back

    spread = ref.spread

    def finish_output():
        for group in range(GROUPS):
            at_lanes = slice(128 * group, 128 * group + 128)
            for step in range(3):
                spread[group, pl.ds(step, SHORT, 3), :] = every_third(second, 8 + step, group) + result[:, at_lanes]
            ref.output[:, at_lanes] = spread[group].astype(BF16)
        store = pltpu.make_async_copy(ref.output, output, more.at[0, 14])
        store.start()
        at.sending.append(store.wait)

    def between_short(point):
        if point == 0:
            finish_output()

    share = ref.share
    spill(share, 0, backward(short, short_feed, grad_short, between_short) * (1.0 / 3.0))

    def halo_back():
        return remote(share.at[:, pl.ds(0, 8), :], ref.ahead, more.at[1, 2], more.at[1, 3], at.along(SEQ - 1))

    at.start(halo_back(), (3, 1))
    short.swapped((7,))
    short.grads_attention(short_heads)
    short_heads.scatter(0)
    short_feed.scattered(0)
    at.finish(halo_back(), (3, 1))
    share[:, SHORT:, :] = jnp.where(at.seq == SEQ - 1, 0.0, ref.ahead[...])
    for group in range(GROUPS):
        own, following = share[group, 0:SHORT, :], share[group, 1 : SHORT + 1, :]
        for step, piece in enumerate((own, following, following)):
            spread[group, pl.ds(step, SHORT, 3), :] = every_third(work, step, group) + piece
    grad_full = jnp.concatenate([spread[group] for group in range(GROUPS)], 1)

    def between_full(point):
        if point == 0:
            short_feed.scattered(1)
        elif point == 1:
            short_heads.scattered(0)
            short_feed.scattered(2)
        else:
            short_feed.gathered(2)
            short_heads.scattered(1)
            short_feed.gathered(1)
            full_feed.scattered(0)
            short_heads.scattered(2)

    ref.result[...] = backward(full, full_feed, grad_full, between_full)
    store = pltpu.make_async_copy(ref.result, tokens_grad, more.at[0, 15])
    store.start()
    at.sending.append(store.wait)
    full_feed.scattered(1)
    full.swapped((7,))
    full.grads_attention(full_heads)
    full_heads.scatter(0)

    gsum, gain_in, gain_out = ref.gsum, ref.gain_in, ref.gain_out

    def gain_copy(axis, distance):
        src = gsum if axis == 0 else gain_out.at[axis - 1]
        return remote(
            src, gain_in.at[axis, at.at[axis]], more.at[2, 3 * axis + distance], more.at[3, 3 * axis + distance],
            at.peer(axis, distance),
        )

    def gain_step(axis):
        for distance in (1, 2, 3):
            at.start(gain_copy(axis, distance), (4, axis, distance))
        gain_in[axis, at.at[axis]] = gsum[...] if axis == 0 else gain_out[axis - 1]

    def gain_done(axis):
        for distance in (1, 2, 3):
            at.finish(gain_copy(axis, distance), (4, axis, distance))
        return (gain_in[axis, 0] + gain_in[axis, 1]) + (gain_in[axis, 2] + gain_in[axis, 3])

    gsum[4:, :] = jnp.zeros((4, D), F32)
    gain_step(0)
    full_feed.scattered(2)
    short_heads.gathered(2)
    full_heads.scattered(0)
    short_feed.gathered(0)
    gain_out[0] = gain_done(0)
    gain_step(1)
    full_feed.gathered(2)
    short_heads.gathered(1)
    full_heads.scattered(1)
    gain_out[1] = gain_done(1)
    gain_step(2)
    full_feed.gathered(1)
    full_heads.scattered(2)
    short_heads.gathered(0)
    gain_in[3, 0] = gain_done(2)
    gain_swap = remote(gain_in.at[3, 0], gain_in.at[3, 1], more.at[1, 4], more.at[1, 5], at.partner())
    at.start(gain_swap, (4, 3, 0))
    full_heads.gathered(2)
    full_heads.gathered(1)
    full_feed.gathered(0)
    full_heads.gathered(0)
    at.finish(gain_swap, (4, 3, 0))
    gain_out[2] = gain_in[3, 0] + gain_in[3, 1]
    store = pltpu.make_async_copy(gain_out.at[2], gain_sum, more.at[0, 16])
    store.start()
    at.sending.append(store.wait)


def tables():
    freq = 10000.0 ** (-np.arange(32) / 32.0)
    freq = np.tile(freq, 4)[None, :]
    offset = np.arange(LONG)[:, None] * freq
    first = np.concatenate([np.arange(SEQ) * LONG, np.arange(SEQ) * SHORT])[:, None] * freq
    return (
        np.stack([np.cos(offset), np.sin(offset)]).astype(np.float32),
        np.stack([np.cos(first), np.sin(first)]).astype(np.float32),
    )


def widen_body(
    feed, heads, gain, output, grad, qkv, out, up, down, gains, output_too, grad_too,
    feed_in, heads_in, gain_in, gain_out, down_out, up_out, out_out, qkv_out, sems,
):
    def place(step):
        return step // 2, step % 2

    loads, stores = [], []
    small = [
        pltpu.make_async_copy(gain, gain_in, sems.at[0, 0]),
        pltpu.make_async_copy(output, output_too.at[0], sems.at[0, 1]),
        pltpu.make_async_copy(grad, grad_too.at[0], sems.at[0, 2]),
    ]
    for step in range(4):
        block, half = place(step)
        for part in range(3):
            loads.append(pltpu.make_async_copy(feed.at[block, half, part], feed_in.at[step, part], sems.at[1 + step, part]))
        loads.append(pltpu.make_async_copy(heads.at[block, half], heads_in.at[step], sems.at[1 + step, 3]))
    for copy in loads + small:
        copy.start()
    small[0].wait()
    gain_out[...] = gain_in[0:4, :].reshape(2, 2, D)
    small[0] = pltpu.make_async_copy(gain_out, gains, sems.at[0, 3])
    small[0].start()
    for step in range(4):
        block, half = place(step)

        def put(copy_to, source, slot):
            copy = pltpu.make_async_copy(source, copy_to, sems.at[5 + step, slot])
            copy.start()
            stores.append(copy)

        for unit in range(9):
            if unit % 3 == 0:
                loads[4 * step + unit // 3].wait()
            lane = slice(128 * (unit % 3), 128 * (unit % 3) + 128)
            tiles = feed_in.at[step, unit // 3]
            if unit < 4:
                rows = slice(256 * unit, 256 * unit + 256)
                for group in range(4):
                    values = tiles[group, :, :, :, lane].reshape(256, 128).astype(F32)
                    down_out[step, rows, 128 * group : 128 * group + 128] = values
            else:
                for group in range(2):
                    values = tiles[2 * group : 2 * group + 2, :, :, :, lane].reshape(512, 128).astype(F32)
                    if unit < 8:
                        column = 256 * (unit - 4) + 128 * group
                        up_out[step, :, column : column + 128] = values
                    else:
                        out_out[step, :, 128 * group : 128 * group + 128] = values
            if unit == 3:
                put(down.at[block, pl.ds(1024 * half, 1024), :], down_out.at[step], 0)
            elif unit == 7:
                put(up.at[block, :, pl.ds(1024 * half, 1024)], up_out.at[step], 1)
            elif unit == 8:
                put(out.at[block, :, pl.ds(256 * half, 256)], out_out.at[step], 2)
        loads[4 * step + 3].wait()
        for unit in range(3):
            for group in range(2):
                column = 256 * unit + 128 * group
                tiles = heads_in[step, unit, 2 * group : 2 * group + 2]
                qkv_out[step, :, column : column + 128] = tiles.reshape(512, 128).astype(F32)
        put(qkv.at[block, :, pl.ds(768 * half, 768)], qkv_out.at[step], 3)
    for copy in stores + small:
        copy.wait()


def widen(feed, heads, gain, output, grad):
    anywhere = pl.BlockSpec(memory_space=pl.ANY)
    return pl.pallas_call(
        widen_body,
        out_shape=(
            jax.ShapeDtypeStruct((2, D, 3 * D), F32),
            jax.ShapeDtypeStruct((2, D, D), F32),
            jax.ShapeDtypeStruct((2, D, FF), F32),
            jax.ShapeDtypeStruct((2, FF, D), F32),
            jax.ShapeDtypeStruct((2, 2, D), F32),
            jax.ShapeDtypeStruct((1, LONG, D), BF16),
            jax.ShapeDtypeStruct((1, LONG, D), F32),
        ),
        in_specs=[anywhere] * 5,
        out_specs=(anywhere,) * 7,
        scratch_shapes=[
            pltpu.VMEM((4, 3, 4, 4, 4, 16, 384), BF16),
            pltpu.VMEM((4, 3, 4, 4, 4, 16, 128), BF16),
            pltpu.VMEM((8, D), F32),
            pltpu.VMEM((2, 2, D), F32),
            pltpu.VMEM((4, 1024, 512), F32),
            pltpu.VMEM((4, 512, 1024), F32),
            pltpu.VMEM((4, 512, 256), F32),
            pltpu.VMEM((4, 512, 768), F32),
            pltpu.SemaphoreType.DMA((9, 4)),
        ],
        compiler_params=pltpu.CompilerParams(vmem_limit_bytes=56 * 2**20),
        name="widen",
    )(feed, heads, gain, output, grad)


def per_device(tokens, segment, w_qkv, w_out, w_up, w_down, gains, cotangent):
    offsets, firsts = tables()
    anywhere = pl.BlockSpec(memory_space=pl.ANY)
    output, tokens_grad, feed, heads, gain = pl.pallas_call(
        body,
        out_shape=(
            jax.ShapeDtypeStruct((LONG, D), BF16),
            jax.ShapeDtypeStruct((LONG, D), F32),
            jax.ShapeDtypeStruct((2, 2, 3, 4, 4, 4, 16, 384), BF16),
            jax.ShapeDtypeStruct((2, 2, 3, 4, 4, 4, 16, 128), BF16),
            jax.ShapeDtypeStruct((8, D), F32),
        ),
        in_specs=[anywhere] * 10,
        out_specs=(anywhere,) * 5,
        scratch_shapes=[shape for part in SPACES for shape in part.values()],
        compiler_params=pltpu.CompilerParams(
            collective_id=0, has_side_effects=True, vmem_limit_bytes=62 * 2**20
        ),
        name="layers",
    )(
        tokens[0], segment, w_qkv, w_out, w_up, w_down, gains, cotangent[0],
        jnp.asarray(offsets), jnp.asarray(firsts),
    )
    qkv, out, up, down, gain, output, tokens_grad = widen(feed, heads, gain, output, tokens_grad)
    return output, tokens_grad, qkv, out, up, down, gain


def solution(mesh):
    return jax.shard_map(
        per_device,
        mesh=mesh,
        in_specs=(
            P("row", "seq", None),
            P("row", "seq"),
            P(),
            P(),
            P(),
            P(),
            P(),
            P("row", "seq", None),
        ),
        out_specs=(P("row", "seq", None), P("row", "seq", None), P(), P(), P(), P(), P()),
        check_vma=False,
    )
```

```python
import types

import jax
import jax.numpy as jnp
import numpy as np
from jax import lax
from jax.experimental import pallas as pl
from jax.experimental.pallas import tpu as pltpu
from jax.sharding import PartitionSpec as P

MESH = pl.DeviceIdType.MESH
F32 = jnp.float32
BF16 = jnp.bfloat16

SEQ = 16
LONG = 144
SHORT = 48
D = 512
FF = 2048
GROUPS = 4
NOTE = 16
KV, Q, DM, MIX, DKV, DQ = range(6)
SEVEN = tuple(range(7))
UNITS = (3, 4, 1)
HOP, BACK = 9, 10
X, Y, Z = range(3)
ORDERS = ((X, Y, Z), (Y, Z, X), (Z, X, Y))


def dot(left, right):
    return jnp.dot(left, right, preferred_element_type=F32)


def dot_nt(left, right):
    return lax.dot_general(left, right, (((1,), (1,)), ((), ())), preferred_element_type=F32)


def dot_tn(left, right):
    return lax.dot_general(left, right, (((0,), (0,)), ((), ())), preferred_element_type=F32)


def lanes(shape):
    return lax.broadcasted_iota(jnp.int32, shape, len(shape) - 1)


def sublanes(shape):
    return lax.broadcasted_iota(jnp.int32, shape, len(shape) - 2)


def normalize(values):
    center = values - jnp.mean(values, -1, keepdims=True)
    scale = lax.rsqrt(jnp.mean(center * center, -1, keepdims=True) + 1e-05)
    return center * scale, scale


def normalize_back(grad, normal, scale, gain):
    inner = grad * gain
    return scale * (
        inner
        - jnp.mean(inner, -1, keepdims=True)
        - normal * jnp.mean(inner * normal, -1, keepdims=True)
    )


def half_turn(tensor):
    up = pltpu.roll(tensor, 96, 1)
    down = pltpu.roll(tensor, 32, 1)
    return jnp.where(lanes(tensor.shape) % 64 < 32, -up, down)


def padded(rows):
    return -(-rows // 32) * 16


def seal(packed):
    rows = packed.shape[0]
    return jnp.concatenate([packed, jnp.zeros((padded(2 * rows) - rows, 128), F32)], 0).astype(BF16)


def pack_pair(pair):
    rows = pair.shape[0] // 2
    top, bottom = pair[:rows], pltpu.roll(pair[rows:], 64, 1)
    low = lanes(top.shape) < 64
    return seal(jnp.where(low, top, bottom)), seal(jnp.where(low, bottom, top))


def unpack_pair(even, odd, rows):
    even, odd = even.astype(F32)[: rows // 2], odd.astype(F32)[: rows // 2]
    low = lanes(even.shape) < 64
    return jnp.concatenate([jnp.where(low, even, odd), pltpu.roll(jnp.where(low, odd, even), 64, 1)], 0)


def unpack_one(packed, rows):
    packed = packed.astype(F32)[: rows // 2]
    return jnp.concatenate([packed, pltpu.roll(packed, 64, 1)], 0)


def spill(ref, first, values):
    for group in range(GROUPS):
        ref[group, first : first + values.shape[0], :] = values[:, 128 * group : 128 * group + 128]


def every_third(ref, first, group):
    return ref[group, pl.ds(first, SHORT, 3), :]


def remote(src, dst, send, recv, device):
    return pltpu.make_async_remote_copy(
        src_ref=src, dst_ref=dst, send_sem=send, recv_sem=recv, device_id=device, device_id_type=MESH
    )


class Place:
    def __init__(self):
        self.row = lax.axis_index("row")
        self.seq = lax.axis_index("seq")
        self.core = lax.rem(self.row, 2)
        self.at = (self.row // 2, lax.rem(self.seq, 4), self.seq // 4)
        self.head = lax.rem(self.seq, 8)
        self.same = (self.seq // 8 == self.core) & (lax.rem(self.seq, 2) == self.core)
        self.sending, self.coming = [], {}

    def peer(self, axis, distance):
        to = lax.rem(self.at[axis] + distance, 4)
        if axis == X:
            return (to * 2 + self.core, self.seq)
        if axis == Y:
            return (self.row, self.at[Z] * 4 + to)
        return (self.row, to * 4 + self.at[Y])

    def partner(self):
        return (self.row + 1 - 2 * self.core, self.seq)

    def along(self, distance):
        return (self.row, lax.rem(self.seq + distance, SEQ))

    def holder(self, head):
        device = (2 * self.at[X] + lax.rem(self.seq, 2), 8 * self.core + head)
        return device, self.same & (self.head == head)

    def owner(self, index):
        device = (2 * self.at[X] + self.seq // 8, 2 * index + self.core)
        return device, self.same & (self.seq // 2 == index)

    def start(self, copy, key):
        copy.start()
        self.sending.append(copy.wait_send)
        self.coming[key] = copy.wait_recv

    def finish(self, copy, key):
        self.coming.pop(key)
        copy.wait_recv()

    def greet(self, barrier):
        for make in (self.holder, self.owner):
            for index in range(8):
                device, same = make(index)

                @pl.when(jnp.logical_not(same))
                def _():
                    pl.semaphore_signal(barrier, inc=1, device_id=device, device_id_type=MESH)

        others = [self.partner(), self.along(1), self.along(SEQ - 1)]
        others += [self.peer(axis, distance) for axis in (X, Y, Z) for distance in (1, 2, 3)]
        for device in others:
            pl.semaphore_signal(barrier, inc=1, device_id=device, device_id_type=MESH)
        return 16 + len(others) - 2 * self.same.astype(jnp.int32)


COUNTS = [-(-2 * LONG * (pair + 1) // 128) * 128 for pair in range(8)]
FIRSTS = [sum(COUNTS[:pair]) for pair in range(8)]


class Layer:
    def __init__(self, at, ref, own, index, rows):
        self.at = at
        self.r = ref
        self.s = own
        self.index = index
        self.rows = rows
        self.slope = own.slope if index else ref.dkey


    def _buffers(self, kind):
        s = self.s
        return (
            (s.kv_out, s.kv_in), (s.q_out, s.q_in), (s.dm_out, s.dm_in),
            (s.mix_out, s.mix_in), (s.dkv_out, s.dkv_in), (s.dq_out, s.dq_in),
        )[kind]

    def _copy(self, kind, index):
        at, sems = self.at, self.s.sems
        out, into = self._buffers(kind)
        if kind in (KV, Q, DM):
            (device, same), slot = at.holder(index), at.seq // 2
            target = at.seq if kind == KV else slot
        else:
            (device, same), slot = at.owner(index), at.head
            target = slot
        recv = sems.at[2, slot] if kind == KV else sems.at[1, kind]
        return out.at[index], into.at[target], sems.at[0, kind], recv, device, same

    def send_one(self, kind, index):
        src, dst, send, recv, device, same = self._copy(kind, index)

        @pl.when(same)
        def _():
            pltpu.make_async_copy(src, dst, recv).start()

        @pl.when(jnp.logical_not(same))
        def _():
            remote(src, dst, send, recv, device).start()

    def send_rest(self, kind):
        self.at.sending.append(lambda: self.sent(kind))
        self.at.coming[(self.index, kind)] = lambda: self.receive(kind)

    def send(self, kind):
        begin = self.at.seq // 2 if kind in (KV, Q, DM) else self.at.head

        def one(step, carry):
            self.send_one(kind, lax.rem(step + begin, 8))
            return carry

        lax.fori_loop(0, 8, one, 0)
        self.send_rest(kind)

    def _wait(self, place, send, recv):
        return remote(place, place, send, recv, self.at.partner())

    def receive(self, kind):
        self.at.coming.pop((self.index, kind), None)
        sems = self.s.sems
        self._wait(self._buffers(kind)[1], sems.at[0, kind], sems.at[1, kind]).wait_recv()

    def sent(self, kind):
        out, sems = self._buffers(kind)[0], self.s.sems

        @pl.when(self.at.same)
        def _():
            self._wait(out.at[pl.ds(0, 7)], sems.at[0, kind], sems.at[1, kind]).wait_send()

        @pl.when(jnp.logical_not(self.at.same))
        def _():
            self._wait(out, sems.at[0, kind], sems.at[1, kind]).wait_send()

    def _relay(self, index):
        place = self.s.kv_in.at[2 * index + self.at.core]
        sems = self.s.sems
        return remote(place, place, sems.at[0, 6], sems.at[1, 6], self.at.partner())

    def receive_keys(self):
        self.at.coming.pop((self.index, KV), None)
        s = self.s

        def one(index, carry):
            self._wait(s.kv_in.at[0], s.sems.at[0, KV], s.sems.at[2, index]).wait_recv()
            self._relay(index).start()
            return carry

        lax.fori_loop(0, 8, one, 0)
        relayed = self._wait(s.kv_in.at[pl.ds(0, 8)], s.sems.at[0, 6], s.sems.at[1, 6])
        relayed.wait_recv()
        self.at.sending.append(relayed.wait_send)


    def angles(self):
        table, first = self.r.offsets, self.r.firsts
        place = self.index * SEQ + self.at.seq
        cos_a, sin_a = first[0, pl.ds(place, 1), :], first[1, pl.ds(place, 1), :]
        cos_b, sin_b = table[0, : self.rows, :], table[1, : self.rows, :]
        return cos_a * cos_b - sin_a * sin_b, sin_a * cos_b + cos_a * sin_b

    def gain(self, which):
        return self.r.gains[self.index, which : which + 1, :].astype(F32)

    def project(self, values, ready=None):
        s, rows = self.s, self.rows
        normal, scale = normalize(values)
        s.normal[0] = normal
        s.scale[0] = jnp.broadcast_to(scale, (rows, 128))
        normed = (normal * self.gain(0)).astype(BF16)
        s.n1[...] = normed
        cosine, sine = self.angles()
        low = lanes((rows, 128)) < 64
        weight = self.r.wqkv.at[self.index]
        for group in range(GROUPS):
            key = dot(normed, weight[:, 512 + 128 * group : 640 + 128 * group])
            value = dot(normed, weight[:, 1024 + 128 * group : 1152 + 128 * group])
            key = key * cosine + half_turn(key) * sine
            value = pltpu.roll(value, 64, 1)
            s.kv_out[2 * group, :rows] = jnp.where(low, key, value).astype(BF16)
            s.kv_out[2 * group + 1, :rows] = jnp.where(low, value, key).astype(BF16)
            query = dot(normed, weight[:, 128 * group : 128 * group + 128])
            query = (query * cosine + half_turn(query) * sine) * 0.125
            s.q_out[2 * group], s.q_out[2 * group + 1] = pack_pair(query)
        if ready is not None:
            ready()
        self.send(KV)
        self.send(Q)

    def native(self, shape):
        return (lanes(shape) // 64) == lax.rem(self.at.seq, 2)

    def pack_one(self, values):
        rows = self.rows // 2
        return seal(jnp.where(self.native((rows, 128)), values[:rows], pltpu.roll(values[rows:], 64, 1)))

    def split_heads(self):
        s, length = self.s, SEQ * self.rows
        both = s.kv_in[:, : self.rows, :].reshape(length, 128).astype(F32)
        own = self.native((length, 128))
        s.key[...] = jnp.where(own, both, 0.0).astype(BF16)
        s.value[...] = jnp.where(own, pltpu.roll(both, 64, 1), 0.0).astype(BF16)

    def attend(self):
        s, core = self.s, self.at.core
        for index in range(8):
            s.query[index] = unpack_one(s.q_in[index], self.rows).astype(BF16)
        if self.index == 0:
            for pair in reversed(range(8)):
                count = COUNTS[pair]
                score = dot_nt(s.query[pair], s.key[:count])
                first = (288 * pair) // 128 * 128
                column = s.column[pair][:, :1]
                allowed = s.line[0:1, :count] == column
                position = sublanes((LONG, count - first)) + (2 * pair + core) * LONG
                causal = lanes((LONG, count - first)) + first <= position
                if first:
                    head = jnp.where(allowed[:, :first], score[:, :first], -1e9)
                    tail = jnp.where(allowed[:, first:] & causal, score[:, first:], -1e9)
                    score = jnp.concatenate([head, tail], 1)
                else:
                    score = jnp.where(allowed & causal, score, -1e9)
                top = jnp.max(score, -1, keepdims=True)
                expo = jnp.exp(score - top)
                share = 1.0 / jnp.sum(expo, -1, keepdims=True)
                expo = expo.astype(BF16)
                s.expo[:, FIRSTS[pair] : FIRSTS[pair] + count] = expo
                s.part[pair] = jnp.broadcast_to(share, (LONG, 128))
                s.mix_out[pair] = self.pack_one(dot(expo, s.value[:count]) * share)
                self.send_one(MIX, pair)
            self.send_rest(MIX)
        else:
            count, length = 8 * SHORT, SEQ * SHORT
            score = dot_nt(s.query[...].reshape(count, 128), s.key[...])
            column = s.column[...].reshape(count, 128)[:, :1]
            row = lax.broadcasted_iota(jnp.int32, (8, SHORT, length), 1)
            block = lax.broadcasted_iota(jnp.int32, (8, SHORT, length), 0)
            position = (row + (2 * block + core) * SHORT).reshape(count, length)
            causal = lanes((count, length)) <= position
            score = jnp.where((s.line[0:1, :] == column) & causal, score, -1e9)
            top = jnp.max(score, -1, keepdims=True)
            expo = jnp.exp(score - top)
            share = 1.0 / jnp.sum(expo, -1, keepdims=True)
            expo = expo.astype(BF16)
            s.expo[...] = expo
            s.part[...] = jnp.broadcast_to(share, (count, 128)).reshape(8, SHORT, 128)
            mixed = (dot(expo, s.value[...]) * share).reshape(8, SHORT, 128)
            for index in range(8):
                s.mix_out[index] = self.pack_one(mixed[index])
            self.send(MIX)

    def feed_forward(self, values):
        i, s = self.index, self.s
        parts = [unpack_pair(s.mix_in[2 * g], s.mix_in[2 * g + 1], self.rows) for g in range(GROUPS)]
        mixed = jnp.concatenate(parts, 1).astype(BF16)
        s.mixed[...] = mixed
        first = values + dot(mixed, self.r.wout[i])
        normal, scale = normalize(first)
        s.normal[1] = normal
        s.scale[1] = jnp.broadcast_to(scale, (self.rows, 128))
        normed = (normal * self.gain(1)).astype(BF16)
        s.n2[...] = normed
        result = first
        for part in range(4):
            at = slice(512 * part, 512 * part + 512)
            hidden = dot(normed, self.r.wup[i, :, at])
            inner = 0.7978845608028654 * (hidden + 0.044715 * hidden * hidden * hidden)
            bend = jnp.tanh(inner)
            active = (0.5 * hidden * (1.0 + bend)).astype(BF16)
            slope = 0.5 * (1.0 + bend) + 0.5 * hidden * (1.0 - bend * bend) * (
                0.7978845608028654 * (1.0 + 3.0 * 0.044715 * hidden * hidden)
            )
            for column in range(4):
                place = self.rows * (4 * part + column)
                self.slope[place : place + self.rows, :] = slope[:, 128 * column : 128 * column + 128]
            s.act[part // 2, :, 512 * (part % 2) : 512 * (part % 2) + 512] = active
            result = result + dot(active, self.r.wdown[i, at, :])
        return result


    def feed_back(self, grad):
        i, s = self.index, self.s
        low = grad.astype(BF16)
        s.glow[...] = low
        back = jnp.zeros((self.rows, D), F32)
        for part in range(4):
            at = slice(512 * part, 512 * part + 512)
            active = dot_nt(low, self.r.wdown[i, at, :])
            places = [self.rows * (4 * part + column) for column in range(4)]
            slope = jnp.concatenate([self.slope[place : place + self.rows, :] for place in places], 1)
            hidden = (slope * active).astype(BF16)
            s.dhid[part // 2, :, 512 * (part % 2) : 512 * (part % 2) + 512] = hidden
            back = back + dot_nt(hidden, self.r.wup[i, :, at])
        normal, scale = s.normal[1], s.scale[1][:, :1]
        self.r.gsum[2 * i + 1 : 2 * i + 2, :] = jnp.sum(back * normal, 0, keepdims=True)
        first = grad + normalize_back(back, normal, scale, self.gain(1))
        s.dfirst[...] = first
        first_low = first.astype(BF16)
        s.dv1[0] = first_low[:, :256]
        s.dv1[1] = first_low[:, 256:]
        for group in range(GROUPS):
            weight = self.r.wout[i, 128 * group : 128 * group + 128, :]
            s.dm_out[2 * group], s.dm_out[2 * group + 1] = pack_pair(dot_nt(first_low, weight))
        self.send(DM)

    def attend_back(self, between):
        s, length = self.s, SEQ * self.rows
        own = self.native((length, 128))
        if self.index == 0:
            self.r.dkey[...] = jnp.zeros((length, 128), F32)
            self.r.dvalue[...] = jnp.zeros((length, 128), F32)
            for pair in reversed(range(8)):
                count = COUNTS[pair]
                share = s.part[pair]
                grad = (unpack_one(s.dm_in[pair], self.rows) * share).astype(BF16)
                expo = s.expo[:, FIRSTS[pair] : FIRSTS[pair] + count]
                weighted = expo * dot_nt(grad, s.value[:count])
                inner = jnp.sum(weighted, -1, keepdims=True) * share[:, :1]
                draw = (weighted - expo * inner).astype(BF16)
                s.dq_out[pair] = self.pack_one(dot(draw, s.key[:count]) * 0.125)
                self.r.dkey[:count] += dot_tn(draw, s.query[pair])
                self.r.dvalue[:count] += dot_tn(expo, grad)
                if pair == 5:
                    between(2)
            dkey, dvalue = self.r.dkey[...], self.r.dvalue[...]
        else:
            count = 8 * SHORT
            share = s.part[...].reshape(count, 128)
            grad = jnp.concatenate([unpack_one(s.dm_in[index], self.rows) for index in range(8)], 0)
            grad = (grad * share).astype(BF16)
            expo = s.expo[...]
            weighted = expo * dot_nt(grad, s.value[...])
            inner = jnp.sum(weighted, -1, keepdims=True) * share[:, :1]
            draw = (weighted - expo * inner).astype(BF16)
            dq = (dot(draw, s.key[...]) * 0.125).reshape(8, SHORT, 128)
            for index in range(8):
                s.dq_out[index] = self.pack_one(dq[index])
            dkey = dot_tn(draw, s.query[...].reshape(count, 128))
            dvalue = dot_tn(expo, grad)
        self.send(DQ)
        both = jnp.where(own, dkey, pltpu.roll(dvalue, 64, 1)).astype(BF16)
        both = both.reshape(8, 2, self.rows, 128)
        for which in range(2):
            s.dkv_part[which] = both[:, which]

    def _merge(self):
        s = self.s
        return remote(
            s.dkv_part.at[1 - self.at.core], s.dkv_other, s.sems.at[0, 7], s.sems.at[1, 7], self.at.partner()
        )

    def merge_start(self):
        self.at.start(self._merge(), (self.index, 14))

    def merge(self):
        s = self.s
        self.at.finish(self._merge(), (self.index, 14))
        s.dkv_out[...] = (s.dkv_part[self.at.core].astype(F32) + s.dkv_other[...].astype(F32)).astype(BF16)

    def project_back(self):
        i, s, rows = self.index, self.s, self.rows
        cosine, sine = self.angles()
        low = lanes((rows, 128)) < 64
        back = jnp.zeros((rows, D), F32)
        for group in range(GROUPS):
            even, odd = s.dkv_in[2 * group].astype(F32), s.dkv_in[2 * group + 1].astype(F32)
            key = jnp.where(low, even, odd)
            key = key * cosine - half_turn(key) * sine
            value = pltpu.roll(jnp.where(low, odd, even), 64, 1)
            query = unpack_pair(s.dq_in[2 * group], s.dq_in[2 * group + 1], rows)
            query = query * cosine - half_turn(query) * sine
            for which, piece in enumerate((query, key, value)):
                place = 4 * which + group
                column = 128 * (place % 6)
                s.dproj[place // 6, :, column : column + 128] = piece.astype(BF16)
        for part in range(2):
            back = back + dot_nt(s.dproj[part], self.r.wqkv[i, :, 768 * part : 768 * part + 768])
        normal, scale = s.normal[0], s.scale[0][:, :1]
        self.r.gsum[2 * i : 2 * i + 1, :] = jnp.sum(back * normal, 0, keepdims=True)
        return s.dfirst[...] + normalize_back(back, normal, scale, self.gain(0))


    def _swap(self, which):
        s, other = self.s, 1 - self.at.core
        src, dst = (
            (s.glow, s.glow_in), (s.n2, s.n2_in), (s.act.at[other], s.act_in), (s.dhid.at[other], s.dhid_in),
            (s.mixed, s.mixed_in), (s.dv1.at[other], s.dv1_in), (s.n1, s.n1_in), (s.dproj.at[other], s.dproj_in),
        )[which]
        return remote(src, dst, s.sems.at[3, which], s.sems.at[4, which], self.at.partner())

    def swap(self, steps):
        copies = [self._swap(which) for which in steps]
        for copy in copies:
            copy.start()
        self.at.sending += [copy.wait_send for copy in copies]
        self.at.coming[(self.index, 10, steps)] = lambda: [copy.wait_recv() for copy in copies]

    def swapped(self, steps):
        self.at.coming.pop((self.index, 10, steps))()

    def grads_feed(self, total):
        s, core = self.s, self.at.core
        for part in range(4):
            at = slice(256 * part, 256 * part + 256)
            total.put_rows(
                part, dot_tn(s.act[core, :, at], s.glow[...]) + dot_tn(s.act_in[:, at], s.glow_in[...])
            )
        for part in range(2):
            at = slice(512 * part, 512 * part + 512)
            up = dot_tn(s.n2[...], s.dhid[core, :, at]) + dot_tn(s.n2_in[...], s.dhid_in[:, at])
            total.put_columns(4 + 2 * part, up[:, :256])
            total.put_columns(5 + 2 * part, up[:, 256:])
        total.put_columns(8, dot_tn(s.mixed[...], s.dv1[core]) + dot_tn(s.mixed_in[...], s.dv1_in[...]))

    def grads_attention(self, total, first):
        s, core = self.s, self.at.core
        grad = dot_tn(s.n1[...], s.dproj[core]) + dot_tn(s.n1_in[...], s.dproj_in[...])
        for part in range(3):
            total.put_columns(first + part, grad[:, 256 * part : 256 * part + 256])


class Total:
    def __init__(self, at, own, kind, result):
        self.at, self.s, self.kind, self.result = at, own, kind, result
        self.first, self.units = own.first, own.grads.shape[1]
        self.ring = self.units > 1

    def put_rows(self, unit, values):
        values = values.astype(BF16)
        for group in range(4):
            self.s.grads[unit // self.units, unit % self.units, group] = values[
                :, 128 * group : 128 * group + 128
            ].reshape(4, 4, 16, 128)

    def put_columns(self, unit, values):
        values = values.astype(BF16)
        for group in range(2):
            self.s.grads[unit // self.units, unit % self.units, 2 * group : 2 * group + 2] = values[
                :, 128 * group : 128 * group + 128
            ].reshape(2, 4, 4, 16, 128)

    def _full(self, part, *places):
        return self.result.at[(self.at.core, part, pl.ds(self.first, self.units), *places)]

    def _place(self, part, stage, distance=0):
        return lax.rem(self.at.at[ORDERS[part][stage]] + distance, 4)

    def _remote(self, src, dst, part, stage, row, distance):
        sems = self.s.sems
        return remote(src, dst, sems.at[row, 3], sems.at[row, part], self.at.peer(ORDERS[part][stage], distance))

    def _scatter(self, part, stage, distance):
        s = self.s
        src = (s.grads, s.sum1, s.sum2)[stage].at[part, :, self._place(part, stage, distance)]
        dst = (s.part0, s.part1, s.part2)[stage].at[part, distance - 1]
        return self._remote(src, dst, part, stage, stage, distance)

    def _gather(self, part, stage, distance):
        place = self._full(part, *[self._place(part, before) for before in range(stage + 1)])
        return self._remote(place, place, part, stage, 3 + stage, distance)

    def _wait(self, row, part=None):
        s = self.s
        place = (s.part0, s.part1, s.part2, s.part0, s.part1, s.part2, None, None, None, s.hop, s.hop)[row]
        sems = s.sems.at[row]
        if part is None:
            remote(place, place, sems.at[3], sems.at[0], self.at.partner()).wait_send()
        else:
            remote(place.at[part], place.at[part], sems.at[3], sems.at[part], self.at.partner()).wait_recv()

    def _begin(self, copies, row, part):
        for copy in copies:
            copy.start()
        self.at.coming[(self.kind, row, part)] = lambda: self._wait(row, part)
        if part == 2:
            self.at.sending.append(lambda: self._wait(row))

    def _arrive(self, row, part):
        self.at.coming.pop((self.kind, row, part))()

    def _direct(self, make, part, stage, row):
        self._begin([make(part, stage, distance) for distance in (1, 3, 2)], row, part)

    def scatter(self):
        s = self.s
        for part in range(3):
            if not self.ring:
                self._direct(self._scatter, part, 0, 0)
                continue
            opposite = s.grads.at[part, :, self._place(part, 0, 2)]
            copies = [
                self._remote(opposite.at[:, pl.ds(2 * way, 2)], s.hop.at[part, way], part, 0, HOP, distance)
                for way, distance in enumerate((1, 3))
            ]
            self._begin(copies, HOP, part)

    def turn(self):
        s = self.s
        for part in range(3):
            self._arrive(HOP, part)
            copies = []
            for way, distance in enumerate((1, 3)):
                place = self._place(part, 0, distance)
                half = pl.ds(2 * way, 2)
                total = s.grads[part, :, place, half].astype(F32) + s.hop[part, way].astype(F32)
                s.grads[part, :, place, half] = total.astype(BF16)
                copies.append(self._remote(s.grads.at[part, :, place], s.part0.at[part, way], part, 0, 0, distance))
            self._begin(copies, 0, part)

    def scattered(self, stage):
        s = self.s
        for part in range(3):
            self._arrive(stage, part)
            src = (s.grads, s.sum1, s.sum2)[stage]
            got = (s.part0, s.part1, s.part2)[stage]
            total = src[part, :, self._place(part, stage)].astype(F32)
            for index in range(got.shape[1]):
                total = total + got[part, index].astype(F32)
            total = total.astype(BF16)
            if stage == 0:
                s.sum1[part] = total
            elif stage == 1:
                s.sum2[part] = total
            else:
                places = [self._place(part, before) for before in range(3)]
                self.result[(self.at.core, part, pl.ds(self.first, self.units), *places)] = total
            if stage < 2:
                self._direct(self._scatter, part, stage + 1, stage + 1)
            else:
                self._direct(self._gather, part, 2, 5)

    def gathered(self, stage):
        for part in range(3):
            self._arrive(3 + stage, part)
            if stage == 2:
                self._direct(self._gather, part, 1, 4)
            else:
                if self.ring:
                    self._begin([self._gather(part, 0, distance) for distance in (1, 3)], 3, part)
                else:
                    self._direct(self._gather, part, 0, 3)
                self._pass(part, (0,))

    def gather_turn(self):
        s = self.s
        for part in range(3):
            self._arrive(3, part)
            copies = []
            for way, distance in enumerate((1, 3)):
                place = self._full(part, self._place(part, 0, 4 - distance), pl.ds(2 * way, 2))
                copies.append(self._remote(place, place, part, 0, BACK, distance))
            self._begin(copies, BACK, part)
            self._pass(part, (1, 3))

    def gather_done(self):
        for part in range(3):
            self._arrive(BACK if self.ring else 3, part)
            self._pass(part, (2,) if self.ring else (1, 2, 3))

    def _pass(self, part, distances):
        send, recv = self.s.sems.at[6, part], self.s.sems.at[7, part]
        for distance in distances:
            place = self._full(part, self._place(part, 0, distance))
            remote(place, place, send, recv, self.at.partner()).start()
        if 2 in distances:
            whole = self._full(part)
            passed = remote(whole, whole, send, recv, self.at.partner())
            self.at.coming[(self.kind, 6, part)] = passed.wait_recv
            self.at.sending.append(passed.wait_send)


def vmem(**shapes):
    return {name: pltpu.VMEM(shape, kind) for name, (shape, kind) in shapes.items()}


def layer_scratch(index, rows):
    length, half = SEQ * rows, padded(rows)
    message = rows + (NOTE if index == 0 else 0)
    shapes = vmem(
        kv_out=((8, message, 128), BF16), kv_in=((SEQ, message, 128), BF16),
        q_out=((8, half, 128), BF16), q_in=((8, half, 128), BF16),
        dm_out=((8, half, 128), BF16), dm_in=((8, half, 128), BF16),
        mix_out=((8, half, 128), BF16), mix_in=((8, half, 128), BF16),
        dq_out=((8, half, 128), BF16), dq_in=((8, half, 128), BF16),
        dkv_part=((2, 8, rows, 128), BF16), dkv_other=((8, rows, 128), BF16),
        dkv_out=((8, rows, 128), BF16), dkv_in=((8, rows, 128), BF16),
        query=((8, rows, 128), BF16), key=((length, 128), BF16), value=((length, 128), BF16),
        expo=((rows, sum(COUNTS)) if index == 0 else (8 * rows, length), BF16), part=((8, rows, 128), F32),
        normal=((2, rows, D), F32), scale=((2, rows, 128), F32),
        dfirst=((rows, D), F32),
        n1=((rows, D), BF16), n2=((rows, D), BF16), mixed=((rows, D), BF16), glow=((rows, D), BF16),
        act=((2, rows, FF // 2), BF16), dhid=((2, rows, FF // 2), BF16),
        dv1=((2, rows, 256), BF16), dproj=((2, rows, 768), BF16),
        n1_in=((rows, D), BF16), n2_in=((rows, D), BF16), mixed_in=((rows, D), BF16), glow_in=((rows, D), BF16),
        act_in=((rows, FF // 2), BF16), dhid_in=((rows, FF // 2), BF16),
        dv1_in=((rows, 256), BF16), dproj_in=((rows, 768), BF16),
        column=((8, rows, 128), F32), line=((8, length), F32),
    )
    if index:
        shapes.update(vmem(slope=((length, 128), F32)))
    shapes.update(sems=pltpu.SemaphoreType.DMA((5, 8)))
    return shapes


def total_scratch(units):
    ways = 2 if units > 1 else 3
    shapes = vmem(
        hop=((3, 2, units, 2, 4, 16, 128), BF16),
        grads=((3, units, 4, 4, 4, 16, 128), BF16),
        part0=((3, ways, units, 4, 4, 16, 128), BF16), sum1=((3, units, 4, 4, 16, 128), BF16),
        part1=((3, 3, units, 4, 16, 128), BF16), sum2=((3, units, 4, 16, 128), BF16),
        part2=((3, 3, units, 16, 128), BF16),
    )
    shapes.update(sems=pltpu.SemaphoreType.DMA((11, 4)))
    return shapes


def common_scratch():
    shapes = vmem(
        tokens=((LONG, D), BF16), cot=((LONG, D), BF16), seg=((1, LONG), jnp.int32), gains=((2, 2, D), BF16),
        offsets=((2, LONG, 128), F32), firsts=((2, 2 * SEQ, 128), F32),
        wqkv=((2, D, 3 * D), BF16), wout=((2, D, D), BF16),
        wup=((2, D, FF), BF16), wdown=((2, FF, D), BF16),
        dkey=((SEQ * LONG, 128), F32), dvalue=((SEQ * LONG, 128), F32),
        second=((4, LONG + 8, 128), F32), share=((4, SHORT + 8, 128), F32),
        work=((4, LONG, 128), F32), spread=((4, LONG, 128), F32),
        tail=((4, 8, 128), F32), ahead=((4, 8, 128), F32),
        output=((LONG, D), BF16), result=((LONG, D), F32),
        gsum=((8, D), F32), gain_in=((4, 4, 8, D), F32), gain_out=((3, 8, D), F32),
    )
    shapes.update(more=pltpu.SemaphoreType.DMA((41,)))
    return shapes


SPACES = (
    common_scratch(), layer_scratch(0, LONG), layer_scratch(1, SHORT),
    *(total_scratch(units) for units in UNITS),
)


def body(*refs):
    spaces, place = [], 14
    for part in SPACES:
        spaces.append(types.SimpleNamespace(**dict(zip(part, refs[place : place + len(part)]))))
        place += len(part)
    at = Place()
    steps(at, spaces, *refs[:14])
    for wait in at.coming.values():
        wait()
    for wait in at.sending:
        wait()


def steps(
    at, spaces, tokens, seg, wqkv, wout, wup, wdown, gains, cot, offsets, firsts,
    output, tokens_grad, sums, gain_sum,
):
    ref = spaces[0]
    more = ref.more
    full, short = Layer(at, ref, spaces[1], 0, LONG), Layer(at, ref, spaces[2], 1, SHORT)
    for kind in range(3):
        spaces[3 + kind].first = sum(UNITS[:kind])
    early, middle, late = (Total(at, spaces[3 + kind], 20 + kind, sums) for kind in range(3))

    pairs = [
        (tokens, ref.tokens), (gains, ref.gains), (wqkv.at[0], ref.wqkv.at[0]),
        (offsets, ref.offsets), (firsts, ref.firsts), (seg, ref.seg),
        (wout.at[0], ref.wout.at[0]), (wup.at[0], ref.wup.at[0]), (wdown.at[0], ref.wdown.at[0]),
        (wqkv.at[1], ref.wqkv.at[1]), (cot, ref.cot),
        (wout.at[1], ref.wout.at[1]), (wup.at[1], ref.wup.at[1]), (wdown.at[1], ref.wdown.at[1]),
    ]
    loads = [pltpu.make_async_copy(src, dst, more.at[step]) for step, (src, dst) in enumerate(pairs)]
    for load in loads:
        load.start()
    waiting = list(range(len(loads)))

    def loaded(count):
        while waiting and waiting[0] < count:
            loads[waiting.pop(0)].wait()

    at.sending.append(lambda: loaded(len(loads)))
    barrier = pltpu.get_barrier_semaphore()
    greeted = at.greet(barrier)

    loaded(6)
    inputs = ref.tokens[...].astype(F32)
    def ready():
        line = ref.seg[...].astype(F32)
        high = jnp.floor(line * (1.0 / 64.0))
        rows = jnp.concatenate([high, line - 64.0 * high, jnp.zeros((6, LONG), F32)], 0)
        third = jnp.where(sublanes((LONG, 128)) == 3 * lanes((LONG, 128)), 1.0, 0.0)
        picked = dot(rows, third)
        wide = jnp.concatenate([rows[:, 128:], jnp.zeros((8, 112), F32)], 1)
        note = jnp.concatenate([rows[0:2, :128], wide[0:2], picked[0:2], jnp.zeros((10, 128), F32)], 0)
        for head in range(8):
            full.s.kv_out[head, LONG:] = note.astype(BF16)
        pl.semaphore_wait(barrier, greeted)

    full.project(inputs, ready)

    def segments():
        notes = [full.s.kv_in[block, LONG:, :].astype(F32) for block in range(SEQ)]
        for block, code in enumerate(notes):
            long = jnp.concatenate([64.0 * code[0:1] + code[1:2], 64.0 * code[2:3, :16] + code[3:4, :16]], 1)
            full.s.line[0:1, LONG * block : LONG * block + LONG] = long
            short.s.line[0:1, SHORT * block : SHORT * block + SHORT] = (64.0 * code[4:5] + code[5:6])[:, :SHORT]
        for layer in (full, short):
            rows = layer.rows
            equal = lanes((rows, rows)) == sublanes((rows, rows))
            for pair in range(8):
                code = full.s.kv_in[2 * pair + at.core, LONG:, :].astype(F32)
                if layer is full:
                    line = jnp.concatenate([64.0 * code[0:1] + code[1:2], 64.0 * code[2:3, :16] + code[3:4, :16]], 1)
                else:
                    line = (64.0 * code[4:5] + code[5:6])[:, :SHORT]
                column = jnp.sum(jnp.where(equal, line, 0.0), 1, keepdims=True)
                layer.s.column[pair] = jnp.broadcast_to(column, (rows, 128))

    def attention(layer):
        layer.receive_keys()
        layer.receive(Q)
        if layer is full:
            segments()
        layer.split_heads()
        layer.attend()
        layer.receive(MIX)

    attention(full)
    loaded(9)
    second = ref.second
    spill(second, 8, full.feed_forward(inputs))

    def halo():
        return remote(second.at[:, pl.ds(LONG, 8), :], ref.tail, more.at[17], more.at[18], at.along(1))

    at.start(halo(), (3, 0))
    loaded(11)
    work = ref.work
    spill(work, 0, ref.cot[...].astype(F32))
    grad_short = jnp.concatenate(
        [every_third(work, 0, g) + every_third(work, 1, g) + every_third(work, 2, g) for g in range(GROUPS)], 1
    )
    at.finish(halo(), (3, 0))
    second[:, 0:8, :] = jnp.where(at.seq == 0, 0.0, ref.tail[...])
    pooled = jnp.concatenate(
        [
            (every_third(second, 6, g) + every_third(second, 7, g) + every_third(second, 8, g)) / 3.0
            for g in range(GROUPS)
        ],
        1,
    )
    short.project(pooled)
    loaded(14)
    attention(short)
    result = short.feed_forward(pooled)

    def backward(layer, total, grad, between):
        layer.feed_back(grad)
        layer.swap(SEVEN)
        between(0)
        layer.swapped(SEVEN)
        layer.grads_feed(total)
        between(1)
        layer.receive(DM)
        layer.attend_back(between)
        layer.merge_start()
        between(3)
        layer.merge()
        layer.send(DKV)
        between(4)
        layer.receive(DQ)
        layer.receive(DKV)
        back = layer.project_back()
        layer.swap((7,))
        return back

    spread = ref.spread

    def finish_output():
        for group in range(GROUPS):
            at_lanes = slice(128 * group, 128 * group + 128)
            for step in range(3):
                spread[group, pl.ds(step, SHORT, 3), :] = every_third(second, 8 + step, group) + result[:, at_lanes]
            ref.output[:, at_lanes] = spread[group].astype(BF16)
        store = pltpu.make_async_copy(ref.output, output, more.at[14])
        store.start()
        at.sending.append(store.wait)

    def between_short(point):
        if point == 0:
            finish_output()
        elif point == 4:
            early.scatter()

    share = ref.share
    spill(share, 0, backward(short, early, grad_short, between_short) * (1.0 / 3.0))

    def halo_back():
        return remote(share.at[:, pl.ds(0, 8), :], ref.ahead, more.at[19], more.at[20], at.along(SEQ - 1))

    at.start(halo_back(), (3, 1))
    early.turn()
    short.swapped((7,))
    short.grads_attention(middle, 9)
    at.finish(halo_back(), (3, 1))
    share[:, SHORT:, :] = jnp.where(at.seq == SEQ - 1, 0.0, ref.ahead[...])
    for group in range(GROUPS):
        own, following = share[group, 0:SHORT, :], share[group, 1 : SHORT + 1, :]
        for step, piece in enumerate((own, following, following)):
            spread[group, pl.ds(step, SHORT, 3), :] = every_third(work, step, group) + piece
    grad_full = jnp.concatenate([spread[group] for group in range(GROUPS)], 1)

    def between_full(point):
        if point == 0:
            early.scattered(0)
        elif point == 1:
            middle.scatter()
            early.scattered(1)
        elif point == 2:
            early.scattered(2)
            middle.turn()
        elif point == 3:
            early.gathered(2)
        else:
            middle.scattered(0)
            early.gathered(1)

    ref.result[...] = backward(full, middle, grad_full, between_full)
    store = pltpu.make_async_copy(ref.result, tokens_grad, more.at[15])
    store.start()
    at.sending.append(store.wait)
    middle.scattered(1)
    full.swapped((7,))
    full.grads_attention(late, 0)
    late.scatter()

    gsum, gain_in, gain_out = ref.gsum, ref.gain_in, ref.gain_out

    def gain_copy(axis, distance):
        src = gsum if axis == 0 else gain_out.at[axis - 1]
        return remote(
            src, gain_in.at[axis, at.at[axis]], more.at[22 + 3 * axis + distance], more.at[31 + 3 * axis + distance],
            at.peer(axis, distance),
        )

    def gain_step(axis):
        for distance in (1, 2, 3):
            at.start(gain_copy(axis, distance), (4, axis, distance))
        gain_in[axis, at.at[axis]] = gsum[...] if axis == 0 else gain_out[axis - 1]

    def gain_done(axis):
        for distance in (1, 2, 3):
            at.finish(gain_copy(axis, distance), (4, axis, distance))
        return (gain_in[axis, 0] + gain_in[axis, 1]) + (gain_in[axis, 2] + gain_in[axis, 3])

    gsum[4:, :] = jnp.zeros((4, D), F32)
    gain_step(0)
    early.gather_turn()
    middle.scattered(2)
    late.scattered(0)
    gain_out[0] = gain_done(0)
    gain_step(1)
    middle.gathered(2)
    late.scattered(1)
    gain_out[1] = gain_done(1)
    gain_step(2)
    early.gather_done()
    late.scattered(2)
    middle.gathered(1)
    late.gathered(2)
    middle.gather_turn()
    late.gathered(1)
    gain_in[3, 0] = gain_done(2)
    gain_swap = remote(gain_in.at[3, 0], gain_in.at[3, 1], more.at[21], more.at[22], at.partner())
    at.start(gain_swap, (4, 3, 0))
    middle.gather_done()
    late.gather_done()
    at.finish(gain_swap, (4, 3, 0))
    gain_out[2] = gain_in[3, 0] + gain_in[3, 1]
    store = pltpu.make_async_copy(gain_out.at[2], gain_sum, more.at[16])
    store.start()
    at.sending.append(store.wait)


def tables():
    freq = 10000.0 ** (-np.arange(32) / 32.0)
    freq = np.tile(freq, 4)[None, :]
    offset = np.arange(LONG)[:, None] * freq
    first = np.concatenate([np.arange(SEQ) * LONG, np.arange(SEQ) * SHORT])[:, None] * freq
    return (
        np.stack([np.cos(offset), np.sin(offset)]).astype(np.float32),
        np.stack([np.cos(first), np.sin(first)]).astype(np.float32),
    )


def widen_body(
    sums, gain, output, grad, qkv, out, up, down, gains, output_too, grad_too,
    gain_in, gain_out, output_in, grad_in, down_out, up_out, out_out, qkv_out, sems,
):
    small = [
        pltpu.make_async_copy(gain, gain_in, sems.at[0, 0]),
        pltpu.make_async_copy(output, output_in, sems.at[0, 1]),
        pltpu.make_async_copy(grad, grad_in, sems.at[0, 2]),
    ]
    stores = []
    for copy in small:
        copy.start()

    def put(dst, src, slot):
        copy = pltpu.make_async_copy(src, dst, sems.at[1 + slot // 8, slot % 8])
        copy.start()
        stores.append(copy)

    def tiles(kind, half, unit):
        return sums.at[half, unit // UNITS[kind], sum(UNITS[:kind]) + unit % UNITS[kind]]

    def rows_of(kind, half, unit, dst, first_row):
        ref = tiles(kind, half, unit)
        for group in range(4):
            values = ref[group].reshape(256, 128).astype(F32)
            dst[first_row : first_row + 256, 128 * group : 128 * group + 128] = values

    def columns_of(kind, half, unit, dst, column):
        ref = tiles(kind, half, unit)
        for group in range(2):
            values = ref[2 * group : 2 * group + 2].reshape(512, 128).astype(F32)
            dst[:, column + 128 * group : column + 128 * group + 128] = values

    def feed(kind, half, block):
        at = 2 * block + half
        for unit in range(4):
            rows_of(kind, half, unit, down_out.at[at], 256 * unit)
        put(down.at[block, pl.ds(1024 * half, 1024), :], down_out.at[at], at)

    def rest(kind, block, kind_heads, unit):
        for half in range(2):
            for part in range(4):
                columns_of(kind, half, 4 + part, up_out.at[block], 1024 * half + 256 * part)
        put(up.at[block], up_out.at[block], 4 + block)
        for half in range(2):
            columns_of(kind, half, 8, out_out.at[block], 256 * half)
        put(out.at[block], out_out.at[block], 6 + block)
        for half in range(2):
            for part in range(3):
                columns_of(kind_heads, half, unit + part, qkv_out.at[block], 768 * half + 256 * part)
        put(qkv.at[block], qkv_out.at[block], 8 + block)

    def through():
        for copy in small:
            copy.wait()
        gain_out[...] = gain_in[0:4, :].reshape(2, 2, D)
        put(gains, gain_out, 10)
        put(output_too.at[0], output_in, 11)
        put(grad_too.at[0], grad_in, 12)

    for kind, block, kind_heads, unit in ((0, 1, 1, 9), (1, 0, 2, 0)):
        for half in range(2):
            feed(kind, half, block)
        rest(kind, block, kind_heads, unit)
        if kind == 0:
            through()
    for copy in stores:
        copy.wait()


def widen(sums, gain, output, grad):
    anywhere, inside = pl.BlockSpec(memory_space=pl.ANY), pl.BlockSpec(memory_space=pltpu.VMEM)
    return pl.pallas_call(
        widen_body,
        out_shape=(
            jax.ShapeDtypeStruct((2, D, 3 * D), F32),
            jax.ShapeDtypeStruct((2, D, D), F32),
            jax.ShapeDtypeStruct((2, D, FF), F32),
            jax.ShapeDtypeStruct((2, FF, D), F32),
            jax.ShapeDtypeStruct((2, 2, D), F32),
            jax.ShapeDtypeStruct((1, LONG, D), BF16),
            jax.ShapeDtypeStruct((1, LONG, D), F32),
        ),
        in_specs=[inside] + [anywhere] * 3,
        out_specs=(anywhere,) * 7,
        scratch_shapes=[
            pltpu.VMEM((8, D), F32),
            pltpu.VMEM((2, 2, D), F32),
            pltpu.VMEM((LONG, D), BF16),
            pltpu.VMEM((LONG, D), F32),
            pltpu.VMEM((4, 1024, 512), F32),
            pltpu.VMEM((2, 512, 2048), F32),
            pltpu.VMEM((2, 512, 512), F32),
            pltpu.VMEM((2, 512, 1536), F32),
            pltpu.SemaphoreType.DMA((3, 8)),
        ],
        compiler_params=pltpu.CompilerParams(vmem_limit_bytes=40 * 2**20),
        name="widen",
    )(
        pltpu.with_memory_space_constraint(sums, pltpu.VMEM),
        *(pltpu.with_memory_space_constraint(array, pltpu.HBM) for array in (gain, output, grad)),
    )


def per_device(tokens, segment, w_qkv, w_out, w_up, w_down, gains, cotangent):
    offsets, firsts = tables()
    anywhere, inside = pl.BlockSpec(memory_space=pl.ANY), pl.BlockSpec(memory_space=pltpu.VMEM)
    output, tokens_grad, sums, gain = pl.pallas_call(
        body,
        out_shape=(
            jax.ShapeDtypeStruct((LONG, D), BF16),
            jax.ShapeDtypeStruct((LONG, D), F32),
            pltpu.VMEM((2, 3, sum(UNITS), 4, 4, 4, 16, 128), BF16),
            jax.ShapeDtypeStruct((8, D), F32),
        ),
        in_specs=[anywhere] * 10,
        out_specs=(anywhere, anywhere, inside, anywhere),
        scratch_shapes=[shape for part in SPACES for shape in part.values()],
        compiler_params=pltpu.CompilerParams(
            collective_id=0, has_side_effects=True, vmem_limit_bytes=51 * 2**20
        ),
        name="layers",
    )(
        tokens[0], segment, w_qkv, w_out, w_up, w_down, gains, cotangent[0],
        jnp.asarray(offsets), jnp.asarray(firsts),
    )
    qkv, out, up, down, gain, output, tokens_grad = widen(sums, gain, output, tokens_grad)
    return output, tokens_grad, qkv, out, up, down, gain


def solution(mesh):
    return jax.shard_map(
        per_device,
        mesh=mesh,
        in_specs=(
            P("row", "seq", None),
            P("row", "seq"),
            P(),
            P(),
            P(),
            P(),
            P(),
            P("row", "seq", None),
        ),
        out_specs=(P("row", "seq", None), P("row", "seq", None), P(), P(), P(), P(), P()),
        check_vma=False,
    )
```

```python
import types

import jax
import jax.numpy as jnp
import numpy as np
from jax import lax
from jax.experimental import pallas as pl
from jax.experimental.pallas import tpu as pltpu
from jax.sharding import PartitionSpec as P

MESH = pl.DeviceIdType.MESH
F32 = jnp.float32
BF16 = jnp.bfloat16

SEQ = 16
LONG = 144
SHORT = 48
D = 512
FF = 2048
GROUPS = 4
NOTE = 16
KV, Q, DM, MIX, DKV, DQ, RELAY, TAIL, MERGE = range(9)
AHEAD, BEHIND = (1, 2, 4, 6), (0, 3, 5)
EXTRA = 16
UNITS = (3, 3, 1, 1)
HOP, BACK = 7, 8
X, Y, Z = range(3)
ORDERS = ((X, Y, Z), (Y, Z, X), (Z, X, Y))


def dot(left, right):
    return jnp.dot(left, right, preferred_element_type=F32)


def dot_nt(left, right):
    return lax.dot_general(left, right, (((1,), (1,)), ((), ())), preferred_element_type=F32)


def dot_tn(left, right):
    return lax.dot_general(left, right, (((0,), (0,)), ((), ())), preferred_element_type=F32)


def lanes(shape):
    return lax.broadcasted_iota(jnp.int32, shape, len(shape) - 1)


def sublanes(shape):
    return lax.broadcasted_iota(jnp.int32, shape, len(shape) - 2)


def normalize(values):
    center = values - jnp.mean(values, -1, keepdims=True)
    scale = lax.rsqrt(jnp.mean(center * center, -1, keepdims=True) + 1e-05)
    return center * scale, scale


def normalize_back(grad, normal, scale, gain):
    inner = grad * gain
    return scale * (
        inner
        - jnp.mean(inner, -1, keepdims=True)
        - normal * jnp.mean(inner * normal, -1, keepdims=True)
    )


def half_turn(tensor):
    up = pltpu.roll(tensor, 96, 1)
    down = pltpu.roll(tensor, 32, 1)
    return jnp.where(lanes(tensor.shape) % 64 < 32, -up, down)


def padded(rows):
    return -(-rows // 32) * 16


def seal(packed):
    rows = packed.shape[0]
    return jnp.concatenate([packed, jnp.zeros((padded(2 * rows) - rows, 128), F32)], 0).astype(BF16)


def pack_pair(pair):
    rows = pair.shape[0] // 2
    top, bottom = pair[:rows], pltpu.roll(pair[rows:], 64, 1)
    low = lanes(top.shape) < 64
    return seal(jnp.where(low, top, bottom)), seal(jnp.where(low, bottom, top))


def unpack_pair(even, odd, rows):
    even, odd = even.astype(F32)[: rows // 2], odd.astype(F32)[: rows // 2]
    low = lanes(even.shape) < 64
    return jnp.concatenate([jnp.where(low, even, odd), pltpu.roll(jnp.where(low, odd, even), 64, 1)], 0)


def unpack_one(packed, rows):
    packed = packed.astype(F32)[: rows // 2]
    return jnp.concatenate([packed, pltpu.roll(packed, 64, 1)], 0)


def spill(ref, first, values):
    for group in range(GROUPS):
        ref[group, first : first + values.shape[0], :] = values[:, 128 * group : 128 * group + 128]


def every_third(ref, first, group):
    return ref[group, pl.ds(first, SHORT, 3), :]


def remote(src, dst, send, recv, device):
    return pltpu.make_async_remote_copy(
        src_ref=src, dst_ref=dst, send_sem=send, recv_sem=recv, device_id=device, device_id_type=MESH
    )


class Place:
    def __init__(self):
        self.row = lax.axis_index("row")
        self.seq = lax.axis_index("seq")
        self.core = lax.rem(self.row, 2)
        self.at = (self.row // 2, lax.rem(self.seq, 4), self.seq // 4)
        self.head = lax.rem(self.seq, 8)
        self.near = self.seq // 8 == self.core
        odd = lax.rem(self.seq, 2)
        self.same, self.next = self.near & (odd == self.core), self.near & (odd != self.core)
        self.sending, self.coming = [], {}

    def peer(self, axis, distance):
        to = lax.rem(self.at[axis] + distance, 4)
        if axis == X:
            return (to * 2 + self.core, self.seq)
        if axis == Y:
            return (self.row, self.at[Z] * 4 + to)
        return (self.row, to * 4 + self.at[Y])

    def partner(self):
        return (self.row + 1 - 2 * self.core, self.seq)

    def along(self, distance):
        return (self.row, lax.rem(self.seq + distance, SEQ))

    def _with_same(self, row, seq):
        return (row, seq), (row == self.row) & (seq == self.seq)

    def holder(self, head, core):
        return self._with_same(2 * self.at[X] + core, 8 * self.core + head)

    def owner(self, stretch):
        return self._with_same(2 * self.at[X] + self.seq // 8, stretch)

    def start(self, copy, key):
        copy.start()
        self.sending.append(copy.wait_send)
        self.coming[key] = copy.wait_recv

    def finish(self, copy, key):
        self.coming.pop(key)
        copy.wait_recv()

    def greet(self, barrier):
        def one(index, carry):
            for device, same in (self.holder(index // 2, lax.rem(index, 2)), self.owner(index)):

                @pl.when(jnp.logical_not(same))
                def _():
                    pl.semaphore_signal(barrier, inc=1, device_id=device, device_id_type=MESH)

            return carry

        lax.fori_loop(0, 16, one, 0)
        others = [self.partner(), self.along(1), self.along(SEQ - 1)]
        others += [self.peer(axis, distance) for axis in (X, Y, Z) for distance in (1, 2, 3)]
        for device in others:
            pl.semaphore_signal(barrier, inc=1, device_id=device, device_id_type=MESH)
        return 32 + len(others) - 2 * self.near.astype(jnp.int32)


COUNTS = [-(-2 * LONG * (pair + 1) // 128) * 128 for pair in range(8)]
FIRSTS = [sum(COUNTS[:pair]) for pair in range(8)]


class Layer:
    def __init__(self, at, ref, own, index, rows):
        self.at = at
        self.r = ref
        self.s = own
        self.index = index
        self.rows = rows
        self.slope = ref.dvalue if index else ref.dkey


    def _buffers(self, kind):
        s = self.s
        return {
            KV: (s.kv_out, s.kv_in), Q: (s.q_out, s.q_in), DM: (s.dm_out, s.dm_in), MIX: (s.mix_out, s.mix_in),
            DKV: (s.dkv_out, s.dkv_in), DQ: (s.dq_out, s.dq_in), TAIL: (self.r.tail_out, self.r.tail_in),
        }[kind]

    def _wide(self, kind):
        return self.index == 1 and kind in (KV, DKV)

    def _copy(self, kind, index):
        at, sems = self.at, self.s.sems
        out, into = self._buffers(kind)
        source, recv = index, sems.at[1, kind]
        if kind in (KV, Q, DM):
            if self._wide(kind):
                source = index // 2
                device, same = at.holder(source, lax.rem(index, 2))
            else:
                device, same = at.holder(index, lax.rem(at.seq, 2))
            target = at.seq if kind == KV else at.seq // 2
            if kind == KV and not self._wide(kind):
                recv = sems.at[2, at.seq // 2]
            into = into.at[target]
        elif self._wide(kind):
            device, same = at.owner(index)
            into = into.at[at.core, at.head]
        else:
            device, same = at.owner(lax.rem(2 * index + at.core + (1 if kind == TAIL else 0), SEQ))
            into = into.at[at.head]
        return out.at[source], into, sems.at[0, kind], recv, device, same

    def send_one(self, kind, index):
        src, dst, send, recv, device, same = self._copy(kind, index)

        @pl.when(same)
        def _():
            pltpu.make_async_copy(src, dst, recv).start()

        @pl.when(jnp.logical_not(same))
        def _():
            remote(src, dst, send, recv, device).start()

    def send_some(self, kind, first):
        def one(step, carry):
            index = lax.rem(step + self.at.head, 4) + first
            self.send_one(kind, index)
            if kind == MIX:
                self.send_one(TAIL, index)
            return carry

        lax.fori_loop(0, 4, one, 0)

    def send_rest(self, kind):
        self.at.sending.append(lambda: self.sent(kind))
        self.at.coming[(self.index, kind)] = lambda: self.receive(kind)

    def send(self, kind):
        count = 16 if self._wide(kind) else 8
        begin = self.at.seq // 2 if kind in (KV, Q, DM) else self.at.head
        begin = begin * (count // 8)

        def one(step, carry):
            self.send_one(kind, lax.rem(step + begin, count))
            return carry

        lax.fori_loop(0, count, one, 0)
        self.send_rest(kind)

    def _wait(self, place, send, recv):
        return remote(place, place, send, recv, self.at.partner())

    def receive(self, kind):
        self.at.coming.pop((self.index, kind), None)
        sems = self.s.sems
        self._wait(self._buffers(kind)[1], sems.at[0, kind], sems.at[1, kind]).wait_recv()

    def sent(self, kind):
        sems = self.s.sems
        count = 16 if self._wide(kind) else 8
        many = self.s.kv_in if kind == KV else self._buffers(kind)[0]
        inside = self.at.near if self._wide(kind) else self.at.next if kind == TAIL else self.at.same
        for number, when in ((count - 1, inside), (count, jnp.logical_not(inside))):

            @pl.when(when)
            def _():
                self._wait(many.at[pl.ds(0, number)], sems.at[0, kind], sems.at[1, kind]).wait_send()

    def _relay(self, index):
        place = self.s.kv_in.at[2 * index + self.at.core]
        sems = self.s.sems
        return remote(place, place, sems.at[0, RELAY], sems.at[1, RELAY], self.at.partner())

    def receive_keys(self):
        if self._wide(KV):
            self.receive(KV)
            return
        self.at.coming.pop((self.index, KV), None)
        s = self.s

        def one(index, carry):
            self._wait(s.kv_in.at[0], s.sems.at[0, KV], s.sems.at[2, index]).wait_recv()
            self._relay(index).start()
            return carry

        lax.fori_loop(0, 8, one, 0)
        relayed = self._wait(s.kv_in.at[pl.ds(0, 8)], s.sems.at[0, RELAY], s.sems.at[1, RELAY])
        relayed.wait_recv()
        self.at.sending.append(relayed.wait_send)


    def angles(self):
        table, first = self.r.offsets, self.r.firsts
        place = self.index * SEQ + self.at.seq
        cos_a, sin_a = first[0, pl.ds(place, 1), :], first[1, pl.ds(place, 1), :]
        cos_b, sin_b = table[0, : self.rows, :], table[1, : self.rows, :]
        return cos_a * cos_b - sin_a * sin_b, sin_a * cos_b + cos_a * sin_b

    def gain(self, which):
        return self.r.gains[self.index, which : which + 1, :].astype(F32)

    def project(self, values, ready=None):
        s, rows = self.s, self.rows
        normal, scale = normalize(values)
        s.normal[0] = normal
        s.scale[0] = jnp.broadcast_to(scale, (rows, 128))
        normed = (normal * self.gain(0)).astype(BF16)
        s.n1[...] = normed
        cosine, sine = self.angles()
        low = lanes((rows, 128)) < 64
        weight = self.r.wqkv.at[self.index]
        for group in range(GROUPS):
            key = dot(normed, weight[:, 512 + 128 * group : 640 + 128 * group])
            value = dot(normed, weight[:, 1024 + 128 * group : 1152 + 128 * group])
            key = key * cosine + half_turn(key) * sine
            value = pltpu.roll(value, 64, 1)
            s.kv_out[2 * group, :rows] = jnp.where(low, key, value).astype(BF16)
            s.kv_out[2 * group + 1, :rows] = jnp.where(low, value, key).astype(BF16)
            query = dot(normed, weight[:, 128 * group : 128 * group + 128])
            query = (query * cosine + half_turn(query) * sine) * 0.125
            s.q_out[2 * group], s.q_out[2 * group + 1] = pack_pair(query)
        if ready is not None:
            ready()
        self.send(KV)
        self.send(Q)

    def native(self, shape):
        return (lanes(shape) // 64) == lax.rem(self.at.seq, 2)

    def pack_one(self, values):
        rows = self.rows // 2
        return seal(jnp.where(self.native((rows, 128)), values[:rows], pltpu.roll(values[rows:], 64, 1)))

    def split_heads(self):
        s, length = self.s, SEQ * self.rows
        both = s.kv_in[:, : self.rows, :].reshape(length, 128).astype(F32)
        own = self.native((length, 128))
        s.key[...] = jnp.where(own, both, 0.0).astype(BF16)
        s.value[...] = jnp.where(own, pltpu.roll(both, 64, 1), 0.0).astype(BF16)

    def attend(self):
        s, core = self.s, self.at.core
        for index in range(8):
            s.query[index] = unpack_one(s.q_in[index], self.rows).astype(BF16)
        if self.index == 0:
            for pair in reversed(range(8)):
                count = COUNTS[pair]
                score = dot_nt(s.query[pair], s.key[:count])
                first = (288 * pair) // 128 * 128
                column = s.column[:, pair : pair + 1]
                allowed = s.line[0:1, :count] == column
                position = sublanes((LONG, count - first)) + (2 * pair + core) * LONG
                causal = lanes((LONG, count - first)) + first <= position
                if first:
                    head = jnp.where(allowed[:, :first], score[:, :first], -1e9)
                    tail = jnp.where(allowed[:, first:] & causal, score[:, first:], -1e9)
                    score = jnp.concatenate([head, tail], 1)
                else:
                    score = jnp.where(allowed & causal, score, -1e9)
                top = jnp.max(score, -1, keepdims=True)
                expo = jnp.exp(score - top)
                share = 1.0 / jnp.sum(expo, -1, keepdims=True)
                expo = expo.astype(BF16)
                s.expo[:, FIRSTS[pair] : FIRSTS[pair] + count] = expo
                s.part[:, pair : pair + 1] = share
                mixed = dot(expo, s.value[:count]) * share
                s.mix_out[pair] = self.pack_one(mixed)
                tail = mixed[LONG - EXTRA :]
                self.r.tail_out[pair] = jnp.where(self.native(tail.shape), tail, 0.0).astype(BF16)
                if pair == 4:
                    self.send_some(MIX, 4)
            self.send_some(MIX, 0)
            self.send_rest(MIX)
            self.send_rest(TAIL)
        else:
            count, length = 8 * SHORT, SEQ * SHORT
            score = dot_nt(s.query[...].reshape(count, 128), s.key[...])
            column = s.column[...].reshape(count, 128)[:, :1]
            row = lax.broadcasted_iota(jnp.int32, (8, SHORT, length), 1)
            block = lax.broadcasted_iota(jnp.int32, (8, SHORT, length), 0)
            position = (row + (2 * block + core) * SHORT).reshape(count, length)
            causal = lanes((count, length)) <= position
            score = jnp.where((s.line[0:1, :] == column) & causal, score, -1e9)
            top = jnp.max(score, -1, keepdims=True)
            expo = jnp.exp(score - top)
            share = 1.0 / jnp.sum(expo, -1, keepdims=True)
            expo = expo.astype(BF16)
            s.expo[...] = expo
            s.part[...] = jnp.broadcast_to(share, (count, 128)).reshape(8, SHORT, 128)
            mixed = (dot(expo, s.value[...]) * share).reshape(8, SHORT, 128)
            for index in range(8):
                s.mix_out[index] = self.pack_one(mixed[index])
            self.send(MIX)

    def feed_forward(self, values):
        i, s, rows = self.index, self.s, self.rows
        parts = [unpack_pair(s.mix_in[2 * g], s.mix_in[2 * g + 1], rows) for g in range(GROUPS)]
        mixed = jnp.concatenate(parts, 1).astype(BF16)
        s.mixed[...] = mixed
        if i == 0:
            tails = [self.r.tail_in[2 * g] + self.r.tail_in[2 * g + 1] for g in range(GROUPS)]
            mixed = jnp.concatenate([mixed, jnp.concatenate(tails, 1)], 0)
        first = values + dot(mixed, self.r.wout[i])
        normal, scale = normalize(first)
        s.normal[1] = normal[:rows]
        s.scale[1] = jnp.broadcast_to(scale[:rows], (rows, 128))
        normed = (normal * self.gain(1)).astype(BF16)
        s.n2[...] = normed[:rows]
        result = first
        for part in range(4):
            at = slice(512 * part, 512 * part + 512)
            hidden = dot(normed, self.r.wup[i, :, at])
            inner = 0.7978845608028654 * (hidden + 0.044715 * hidden * hidden * hidden)
            bend = jnp.tanh(inner)
            active = (0.5 * hidden * (1.0 + bend)).astype(BF16)
            result = result + dot(active, self.r.wdown[i, at, :])
            s.act[part // 2, :, 512 * (part % 2) : 512 * (part % 2) + 512] = active[:rows]
            hidden, bend = hidden[:rows], bend[:rows]
            slope = 0.5 * (1.0 + bend) + 0.5 * hidden * (1.0 - bend * bend) * (
                0.7978845608028654 * (1.0 + 3.0 * 0.044715 * hidden * hidden)
            )
            for column in range(4):
                place = rows * (4 * part + column)
                self.slope[place : place + rows, :] = slope[:, 128 * column : 128 * column + 128]
        return result


    def feed_back(self, grad):
        i, s = self.index, self.s
        low = grad.astype(BF16)
        s.glow[...] = low
        self.swap((0,))
        back = jnp.zeros((self.rows, D), F32)
        for part in range(4):
            at = slice(512 * part, 512 * part + 512)
            active = dot_nt(low, self.r.wdown[i, at, :])
            places = [self.rows * (4 * part + column) for column in range(4)]
            slope = jnp.concatenate([self.slope[place : place + self.rows, :] for place in places], 1)
            hidden = (slope * active).astype(BF16)
            s.dhid[part // 2, :, 512 * (part % 2) : 512 * (part % 2) + 512] = hidden
            back = back + dot_nt(hidden, self.r.wup[i, :, at])
        self.swap((3,))
        normal, scale = s.normal[1], s.scale[1][:, :1]
        self.r.gsum[2 * i + 1 : 2 * i + 2, :] = jnp.sum(back * normal, 0, keepdims=True)
        first = grad + normalize_back(back, normal, scale, self.gain(1))
        s.dfirst[...] = first
        first_low = first.astype(BF16)
        s.dv1[0] = first_low[:, :256]
        s.dv1[1] = first_low[:, 256:]
        self.swap((5,))
        for group in range(GROUPS):
            weight = self.r.wout[i, 128 * group : 128 * group + 128, :]
            s.dm_out[2 * group], s.dm_out[2 * group + 1] = pack_pair(dot_nt(first_low, weight))
        self.send(DM)

    def attend_back(self, between):
        s, length = self.s, SEQ * self.rows
        own = self.native((length, 128))
        if self.index == 0:
            for pair in reversed(range(8)):
                count = COUNTS[pair]
                share = s.part[:, pair : pair + 1]
                grad = (unpack_one(s.dm_in[pair], self.rows) * share).astype(BF16)
                expo = s.expo[:, FIRSTS[pair] : FIRSTS[pair] + count]
                weighted = expo * dot_nt(grad, s.value[:count])
                inner = jnp.sum(weighted, -1, keepdims=True) * share
                draw = (weighted - expo * inner).astype(BF16)
                s.dq_out[pair] = self.pack_one(dot(draw, s.key[:count]) * 0.125)
                for total, left, right in ((self.r.dkey, draw, s.query[pair]), (self.r.dvalue, expo, grad)):
                    if pair == 7:
                        total[...] = dot_tn(left, right)
                    else:
                        total[:count] += dot_tn(left, right)
                if pair == 4:
                    self.part_done(1)
                    self.send_some(DQ, 4)
                if pair == 1:
                    self.merge(1)
                between(10 + pair)
            self.part_done(0)
            self.send_some(DQ, 0)
            self.send_rest(DQ)
            return
        else:
            count = 8 * SHORT
            share = s.part[...].reshape(count, 128)
            grad = jnp.concatenate([unpack_one(s.dm_in[index], self.rows) for index in range(8)], 0)
            grad = (grad * share).astype(BF16)
            expo = s.expo[...]
            weighted = expo * dot_nt(grad, s.value[...])
            inner = jnp.sum(weighted, -1, keepdims=True) * share[:, :1]
            draw = (weighted - expo * inner).astype(BF16)
            dq = (dot(draw, s.key[...]) * 0.125).reshape(8, SHORT, 128)
            for index in range(8):
                s.dq_out[index] = self.pack_one(dq[index])
            dkey = dot_tn(draw, s.query[...].reshape(count, 128))
            dvalue = dot_tn(expo, grad)
        self.send(DQ)
        both = jnp.where(own, dkey, pltpu.roll(dvalue, 64, 1)).astype(BF16)
        s.dkv_out[...] = both.reshape(SEQ, self.rows, 128)

    def part_done(self, half):
        s, rows = self.s, SEQ * self.rows // 2
        place = slice(rows * half, rows * half + rows)
        value = pltpu.roll(self.r.dvalue[place], 64, 1)
        both = jnp.where(self.native((rows, 128)), self.r.dkey[place], value).astype(BF16)
        both = both.reshape(4, 2, self.rows, 128)
        for which in range(2):
            s.dkv_part[which, 4 * half : 4 * half + 4] = both[:, which]
        self.at.start(self._merge(half), (self.index, 14, half))

    def _merge(self, half):
        s, four = self.s, pl.ds(4 * half, 4)
        send, recv = s.sems.at[0, MERGE + half], s.sems.at[1, MERGE + half]
        return remote(s.dkv_part.at[1 - self.at.core, four], s.dkv_other.at[four], send, recv, self.at.partner())

    def merge(self, half):
        s, four = self.s, slice(4 * half, 4 * half + 4)
        self.at.finish(self._merge(half), (self.index, 14, half))
        s.dkv_out[four] = (s.dkv_part[self.at.core, four].astype(F32) + s.dkv_other[four].astype(F32)).astype(BF16)
        self.send_some(DKV, 4 * half)

    def project_back(self):
        i, s, rows = self.index, self.s, self.rows
        cosine, sine = self.angles()
        low = lanes((rows, 128)) < 64
        back = jnp.zeros((rows, D), F32)
        for group in range(GROUPS):
            if i:
                even, odd = (
                    s.dkv_in[0, head].astype(F32) + s.dkv_in[1, head].astype(F32)
                    for head in (2 * group, 2 * group + 1)
                )
            else:
                even, odd = s.dkv_in[2 * group].astype(F32), s.dkv_in[2 * group + 1].astype(F32)
            key = jnp.where(low, even, odd)
            key = key * cosine - half_turn(key) * sine
            value = pltpu.roll(jnp.where(low, odd, even), 64, 1)
            query = unpack_pair(s.dq_in[2 * group], s.dq_in[2 * group + 1], rows)
            query = query * cosine - half_turn(query) * sine
            for which, piece in enumerate((query, key, value)):
                place = 4 * which + group
                column = 128 * (place % 6)
                s.dproj[place // 6, :, column : column + 128] = piece.astype(BF16)
        for part in range(2):
            back = back + dot_nt(s.dproj[part], self.r.wqkv[i, :, 768 * part : 768 * part + 768])
        normal, scale = s.normal[0], s.scale[0][:, :1]
        self.r.gsum[2 * i : 2 * i + 1, :] = jnp.sum(back * normal, 0, keepdims=True)
        return s.dfirst[...] + normalize_back(back, normal, scale, self.gain(0))


    def _swap(self, which):
        s, other = self.s, 1 - self.at.core
        src, dst = (
            (s.glow, s.glow_in), (s.n2, s.n2_in), (s.act.at[other], s.act_in), (s.dhid.at[other], s.dhid_in),
            (s.mixed, s.mixed_in), (s.dv1.at[other], s.dv1_in), (s.n1, s.n1_in), (s.dproj.at[other], s.dproj_in),
        )[which]
        return remote(src, dst, s.sems.at[3, which], s.sems.at[4, which], self.at.partner())

    def swap(self, steps):
        copies = [self._swap(which) for which in steps]
        for copy in copies:
            copy.start()
        self.at.sending += [copy.wait_send for copy in copies]
        self.at.coming[(self.index, 10, steps)] = lambda: [copy.wait_recv() for copy in copies]

    def swapped(self, steps):
        self.at.coming.pop((self.index, 10, steps))()

    def grads_feed(self, total):
        s, core = self.s, self.at.core
        for part in range(4):
            at = slice(256 * part, 256 * part + 256)
            total.put_rows(
                part, dot_tn(s.act[core, :, at], s.glow[...]) + dot_tn(s.act_in[:, at], s.glow_in[...])
            )
        for part in range(2):
            at = slice(512 * part, 512 * part + 512)
            up = dot_tn(s.n2[...], s.dhid[core, :, at]) + dot_tn(s.n2_in[...], s.dhid_in[:, at])
            total.put_columns(4 + 2 * part, up[:, :256])
            total.put_columns(5 + 2 * part, up[:, 256:])
        total.put_columns(8, dot_tn(s.mixed[...], s.dv1[core]) + dot_tn(s.mixed_in[...], s.dv1_in[...]))

    def grads_attention(self, total, first):
        s, core = self.s, self.at.core
        grad = dot_tn(s.n1[...], s.dproj[core]) + dot_tn(s.n1_in[...], s.dproj_in[...])
        for part in range(3):
            total.put_columns(first + part, grad[:, 256 * part : 256 * part + 256])


class Total:
    def __init__(self, at, own, kind, result):
        self.at, self.s, self.kind, self.result = at, own, kind, result
        self.first, self.units = own.first, own.grads.shape[1]
        self.ring = self.units > 1
        self.spread = (self.units, self.units + 1, 0, self.units)[kind - 20]

    def put_rows(self, unit, values):
        values = values.astype(BF16)
        for group in range(4):
            self.s.grads[unit // self.units, unit % self.units, group] = values[
                :, 128 * group : 128 * group + 128
            ].reshape(4, 4, 16, 128)

    def put_columns(self, unit, values):
        values = values.astype(BF16)
        for group in range(2):
            self.s.grads[unit // self.units, unit % self.units, 2 * group : 2 * group + 2] = values[
                :, 128 * group : 128 * group + 128
            ].reshape(2, 4, 4, 16, 128)

    def _full(self, *places):
        if not places:
            places = (slice(None),)
        return self.result.at[(self.at.core, places[0], pl.ds(self.first, self.spread), *places[1:])]

    def _place(self, part, stage, distance=0):
        return lax.rem(self.at.at[ORDERS[part][stage]] + distance, 4)

    def _mine(self, part, count):
        return [self._place(part, before) for before in range(count)]

    def _remote(self, src, dst, part, stage, row, distance):
        sems = self.s.sems
        return remote(src, dst, sems.at[row, 0], sems.at[row, 1], self.at.peer(ORDERS[part][stage], distance))

    def _scatter(self, part, stage, distance):
        s = self.s
        src = s.grads.at[(part, slice(None), *self._mine(part, stage), self._place(part, stage, distance))]
        dst = (s.part0, s.part1, s.part2)[stage].at[part, distance - 1]
        return self._remote(src, dst, part, stage, stage, distance)

    def _gather(self, part, stage, distance):
        place = self._full(part, *[self._place(part, before) for before in range(stage + 1)])
        return self._remote(place, place, part, stage, 3 + stage, distance)

    def _whole(self, row):
        s, sems, every = self.s, self.s.sems, slice(None)
        if row in (0, 1, 2, HOP):
            place = s.hop if row == HOP else (s.part0, s.part1, s.part2)[row]
        else:
            three = pl.ds(0, 3)
            places = {
                3: (pl.ds(0, 2) if self.ring else three,), 4: (0, three), 5: (0, 0, three), 6: (), BACK: (0,),
            }[row]
            place = self._full(every, *places)
        return remote(place, place, sems.at[row, 0], sems.at[row, 1], self.at.partner())

    def _begin(self, copies, row):
        for copy in copies:
            copy.start()
        self.at.coming[(self.kind, row)] = lambda: self._whole(row).wait_recv()
        self.at.sending.append(lambda: self._whole(row).wait_send())

    def _arrive(self, row):
        self.at.coming.pop((self.kind, row))()

    def _direct(self, make, stage, row):
        self._begin([make(part, stage, distance) for part in range(3) for distance in (1, 3, 2)], row)

    def scatter(self):
        s = self.s
        if not self.ring:
            self._direct(self._scatter, 0, 0)
            return
        copies = []
        for part in range(3):
            opposite = s.grads.at[part, :, self._place(part, 0, 2)]
            copies += [
                self._remote(opposite.at[:, pl.ds(2 * way, 2)], s.hop.at[part, way], part, 0, HOP, distance)
                for way, distance in enumerate((1, 3))
            ]
        self._begin(copies, HOP)

    def turn(self):
        s = self.s
        self._arrive(HOP)
        copies = []
        for part in range(3):
            for way, distance in enumerate((1, 3)):
                place = self._place(part, 0, distance)
                half = pl.ds(2 * way, 2)
                total = s.grads[part, :, place, half].astype(F32) + s.hop[part, way].astype(F32)
                s.grads[part, :, place, half] = total.astype(BF16)
                copies.append(self._remote(s.grads.at[part, :, place], s.part0.at[part, way], part, 0, 0, distance))
        self._begin(copies, 0)

    def scattered(self, stage):
        s = self.s
        self._arrive(stage)
        got = (s.part0, s.part1, s.part2)[stage]
        for part in range(3):
            mine = self._mine(part, stage + 1)
            total = s.grads[(part, slice(None), *mine)].astype(F32)
            for index in range(got.shape[1]):
                total = total + got[part, index].astype(F32)
            total = total.astype(BF16)
            if stage < 2:
                s.grads[(part, slice(None), *mine)] = total
            else:
                self.result[(self.at.core, part, pl.ds(self.first, self.units), *mine)] = total
        if stage < 2:
            self._direct(self._scatter, stage + 1, stage + 1)
        elif self.spread:
            self._direct(self._gather, 2, 5)

    def gathered(self, stage, hold=False):
        self._arrive(3 + stage)
        if stage == 2:
            self._direct(self._gather, 1, 4)
        elif not hold:
            self.gather_last()

    def gather_last(self):
        if self.ring:
            self.gather_some(0, self.spread)
        else:
            self._direct(self._gather, 0, 3)
            self._pass((0,))

    def gather_some(self, begin, end):
        copies = []
        for part in range(3):
            units = pl.ds(self.first + begin, end - begin)
            place = self.result.at[self.at.core, part, units, self._place(part, 0)]
            copies += [self._remote(place, place, part, 0, 3, distance) for distance in (1, 3)]
        if end == self.spread:
            self._begin(copies, 3)
            self._pass((0,))
        else:
            for copy in copies:
                copy.start()

    def gather_turn(self):
        self._arrive(3)
        copies = []
        for part in range(3):
            for way, distance in enumerate((1, 3)):
                place = self._full(part, self._place(part, 0, 4 - distance), pl.ds(2 * way, 2))
                copies.append(self._remote(place, place, part, 0, BACK, distance))
        self._begin(copies, BACK)
        self._pass((1, 3))

    def gather_done(self):
        self._arrive(BACK if self.ring else 3)
        self._pass((2,) if self.ring else (1, 2, 3))

    def _pass(self, distances):
        sems = self.s.sems
        for part in range(3):
            for distance in distances:
                place = self._full(part, self._place(part, 0, distance))
                remote(place, place, sems.at[6, 0], sems.at[6, 1], self.at.partner()).start()
        if 2 in distances:
            self.at.coming[(self.kind, 6)] = lambda: self._whole(6).wait_recv()
            self.at.sending.append(lambda: self._whole(6).wait_send())


def vmem(**shapes):
    return {name: pltpu.VMEM(shape, kind) for name, (shape, kind) in shapes.items()}


def layer_scratch(index, rows):
    length, half = SEQ * rows, padded(rows)
    message = rows + (NOTE if index == 0 else 0)
    shapes = vmem(
        kv_out=((8, message, 128), BF16), kv_in=((SEQ, message, 128), BF16),
        q_out=((8, half, 128), BF16), q_in=((8, half, 128), BF16),
        dm_out=((8, half, 128), BF16), dm_in=((8, half, 128), BF16),
        mix_out=((8, half, 128), BF16), mix_in=((8, half, 128), BF16),
        dq_out=((8, half, 128), BF16), dq_in=((8, half, 128), BF16),
        dkv_out=((16 if index else 8, rows, 128), BF16), dkv_in=((2, 8, rows, 128) if index else (8, rows, 128), BF16),
        query=((8, rows, 128), BF16), key=((length, 128), BF16), value=((length, 128), BF16),
        expo=((rows, sum(COUNTS)) if index == 0 else (8 * rows, length), BF16), part=((8, rows, 128) if index else (rows, 128), F32),
        normal=((2, rows, D), F32), scale=((2, rows, 128), F32),
        dfirst=((rows, D), F32),
        n1=((rows, D), BF16), n2=((rows, D), BF16), mixed=((rows, D), BF16), glow=((rows, D), BF16),
        act=((2, rows, FF // 2), BF16), dhid=((2, rows, FF // 2), BF16),
        dv1=((2, rows, 256), BF16), dproj=((2, rows, 768), BF16),
        n1_in=((rows, D), BF16), n2_in=((rows, D), BF16), mixed_in=((rows, D), BF16), glow_in=((rows, D), BF16),
        act_in=((rows, FF // 2), BF16), dhid_in=((rows, FF // 2), BF16),
        dv1_in=((rows, 256), BF16), dproj_in=((rows, 768), BF16),
        column=((8, rows, 128) if index else (rows, 128), F32), line=((8, length), F32),
    )
    if not index:
        shapes.update(vmem(dkv_part=((2, 8, rows, 128), BF16), dkv_other=((8, rows, 128), BF16)))
    shapes.update(sems=pltpu.SemaphoreType.DMA((5, 10)))
    return shapes


def total_scratch(units):
    ways = 2 if units > 1 else 3
    shapes = vmem(
        grads=((3, units, 4, 4, 4, 16, 128), BF16), part0=((3, ways, units, 4, 4, 16, 128), BF16),
        part1=((3, 3, units, 4, 16, 128), BF16), part2=((3, 3, units, 16, 128), BF16),
    )
    if units > 1:
        shapes.update(vmem(hop=((3, 2, units, 2, 4, 16, 128), BF16)))
    shapes.update(sems=pltpu.SemaphoreType.DMA((9, 2)))
    return shapes


def common_scratch():
    shapes = vmem(
        tokens=((LONG, D), BF16), cot=((LONG, D), BF16), seg=((1, LONG), jnp.int32), gains=((2, 2, D), BF16),
        offsets=((2, LONG, 128), F32), firsts=((2, 2 * SEQ, 128), F32),
        wqkv=((2, D, 3 * D), BF16), wout=((2, D, D), BF16),
        wup=((2, D, FF), BF16), wdown=((2, FF, D), BF16),
        dkey=((SEQ * LONG, 128), F32), dvalue=((SEQ * LONG, 128), F32),
        second=((4, LONG + 8, 128), F32), share=((4, SHORT + 8, 128), F32),
        work=((4, LONG, 128), F32),
        ahead=((4, 8, 128), F32), before=((EXTRA, D), BF16),
        tail_out=((8, EXTRA, 128), BF16), tail_in=((8, EXTRA, 128), BF16),
        output=((LONG, D), BF16), result=((LONG, D), F32),
        gsum=((8, D), F32), gain_in=((4, 4, 8, D), F32), gain_out=((3, 8, D), F32),
    )
    shapes.update(more=pltpu.SemaphoreType.DMA((29,)))
    return shapes


SPACES = (
    common_scratch(), layer_scratch(0, LONG), layer_scratch(1, SHORT),
    *(total_scratch(units) for units in UNITS),
)


def body(*refs):
    spaces, place = [], 14
    for part in SPACES:
        spaces.append(types.SimpleNamespace(**dict(zip(part, refs[place : place + len(part)]))))
        place += len(part)
    at = Place()
    steps(at, spaces, *refs[:14])
    for wait in at.coming.values():
        wait()
    for wait in at.sending:
        wait()


def steps(
    at, spaces, tokens, seg, wqkv, wout, wup, wdown, gains, cot, offsets, firsts,
    output, tokens_grad, sums, gain_sum,
):
    ref = spaces[0]
    more = ref.more
    full, short = Layer(at, ref, spaces[1], 0, LONG), Layer(at, ref, spaces[2], 1, SHORT)
    for kind in range(4):
        spaces[3 + kind].first = sum(UNITS[:kind])
    early, middle, minor, late = (Total(at, spaces[3 + kind], 20 + kind, sums) for kind in range(4))

    pairs = [
        (tokens, ref.tokens), (gains, ref.gains), (wqkv.at[0], ref.wqkv.at[0]),
        (offsets, ref.offsets), (firsts, ref.firsts), (seg, ref.seg),
        (wout.at[0], ref.wout.at[0]), (wup.at[0], ref.wup.at[0]), (wdown.at[0], ref.wdown.at[0]),
        (wqkv.at[1], ref.wqkv.at[1]), (cot, ref.cot),
        (wout.at[1], ref.wout.at[1]), (wup.at[1], ref.wup.at[1]), (wdown.at[1], ref.wdown.at[1]),
    ]
    loads = [pltpu.make_async_copy(src, dst, more.at[step]) for step, (src, dst) in enumerate(pairs)]
    for load in loads:
        load.start()
    waiting = list(range(len(loads)))

    def loaded(count):
        while waiting and waiting[0] < count:
            loads[waiting.pop(0)].wait()

    at.sending.append(lambda: loaded(len(loads)))
    barrier = pltpu.get_barrier_semaphore()
    greeted = at.greet(barrier)

    loaded(6)
    inputs = ref.tokens[...].astype(F32)
    def ready():
        line = ref.seg[...].astype(F32)
        high = jnp.floor(line * (1.0 / 64.0))
        rows = jnp.concatenate([high, line - 64.0 * high, jnp.zeros((6, LONG), F32)], 0)
        third = jnp.where(sublanes((LONG, 128)) == 3 * lanes((LONG, 128)), 1.0, 0.0)
        picked = dot(rows, third)
        wide = jnp.concatenate([rows[:, 128:], jnp.zeros((8, 112), F32)], 1)
        note = jnp.concatenate([rows[0:2, :128], wide[0:2], picked[0:2], jnp.zeros((10, 128), F32)], 0)
        for head in range(8):
            full.s.kv_out[head, LONG:] = note.astype(BF16)
        pl.semaphore_wait(barrier, greeted)
        at.start(
            remote(ref.tokens.at[pl.ds(LONG - EXTRA, EXTRA)], ref.before, more.at[17], more.at[18], at.along(1)), (3, 0)
        )

    full.project(inputs, ready)

    def segments():
        notes = [full.s.kv_in[block, LONG:, :].astype(F32) for block in range(SEQ)]
        for block, code in enumerate(notes):
            long = jnp.concatenate([64.0 * code[0:1] + code[1:2], 64.0 * code[2:3, :16] + code[3:4, :16]], 1)
            full.s.line[0:1, LONG * block : LONG * block + LONG] = long
            short.s.line[0:1, SHORT * block : SHORT * block + SHORT] = (64.0 * code[4:5] + code[5:6])[:, :SHORT]
        for layer in (full, short):
            rows = layer.rows
            equal = lanes((rows, rows)) == sublanes((rows, rows))
            for pair in range(8):
                code = full.s.kv_in[2 * pair + at.core, LONG:, :].astype(F32)
                if layer is full:
                    line = jnp.concatenate([64.0 * code[0:1] + code[1:2], 64.0 * code[2:3, :16] + code[3:4, :16]], 1)
                else:
                    line = (64.0 * code[4:5] + code[5:6])[:, :SHORT]
                column = jnp.sum(jnp.where(equal, line, 0.0), 1, keepdims=True)
                if layer is full:
                    layer.s.column[:, pair : pair + 1] = column
                else:
                    layer.s.column[pair] = jnp.broadcast_to(column, (rows, 128))

    def attention(layer):
        layer.receive_keys()
        layer.receive(Q)
        if layer is full:
            segments()
        layer.split_heads()
        layer.attend()
        layer.receive(MIX)
        if layer is full:
            layer.receive(TAIL)

    attention(full)
    loaded(9)
    second = ref.second
    at.coming.pop((3, 0))()
    wide = full.feed_forward(jnp.concatenate([inputs, ref.before[...].astype(F32)], 0))
    spill(second, 8, wide[:LONG])
    spill(second, 0, jnp.where(at.seq == 0, 0.0, wide[LONG + EXTRA - 8 :]))
    full.swap(AHEAD)
    loaded(11)
    pooled = jnp.concatenate(
        [
            (every_third(second, 6, g) + every_third(second, 7, g) + every_third(second, 8, g)) / 3.0
            for g in range(GROUPS)
        ],
        1,
    )
    short.project(pooled)
    loaded(14)
    work = ref.work
    spill(work, 0, ref.cot[...].astype(F32))
    grad_short = jnp.concatenate(
        [every_third(work, 0, g) + every_third(work, 1, g) + every_third(work, 2, g) for g in range(GROUPS)], 1
    )
    attention(short)
    result = short.feed_forward(pooled)
    short.swap(AHEAD)

    def backward(layer, total, grad, between):
        layer.feed_back(grad)
        between(0)
        layer.swapped(AHEAD)
        for which in BEHIND:
            layer.swapped((which,))
        layer.grads_feed(total)
        between(1)
        layer.receive(DM)
        layer.attend_back(between)
        if layer is full:
            layer.merge(0)
            layer.send_rest(DKV)
        else:
            layer.send(DKV)
        between(4)
        layer.receive(DQ)
        layer.receive(DKV)
        between(6)
        back = layer.project_back()
        layer.swap((7,))
        return back

    def finish_output():
        for group in range(GROUPS):
            at_lanes = slice(128 * group, 128 * group + 128)
            for step in range(3):
                second[group, pl.ds(8 + step, SHORT, 3), :] = every_third(second, 8 + step, group) + result[:, at_lanes]
            ref.output[:, at_lanes] = second[group, 8:, :].astype(BF16)
        store = pltpu.make_async_copy(ref.output, output, more.at[14])
        store.start()
        at.sending.append(store.wait)

    def between_short(point):
        if point == 0:
            finish_output()
        elif point == 1:
            early.scatter()
        elif point == 4:
            early.turn()

    share = ref.share
    spill(share, 0, backward(short, early, grad_short, between_short) * (1.0 / 3.0))

    def halo_back():
        return remote(share.at[:, pl.ds(0, 8), :], ref.ahead, more.at[19], more.at[20], at.along(SEQ - 1))

    at.start(halo_back(), (3, 1))
    short.swapped((7,))
    short.grads_attention(minor, 0)
    minor.scatter()
    at.finish(halo_back(), (3, 1))
    early.scattered(0)
    share[:, SHORT:, :] = jnp.where(at.seq == SEQ - 1, 0.0, ref.ahead[...])
    for group in range(GROUPS):
        own, following = share[group, 0:SHORT, :], share[group, 1 : SHORT + 1, :]
        for step, piece in enumerate((own, following, following)):
            work[group, pl.ds(step, SHORT, 3), :] = every_third(work, step, group) + piece
    grad_full = jnp.concatenate([work[group] for group in range(GROUPS)], 1)

    def between_full(point):
        if point == 1:
            middle.scatter()
            early.scattered(1)
        elif point == 17:
            minor.scattered(0)
        elif point == 16:
            early.scattered(2)
        elif point == 15:
            middle.turn()
        elif point == 13:
            early.gathered(2)
        elif point == 11:
            minor.scattered(1)
        elif point == 4:
            middle.scattered(0)
            early.gathered(1)
            minor.scattered(2)
        elif point == 6:
            middle.scattered(1)

    ref.result[...] = backward(full, middle, grad_full, between_full)
    store = pltpu.make_async_copy(ref.result, tokens_grad, more.at[15])
    store.start()
    at.sending.append(store.wait)
    full.swapped((7,))
    full.grads_attention(late, 0)
    late.scatter()

    gsum, gain_in, gain_out = ref.gsum, ref.gain_in, ref.gain_out

    def gain_copy(axis, distance):
        src = gsum if axis == 0 else gain_out.at[axis - 1]
        return remote(src, gain_in.at[axis, at.at[axis]], more.at[23 + axis], more.at[26 + axis], at.peer(axis, distance))

    def gain_step(axis):
        for distance in (1, 2, 3):
            gain_copy(axis, distance).start()
        gain_in[axis, at.at[axis]] = gsum[...] if axis == 0 else gain_out[axis - 1]
        three = gain_in.at[axis, pl.ds(0, 3)]
        copies = remote(three, three, more.at[23 + axis], more.at[26 + axis], at.partner())
        at.coming[(4, axis)] = copies.wait_recv
        at.sending.append(copies.wait_send)

    def gain_done(axis):
        at.coming.pop((4, axis))()
        return (gain_in[axis, 0] + gain_in[axis, 1]) + (gain_in[axis, 2] + gain_in[axis, 3])

    gsum[4:, :] = jnp.zeros((4, D), F32)
    gain_step(0)
    middle.scattered(2)
    early.gather_turn()
    late.scattered(0)
    gain_out[0] = gain_done(0)
    gain_step(1)
    middle.gathered(2)
    late.scattered(1)
    gain_out[1] = gain_done(1)
    gain_step(2)
    late.scattered(2)
    middle.gathered(1, True)
    middle.gather_some(0, 2)
    early.gather_done()
    late.gathered(2)
    middle.gather_some(2, 4)
    late.gathered(1)
    middle.gather_turn()
    gain_in[3, 0] = gain_done(2)
    gain_swap = remote(gain_in.at[3, 0], gain_in.at[3, 1], more.at[21], more.at[22], at.partner())
    at.start(gain_swap, (4, 3, 0))
    late.gather_done()
    middle.gather_done()
    at.finish(gain_swap, (4, 3, 0))
    gain_out[2] = gain_in[3, 0] + gain_in[3, 1]
    store = pltpu.make_async_copy(gain_out.at[2], gain_sum, more.at[16])
    store.start()
    at.sending.append(store.wait)


def tables():
    freq = 10000.0 ** (-np.arange(32) / 32.0)
    freq = np.tile(freq, 4)[None, :]
    offset = np.arange(LONG)[:, None] * freq
    first = np.concatenate([np.arange(SEQ) * LONG, np.arange(SEQ) * SHORT])[:, None] * freq
    return (
        np.stack([np.cos(offset), np.sin(offset)]).astype(np.float32),
        np.stack([np.cos(first), np.sin(first)]).astype(np.float32),
    )


def widen_body(
    sums, gain, output, grad, qkv, out, up, down, gains, output_too, grad_too,
    gain_in, gain_out, output_in, grad_in, down_out, up_out, out_out, qkv_out, sems,
):
    small = [
        pltpu.make_async_copy(gain, gain_in, sems.at[0, 0]),
        pltpu.make_async_copy(output, output_in, sems.at[0, 1]),
        pltpu.make_async_copy(grad, grad_in, sems.at[0, 2]),
    ]
    stores = []
    for copy in small:
        copy.start()

    def put(dst, src, slot):
        copy = pltpu.make_async_copy(src, dst, sems.at[1 + slot // 8, slot % 8])
        copy.start()
        stores.append(copy)

    def tiles(kind, half, unit):
        return sums.at[half, unit // UNITS[kind], sum(UNITS[:kind]) + unit % UNITS[kind]]

    def rows_of(kind, half, unit, dst, first_row):
        ref = tiles(kind, half, unit)
        for group in range(4):
            values = ref[group].reshape(256, 128).astype(F32)
            dst[first_row : first_row + 256, 128 * group : 128 * group + 128] = values

    def columns_of(kind, half, unit, dst, column):
        ref = tiles(kind, half, unit)
        for group in range(2):
            values = ref[2 * group : 2 * group + 2].reshape(512, 128).astype(F32)
            dst[:, column + 128 * group : column + 128 * group + 128] = values

    def feed(kind, half, block):
        at = 2 * block + half
        for unit in range(4):
            rows_of(kind, half, unit, down_out.at[at], 256 * unit)
        put(down.at[block, pl.ds(1024 * half, 1024), :], down_out.at[at], at)

    def rest(kind, block, kind_heads, unit):
        for half in range(2):
            for part in range(4):
                columns_of(kind, half, 4 + part, up_out.at[block], 1024 * half + 256 * part)
        put(up.at[block], up_out.at[block], 4 + block)
        for half in range(2):
            columns_of(kind, half, 8, out_out.at[block], 256 * half)
        put(out.at[block], out_out.at[block], 6 + block)
        for half in range(2):
            for part in range(3):
                columns_of(kind_heads, half, unit + part, qkv_out.at[block], 768 * half + 256 * part)
        put(qkv.at[block], qkv_out.at[block], 8 + block)

    def through():
        for copy in small:
            copy.wait()
        gain_out[...] = gain_in[0:4, :].reshape(2, 2, D)
        put(gains, gain_out, 10)
        put(output_too.at[0], output_in, 11)
        put(grad_too.at[0], grad_in, 12)

    for kind, block, kind_heads, unit in ((0, 1, 2, 0), (1, 0, 3, 0)):
        for half in range(2):
            feed(kind, half, block)
        rest(kind, block, kind_heads, unit)
        if kind == 0:
            through()
    for copy in stores:
        copy.wait()


def widen(sums, gain, output, grad):
    anywhere, inside = pl.BlockSpec(memory_space=pl.ANY), pl.BlockSpec(memory_space=pltpu.VMEM)
    return pl.pallas_call(
        widen_body,
        out_shape=(
            jax.ShapeDtypeStruct((2, D, 3 * D), F32),
            jax.ShapeDtypeStruct((2, D, D), F32),
            jax.ShapeDtypeStruct((2, D, FF), F32),
            jax.ShapeDtypeStruct((2, FF, D), F32),
            jax.ShapeDtypeStruct((2, 2, D), F32),
            jax.ShapeDtypeStruct((1, LONG, D), BF16),
            jax.ShapeDtypeStruct((1, LONG, D), F32),
        ),
        in_specs=[inside] + [anywhere] * 3,
        out_specs=(anywhere,) * 7,
        scratch_shapes=[
            pltpu.VMEM((8, D), F32),
            pltpu.VMEM((2, 2, D), F32),
            pltpu.VMEM((LONG, D), BF16),
            pltpu.VMEM((LONG, D), F32),
            pltpu.VMEM((4, 1024, 512), F32),
            pltpu.VMEM((2, 512, 2048), F32),
            pltpu.VMEM((2, 512, 512), F32),
            pltpu.VMEM((2, 512, 1536), F32),
            pltpu.SemaphoreType.DMA((3, 8)),
        ],
        compiler_params=pltpu.CompilerParams(vmem_limit_bytes=40 * 2**20),
        name="widen",
    )(
        pltpu.with_memory_space_constraint(sums, pltpu.VMEM),
        *(pltpu.with_memory_space_constraint(array, pltpu.HBM) for array in (gain, output, grad)),
    )


def per_device(tokens, segment, w_qkv, w_out, w_up, w_down, gains, cotangent):
    offsets, firsts = tables()
    anywhere, inside = pl.BlockSpec(memory_space=pl.ANY), pl.BlockSpec(memory_space=pltpu.VMEM)
    output, tokens_grad, sums, gain = pl.pallas_call(
        body,
        out_shape=(
            jax.ShapeDtypeStruct((LONG, D), BF16),
            jax.ShapeDtypeStruct((LONG, D), F32),
            pltpu.VMEM((2, 3, sum(UNITS), 4, 4, 4, 16, 128), BF16),
            jax.ShapeDtypeStruct((8, D), F32),
        ),
        in_specs=[anywhere] * 10,
        out_specs=(anywhere, anywhere, inside, anywhere),
        scratch_shapes=[shape for part in SPACES for shape in part.values()],
        compiler_params=pltpu.CompilerParams(
            collective_id=0, has_side_effects=True, vmem_limit_bytes=51 * 2**20
        ),
        name="layers",
    )(
        tokens[0], segment, w_qkv, w_out, w_up, w_down, gains, cotangent[0],
        jnp.asarray(offsets), jnp.asarray(firsts),
    )
    qkv, out, up, down, gain, output, tokens_grad = widen(sums, gain, output, tokens_grad)
    return output, tokens_grad, qkv, out, up, down, gain


def solution(mesh):
    return jax.shard_map(
        per_device,
        mesh=mesh,
        in_specs=(
            P("row", "seq", None),
            P("row", "seq"),
            P(),
            P(),
            P(),
            P(),
            P(),
            P("row", "seq", None),
        ),
        out_specs=(P("row", "seq", None), P("row", "seq", None), P(), P(), P(), P(), P()),
        check_vma=False,
    )
```

```python
import types

import jax
import jax.numpy as jnp
import numpy as np
from jax import lax
from jax.experimental import pallas as pl
from jax.experimental.pallas import tpu as pltpu
from jax.sharding import PartitionSpec as P

MESH = pl.DeviceIdType.MESH
F32 = jnp.float32
BF16 = jnp.bfloat16

SEQ = 16
LONG = 144
SHORT = 48
D = 512
FF = 2048
GROUPS = 4
NOTE = 16
KV, Q, DM, MIX, DKV, DQ, RELAY, TAIL, MERGE = range(9)
AHEAD, BEHIND = (1, 2, 4, 6), (0, 3, 5)
EXTRA = 16
UNITS = (3, 3, 1, 1)
HOP, BACK = 7, 8
X, Y, Z = range(3)
ORDERS = ((X, Y, Z), (Y, Z, X), (Z, X, Y))


def dot(left, right):
    return jnp.dot(left, right, preferred_element_type=F32)


def dot_nt(left, right):
    return lax.dot_general(left, right, (((1,), (1,)), ((), ())), preferred_element_type=F32)


def dot_tn(left, right):
    return lax.dot_general(left, right, (((0,), (0,)), ((), ())), preferred_element_type=F32)


def lanes(shape):
    return lax.broadcasted_iota(jnp.int32, shape, len(shape) - 1)


def sublanes(shape):
    return lax.broadcasted_iota(jnp.int32, shape, len(shape) - 2)


def normalize(values):
    center = values - jnp.mean(values, -1, keepdims=True)
    scale = lax.rsqrt(jnp.mean(center * center, -1, keepdims=True) + 1e-05)
    return center * scale, scale


def normalize_back(grad, normal, scale, gain):
    inner = grad * gain
    return scale * (
        inner
        - jnp.mean(inner, -1, keepdims=True)
        - normal * jnp.mean(inner * normal, -1, keepdims=True)
    )


def half_turn(tensor):
    up = pltpu.roll(tensor, 96, 1)
    down = pltpu.roll(tensor, 32, 1)
    return jnp.where(lanes(tensor.shape) % 64 < 32, -up, down)


def padded(rows):
    return -(-rows // 32) * 16


def seal(packed):
    rows = packed.shape[0]
    return jnp.concatenate([packed, jnp.zeros((padded(2 * rows) - rows, 128), F32)], 0).astype(BF16)


def pack_pair(pair):
    rows = pair.shape[0] // 2
    top, bottom = pair[:rows], pltpu.roll(pair[rows:], 64, 1)
    low = lanes(top.shape) < 64
    return seal(jnp.where(low, top, bottom)), seal(jnp.where(low, bottom, top))


def unpack_pair(even, odd, rows):
    even, odd = even.astype(F32)[: rows // 2], odd.astype(F32)[: rows // 2]
    low = lanes(even.shape) < 64
    return jnp.concatenate([jnp.where(low, even, odd), pltpu.roll(jnp.where(low, odd, even), 64, 1)], 0)


def unpack_one(packed, rows):
    packed = packed.astype(F32)[: rows // 2]
    return jnp.concatenate([packed, pltpu.roll(packed, 64, 1)], 0)


def spill(ref, first, values):
    for group in range(GROUPS):
        ref[group, first : first + values.shape[0], :] = values[:, 128 * group : 128 * group + 128]


def every_third(ref, first, group):
    return ref[group, pl.ds(first, SHORT, 3), :]


def remote(src, dst, send, recv, device):
    return pltpu.make_async_remote_copy(
        src_ref=src, dst_ref=dst, send_sem=send, recv_sem=recv, device_id=device, device_id_type=MESH
    )


class Place:
    def __init__(self):
        self.row = lax.axis_index("row")
        self.seq = lax.axis_index("seq")
        self.core = lax.rem(self.row, 2)
        self.at = (self.row // 2, lax.rem(self.seq, 4), self.seq // 4)
        self.head = lax.rem(self.seq, 8)
        self.near = self.seq // 8 == self.core
        odd = lax.rem(self.seq, 2)
        self.same, self.next = self.near & (odd == self.core), self.near & (odd != self.core)
        self.sending, self.coming = [], {}

    def peer(self, axis, distance):
        to = lax.rem(self.at[axis] + distance, 4)
        if axis == X:
            return (to * 2 + self.core, self.seq)
        if axis == Y:
            return (self.row, self.at[Z] * 4 + to)
        return (self.row, to * 4 + self.at[Y])

    def partner(self):
        return (self.row + 1 - 2 * self.core, self.seq)

    def along(self, distance):
        return (self.row, lax.rem(self.seq + distance, SEQ))

    def _with_same(self, row, seq):
        return (row, seq), (row == self.row) & (seq == self.seq)

    def holder(self, head, core):
        return self._with_same(2 * self.at[X] + core, 8 * self.core + head)

    def owner(self, stretch):
        return self._with_same(2 * self.at[X] + self.seq // 8, stretch)

    def start(self, copy, key):
        copy.start()
        self.sending.append(copy.wait_send)
        self.coming[key] = copy.wait_recv

    def finish(self, copy, key):
        self.coming.pop(key)
        copy.wait_recv()

    def greet(self, barrier):
        def one(index, carry):
            for device, same in (self.holder(index // 2, lax.rem(index, 2)), self.owner(index)):

                @pl.when(jnp.logical_not(same))
                def _():
                    pl.semaphore_signal(barrier, inc=1, device_id=device, device_id_type=MESH)

            return carry

        lax.fori_loop(0, 16, one, 0)
        others = [self.partner(), self.along(1), self.along(SEQ - 1)]
        others += [self.peer(axis, distance) for axis in (X, Y, Z) for distance in (1, 2, 3)]
        for device in others:
            pl.semaphore_signal(barrier, inc=1, device_id=device, device_id_type=MESH)
        return 32 + len(others) - 2 * self.near.astype(jnp.int32)


COUNTS = [-(-2 * LONG * (pair + 1) // 128) * 128 for pair in range(8)]
FIRSTS = [sum(COUNTS[:pair]) for pair in range(8)]


class Layer:
    def __init__(self, at, ref, own, index, rows):
        self.at = at
        self.r = ref
        self.s = own
        self.index = index
        self.rows = rows
        self.slope = ref.dvalue if index else ref.dkey

    def _sem(self, row, column):
        rows = (0, 10, 20, 28, 36) if self.index == 0 else (0, 6, None, 12, 20)
        return self.s.sems.at[rows[row] + column]


    def _buffers(self, kind):
        s = self.s
        return {
            KV: (s.kv_out, s.kv_in), Q: (s.q_out, s.q_in), DM: (s.dm_out, s.dm_in), MIX: (s.mix_out, s.mix_in),
            DKV: (s.dkv_out, s.dkv_in), DQ: (s.dq_out, s.dq_in), TAIL: (self.r.tail_out, self.r.tail_in),
        }[kind]

    def _wide(self, kind):
        return self.index == 1 and kind in (KV, DKV)

    def _copy(self, kind, index):
        at = self.at
        out, into = self._buffers(kind)
        source, recv = index, self._sem(1, kind)
        if kind in (KV, Q, DM):
            if self._wide(kind):
                source = index // 2
                device, same = at.holder(source, lax.rem(index, 2))
            else:
                device, same = at.holder(index, lax.rem(at.seq, 2))
            target = at.seq if kind == KV else at.seq // 2
            if kind == KV and not self._wide(kind):
                recv = self._sem(2, at.seq // 2)
            into = into.at[target]
        elif self._wide(kind):
            device, same = at.owner(index)
            into = into.at[at.core, at.head]
        else:
            device, same = at.owner(lax.rem(2 * index + at.core + (1 if kind == TAIL else 0), SEQ))
            into = into.at[at.head]
        return out.at[source], into, self._sem(0, kind), recv, device, same

    def send_one(self, kind, index):
        src, dst, send, recv, device, same = self._copy(kind, index)

        @pl.when(same)
        def _():
            pltpu.make_async_copy(src, dst, recv).start()

        @pl.when(jnp.logical_not(same))
        def _():
            remote(src, dst, send, recv, device).start()

    def send_some(self, kind, first):
        def one(step, carry):
            index = lax.rem(step + self.at.head, 4) + first
            self.send_one(kind, index)
            if kind == MIX:
                self.send_one(TAIL, index)
            return carry

        lax.fori_loop(0, 4, one, 0)

    def send_rest(self, kind):
        self.at.sending.append(lambda: self.sent(kind))
        self.at.coming[(self.index, kind)] = lambda: self.receive(kind)

    def send(self, kind):
        count = 16 if self._wide(kind) else 8
        begin = self.at.seq // 2 if kind in (KV, Q, DM) else self.at.head
        begin = begin * (count // 8)

        def one(step, carry):
            self.send_one(kind, lax.rem(step + begin, count))
            return carry

        lax.fori_loop(0, count, one, 0)
        self.send_rest(kind)

    def _wait(self, place, send, recv):
        return remote(place, place, send, recv, self.at.partner())

    def receive(self, kind):
        self.at.coming.pop((self.index, kind), None)
        self._wait(self._buffers(kind)[1], self._sem(0, kind), self._sem(1, kind)).wait_recv()

    def sent(self, kind):
        count = 16 if self._wide(kind) else 8
        many = self.s.kv_in if kind == KV else self._buffers(kind)[0]
        inside = self.at.near if self._wide(kind) else self.at.next if kind == TAIL else self.at.same
        for number, when in ((count - 1, inside), (count, jnp.logical_not(inside))):

            @pl.when(when)
            def _():
                self._wait(many.at[pl.ds(0, number)], self._sem(0, kind), self._sem(1, kind)).wait_send()

    def _relay(self, index):
        place = self.s.kv_in.at[2 * index + self.at.core]
        return remote(place, place, self._sem(0, RELAY), self._sem(1, RELAY), self.at.partner())

    def receive_keys(self):
        if self._wide(KV):
            self.receive(KV)
            return
        self.at.coming.pop((self.index, KV), None)
        s = self.s

        def one(index, carry):
            self._wait(s.kv_in.at[0], self._sem(0, KV), self._sem(2, index)).wait_recv()
            self._relay(index).start()
            return carry

        lax.fori_loop(0, 8, one, 0)
        relayed = self._wait(s.kv_in.at[pl.ds(0, 8)], self._sem(0, RELAY), self._sem(1, RELAY))
        relayed.wait_recv()
        self.at.sending.append(relayed.wait_send)


    def angles(self):
        table, first = self.r.offsets, self.r.firsts
        place = self.index * SEQ + self.at.seq
        cos_a, sin_a = first[0, pl.ds(place, 1), :], first[1, pl.ds(place, 1), :]
        cos_b, sin_b = table[0, : self.rows, :], table[1, : self.rows, :]
        return cos_a * cos_b - sin_a * sin_b, sin_a * cos_b + cos_a * sin_b

    def gain(self, which):
        return self.r.gains[self.index, which : which + 1, :].astype(F32)

    def project(self, values, ready=None):
        s, rows = self.s, self.rows
        normal, scale = normalize(values)
        s.normal[0] = normal
        s.scale[0] = jnp.broadcast_to(scale, (rows, 128))
        normed = (normal * self.gain(0)).astype(BF16)
        s.n1[...] = normed
        cosine, sine = self.angles()
        low = lanes((rows, 128)) < 64
        weight = self.r.wqkv.at[self.index]
        for group in range(GROUPS):
            key = dot(normed, weight[:, 512 + 128 * group : 640 + 128 * group])
            value = dot(normed, weight[:, 1024 + 128 * group : 1152 + 128 * group])
            key = key * cosine + half_turn(key) * sine
            value = pltpu.roll(value, 64, 1)
            s.kv_out[2 * group, :rows] = jnp.where(low, key, value).astype(BF16)
            s.kv_out[2 * group + 1, :rows] = jnp.where(low, value, key).astype(BF16)
            query = dot(normed, weight[:, 128 * group : 128 * group + 128])
            query = (query * cosine + half_turn(query) * sine) * 0.125
            s.q_out[2 * group], s.q_out[2 * group + 1] = pack_pair(query)
        if ready is not None:
            ready()
        self.send(KV)
        self.send(Q)

    def native(self, shape):
        return (lanes(shape) // 64) == lax.rem(self.at.seq, 2)

    def pack_one(self, values):
        rows = self.rows // 2
        return seal(jnp.where(self.native((rows, 128)), values[:rows], pltpu.roll(values[rows:], 64, 1)))

    def split_heads(self):
        s, length = self.s, SEQ * self.rows
        both = s.kv_in[:, : self.rows, :].reshape(length, 128).astype(F32)
        own = self.native((length, 128))
        s.key[...] = jnp.where(own, both, 0.0).astype(BF16)
        s.value[...] = jnp.where(own, pltpu.roll(both, 64, 1), 0.0).astype(BF16)

    def attend(self):
        s, core = self.s, self.at.core
        for index in range(8):
            s.query[index] = unpack_one(s.q_in[index], self.rows).astype(BF16)
        if self.index == 0:
            for pair in reversed(range(8)):
                count = COUNTS[pair]
                score = dot_nt(s.query[pair], s.key[:count])
                first = (288 * pair) // 128 * 128
                column = s.column[:, pair : pair + 1]
                allowed = s.line[0:1, :count] == column
                position = sublanes((LONG, count - first)) + (2 * pair + core) * LONG
                causal = lanes((LONG, count - first)) + first <= position
                if first:
                    head = jnp.where(allowed[:, :first], score[:, :first], -1e9)
                    tail = jnp.where(allowed[:, first:] & causal, score[:, first:], -1e9)
                    score = jnp.concatenate([head, tail], 1)
                else:
                    score = jnp.where(allowed & causal, score, -1e9)
                top = jnp.max(score, -1, keepdims=True)
                expo = jnp.exp(score - top)
                share = 1.0 / jnp.sum(expo, -1, keepdims=True)
                expo = expo.astype(BF16)
                s.expo[:, FIRSTS[pair] : FIRSTS[pair] + count] = expo
                s.part[:, pair : pair + 1] = share
                mixed = dot(expo, s.value[:count]) * share
                s.mix_out[pair] = self.pack_one(mixed)
                tail = mixed[LONG - EXTRA :]
                self.r.tail_out[pair] = jnp.where(self.native(tail.shape), tail, 0.0).astype(BF16)
                if pair == 4:
                    self.send_some(MIX, 4)
            self.send_some(MIX, 0)
            self.send_rest(MIX)
            self.send_rest(TAIL)
        else:
            count, length = 8 * SHORT, SEQ * SHORT
            score = dot_nt(s.query[...].reshape(count, 128), s.key[...])
            column = s.column[...].reshape(count, 128)[:, :1]
            row = lax.broadcasted_iota(jnp.int32, (8, SHORT, length), 1)
            block = lax.broadcasted_iota(jnp.int32, (8, SHORT, length), 0)
            position = (row + (2 * block + core) * SHORT).reshape(count, length)
            causal = lanes((count, length)) <= position
            score = jnp.where((s.line[0:1, :] == column) & causal, score, -1e9)
            top = jnp.max(score, -1, keepdims=True)
            expo = jnp.exp(score - top)
            share = 1.0 / jnp.sum(expo, -1, keepdims=True)
            expo = expo.astype(BF16)
            s.expo[...] = expo
            s.part[...] = jnp.broadcast_to(share, (count, 128)).reshape(8, SHORT, 128)
            mixed = (dot(expo, s.value[...]) * share).reshape(8, SHORT, 128)
            for index in range(8):
                s.mix_out[index] = self.pack_one(mixed[index])
            self.send(MIX)

    def feed_forward(self, values):
        i, s, rows = self.index, self.s, self.rows
        parts = [unpack_pair(s.mix_in[2 * g], s.mix_in[2 * g + 1], rows) for g in range(GROUPS)]
        mixed = jnp.concatenate(parts, 1).astype(BF16)
        s.mixed[...] = mixed
        if i == 0:
            tails = [self.r.tail_in[2 * g] + self.r.tail_in[2 * g + 1] for g in range(GROUPS)]
            mixed = jnp.concatenate([mixed, jnp.concatenate(tails, 1)], 0)
        first = values + dot(mixed, self.r.wout[i])
        normal, scale = normalize(first)
        s.normal[1] = normal[:rows]
        s.scale[1] = jnp.broadcast_to(scale[:rows], (rows, 128))
        normed = (normal * self.gain(1)).astype(BF16)
        s.n2[...] = normed[:rows]
        result = first
        for part in range(4):
            at = slice(512 * part, 512 * part + 512)
            hidden = dot(normed, self.r.wup[i, :, at])
            inner = 0.7978845608028654 * (hidden + 0.044715 * hidden * hidden * hidden)
            bend = jnp.tanh(inner)
            active = (0.5 * hidden * (1.0 + bend)).astype(BF16)
            result = result + dot(active, self.r.wdown[i, at, :])
            s.act[part // 2, :, 512 * (part % 2) : 512 * (part % 2) + 512] = active[:rows]
            hidden, bend = hidden[:rows], bend[:rows]
            slope = 0.5 * (1.0 + bend) + 0.5 * hidden * (1.0 - bend * bend) * (
                0.7978845608028654 * (1.0 + 3.0 * 0.044715 * hidden * hidden)
            )
            for column in range(4):
                place = rows * (4 * part + column)
                self.slope[place : place + rows, :] = slope[:, 128 * column : 128 * column + 128]
        return result


    def feed_back(self, grad):
        i, s = self.index, self.s
        low = grad.astype(BF16)
        s.glow[...] = low
        self.swap((0,))
        back = jnp.zeros((self.rows, D), F32)
        for part in range(4):
            at = slice(512 * part, 512 * part + 512)
            active = dot_nt(low, self.r.wdown[i, at, :])
            places = [self.rows * (4 * part + column) for column in range(4)]
            slope = jnp.concatenate([self.slope[place : place + self.rows, :] for place in places], 1)
            hidden = (slope * active).astype(BF16)
            s.dhid[part // 2, :, 512 * (part % 2) : 512 * (part % 2) + 512] = hidden
            back = back + dot_nt(hidden, self.r.wup[i, :, at])
        self.swap((3,))
        normal, scale = s.normal[1], s.scale[1][:, :1]
        self.r.gsum[2 * i + 1 : 2 * i + 2, :] = jnp.sum(back * normal, 0, keepdims=True)
        first = grad + normalize_back(back, normal, scale, self.gain(1))
        s.dfirst[...] = first
        first_low = first.astype(BF16)
        s.dv1[0] = first_low[:, :256]
        s.dv1[1] = first_low[:, 256:]
        self.swap((5,))
        for group in range(GROUPS):
            weight = self.r.wout[i, 128 * group : 128 * group + 128, :]
            s.dm_out[2 * group], s.dm_out[2 * group + 1] = pack_pair(dot_nt(first_low, weight))
        self.send(DM)

    def attend_back(self, between):
        s, length = self.s, SEQ * self.rows
        own = self.native((length, 128))
        if self.index == 0:
            for pair in reversed(range(8)):
                count = COUNTS[pair]
                share = s.part[:, pair : pair + 1]
                grad = (unpack_one(s.dm_in[pair], self.rows) * share).astype(BF16)
                expo = s.expo[:, FIRSTS[pair] : FIRSTS[pair] + count]
                weighted = expo * dot_nt(grad, s.value[:count])
                inner = jnp.sum(weighted, -1, keepdims=True) * share
                draw = (weighted - expo * inner).astype(BF16)
                s.dq_out[pair] = self.pack_one(dot(draw, s.key[:count]) * 0.125)
                for total, left, right in ((self.r.dkey, draw, s.query[pair]), (self.r.dvalue, expo, grad)):
                    if pair == 7:
                        total[...] = dot_tn(left, right)
                    else:
                        total[:count] += dot_tn(left, right)
                if pair == 4:
                    self.part_done(1)
                    self.send_some(DQ, 4)
                if pair == 1:
                    self.merge(1)
                between(10 + pair)
            self.part_done(0)
            self.send_some(DQ, 0)
            self.send_rest(DQ)
            return
        else:
            count = 8 * SHORT
            share = s.part[...].reshape(count, 128)
            grad = jnp.concatenate([unpack_one(s.dm_in[index], self.rows) for index in range(8)], 0)
            grad = (grad * share).astype(BF16)
            expo = s.expo[...]
            weighted = expo * dot_nt(grad, s.value[...])
            inner = jnp.sum(weighted, -1, keepdims=True) * share[:, :1]
            draw = (weighted - expo * inner).astype(BF16)
            dq = (dot(draw, s.key[...]) * 0.125).reshape(8, SHORT, 128)
            for index in range(8):
                s.dq_out[index] = self.pack_one(dq[index])
            dkey = dot_tn(draw, s.query[...].reshape(count, 128))
            dvalue = dot_tn(expo, grad)
        self.send(DQ)
        both = jnp.where(own, dkey, pltpu.roll(dvalue, 64, 1)).astype(BF16)
        s.dkv_out[...] = both.reshape(SEQ, self.rows, 128)

    def part_done(self, half):
        s, rows = self.s, SEQ * self.rows // 2
        place = slice(rows * half, rows * half + rows)
        value = pltpu.roll(self.r.dvalue[place], 64, 1)
        both = jnp.where(self.native((rows, 128)), self.r.dkey[place], value).astype(BF16)
        both = both.reshape(4, 2, self.rows, 128)
        for which in range(2):
            s.dkv_part[which, 4 * half : 4 * half + 4] = both[:, which]
        self.at.start(self._merge(half), (self.index, 14, half))

    def _merge(self, half):
        s, four = self.s, pl.ds(4 * half, 4)
        send, recv = self._sem(0, MERGE + half), self._sem(1, MERGE + half)
        return remote(s.dkv_part.at[1 - self.at.core, four], s.dkv_other.at[four], send, recv, self.at.partner())

    def merge(self, half):
        s, four = self.s, slice(4 * half, 4 * half + 4)
        self.at.finish(self._merge(half), (self.index, 14, half))
        s.dkv_out[four] = (s.dkv_part[self.at.core, four].astype(F32) + s.dkv_other[four].astype(F32)).astype(BF16)
        self.send_some(DKV, 4 * half)

    def project_back(self):
        i, s, rows = self.index, self.s, self.rows
        cosine, sine = self.angles()
        low = lanes((rows, 128)) < 64
        back = jnp.zeros((rows, D), F32)
        for group in range(GROUPS):
            if i:
                even, odd = (
                    s.dkv_in[0, head].astype(F32) + s.dkv_in[1, head].astype(F32)
                    for head in (2 * group, 2 * group + 1)
                )
            else:
                even, odd = s.dkv_in[2 * group].astype(F32), s.dkv_in[2 * group + 1].astype(F32)
            key = jnp.where(low, even, odd)
            key = key * cosine - half_turn(key) * sine
            value = pltpu.roll(jnp.where(low, odd, even), 64, 1)
            query = unpack_pair(s.dq_in[2 * group], s.dq_in[2 * group + 1], rows)
            query = query * cosine - half_turn(query) * sine
            for which, piece in enumerate((query, key, value)):
                place = 4 * which + group
                column = 128 * (place % 6)
                s.dproj[place // 6, :, column : column + 128] = piece.astype(BF16)
        for part in range(2):
            back = back + dot_nt(s.dproj[part], self.r.wqkv[i, :, 768 * part : 768 * part + 768])
        normal, scale = s.normal[0], s.scale[0][:, :1]
        self.r.gsum[2 * i : 2 * i + 1, :] = jnp.sum(back * normal, 0, keepdims=True)
        return s.dfirst[...] + normalize_back(back, normal, scale, self.gain(0))


    def _swap(self, which):
        s, other = self.s, 1 - self.at.core
        src, dst = (
            (s.glow, s.glow_in), (s.n2, s.n2_in), (s.act.at[other], s.act_in), (s.dhid.at[other], s.dhid_in),
            (s.mixed, s.mixed_in), (s.dv1.at[other], s.dv1_in), (s.n1, s.n1_in), (s.dproj.at[other], s.dproj_in),
        )[which]
        return remote(src, dst, self._sem(3, which), self._sem(4, which), self.at.partner())

    def swap(self, steps):
        copies = [self._swap(which) for which in steps]
        for copy in copies:
            copy.start()
        self.at.sending += [copy.wait_send for copy in copies]
        self.at.coming[(self.index, 10, steps)] = lambda: [copy.wait_recv() for copy in copies]

    def swapped(self, steps):
        self.at.coming.pop((self.index, 10, steps))()

    def grads_feed(self, total):
        s, core = self.s, self.at.core
        for part in range(4):
            at = slice(256 * part, 256 * part + 256)
            total.put_rows(
                part, dot_tn(s.act[core, :, at], s.glow[...]) + dot_tn(s.act_in[:, at], s.glow_in[...])
            )
        for part in range(2):
            at = slice(512 * part, 512 * part + 512)
            up = dot_tn(s.n2[...], s.dhid[core, :, at]) + dot_tn(s.n2_in[...], s.dhid_in[:, at])
            total.put_columns(4 + 2 * part, up[:, :256])
            total.put_columns(5 + 2 * part, up[:, 256:])
        total.put_columns(8, dot_tn(s.mixed[...], s.dv1[core]) + dot_tn(s.mixed_in[...], s.dv1_in[...]))

    def grads_attention(self, total, first):
        s, core = self.s, self.at.core
        grad = dot_tn(s.n1[...], s.dproj[core]) + dot_tn(s.n1_in[...], s.dproj_in[...])
        for part in range(3):
            total.put_columns(first + part, grad[:, 256 * part : 256 * part + 256])


class Total:
    def __init__(self, at, own, kind, result):
        self.at, self.s, self.kind, self.result = at, own, kind, result
        self.first, self.units = own.first, own.grads.shape[1]
        self.ring = self.units > 1
        self.spread = (self.units, self.units + 1, 0, self.units)[kind - 20]

    def put_rows(self, unit, values):
        values = values.astype(BF16)
        for group in range(4):
            self.s.grads[unit // self.units, unit % self.units, group] = values[
                :, 128 * group : 128 * group + 128
            ].reshape(4, 4, 16, 128)

    def put_columns(self, unit, values):
        values = values.astype(BF16)
        for group in range(2):
            self.s.grads[unit // self.units, unit % self.units, 2 * group : 2 * group + 2] = values[
                :, 128 * group : 128 * group + 128
            ].reshape(2, 4, 4, 16, 128)

    def _full(self, *places):
        if not places:
            places = (slice(None),)
        return self.result.at[(self.at.core, places[0], pl.ds(self.first, self.spread), *places[1:])]

    def _place(self, part, stage, distance=0):
        return lax.rem(self.at.at[ORDERS[part][stage]] + distance, 4)

    def _mine(self, part, count):
        return [self._place(part, before) for before in range(count)]

    def _remote(self, src, dst, part, stage, row, distance):
        sems = self.s.sems
        return remote(src, dst, sems.at[row, 0], sems.at[row, 1], self.at.peer(ORDERS[part][stage], distance))

    def _scatter(self, part, stage, distance):
        s = self.s
        src = s.grads.at[(part, slice(None), *self._mine(part, stage), self._place(part, stage, distance))]
        dst = (s.part0, s.part1, s.part2)[stage].at[part, distance - 1]
        return self._remote(src, dst, part, stage, stage, distance)

    def _gather(self, part, stage, distance):
        place = self._full(part, *[self._place(part, before) for before in range(stage + 1)])
        return self._remote(place, place, part, stage, 3 + stage, distance)

    def _whole(self, row):
        s, sems, every = self.s, self.s.sems, slice(None)
        if row in (0, 1, 2, HOP):
            place = s.hop if row == HOP else (s.part0, s.part1, s.part2)[row]
        else:
            three = pl.ds(0, 3)
            places = {
                3: (pl.ds(0, 2) if self.ring else three,), 4: (0, three), 5: (0, 0, three), 6: (), BACK: (0,),
            }[row]
            place = self._full(every, *places)
        return remote(place, place, sems.at[row, 0], sems.at[row, 1], self.at.partner())

    def _begin(self, copies, row):
        for copy in copies:
            copy.start()
        self.at.coming[(self.kind, row)] = lambda: self._whole(row).wait_recv()
        self.at.sending.append(lambda: self._whole(row).wait_send())

    def _arrive(self, row):
        self.at.coming.pop((self.kind, row))()

    def _direct(self, make, stage, row):
        self._begin([make(part, stage, distance) for part in range(3) for distance in (1, 3, 2)], row)

    def scatter(self):
        s = self.s
        if not self.ring:
            self._direct(self._scatter, 0, 0)
            return
        copies = []
        for part in range(3):
            opposite = s.grads.at[part, :, self._place(part, 0, 2)]
            copies += [
                self._remote(opposite.at[:, pl.ds(2 * way, 2)], s.hop.at[part, way], part, 0, HOP, distance)
                for way, distance in enumerate((1, 3))
            ]
        self._begin(copies, HOP)

    def turn(self):
        s = self.s
        self._arrive(HOP)
        copies = []
        for part in range(3):
            for way, distance in enumerate((1, 3)):
                place = self._place(part, 0, distance)
                half = pl.ds(2 * way, 2)
                total = s.grads[part, :, place, half].astype(F32) + s.hop[part, way].astype(F32)
                s.grads[part, :, place, half] = total.astype(BF16)
                copies.append(self._remote(s.grads.at[part, :, place], s.part0.at[part, way], part, 0, 0, distance))
        self._begin(copies, 0)

    def scattered(self, stage):
        s = self.s
        self._arrive(stage)
        got = (s.part0, s.part1, s.part2)[stage]
        for part in range(3):
            mine = self._mine(part, stage + 1)
            total = s.grads[(part, slice(None), *mine)].astype(F32)
            for index in range(got.shape[1]):
                total = total + got[part, index].astype(F32)
            total = total.astype(BF16)
            if stage < 2:
                s.grads[(part, slice(None), *mine)] = total
            else:
                self.result[(self.at.core, part, pl.ds(self.first, self.units), *mine)] = total
        if stage < 2:
            self._direct(self._scatter, stage + 1, stage + 1)
        elif self.spread:
            self._direct(self._gather, 2, 5)

    def gathered(self, stage, hold=False):
        self._arrive(3 + stage)
        if stage == 2:
            self._direct(self._gather, 1, 4)
        elif not hold:
            self.gather_last()

    def gather_last(self):
        if self.ring:
            self.gather_some(0, self.spread)
        else:
            self._direct(self._gather, 0, 3)
            self._pass((0,))

    def gather_some(self, begin, end):
        copies = []
        for part in range(3):
            units = pl.ds(self.first + begin, end - begin)
            place = self.result.at[self.at.core, part, units, self._place(part, 0)]
            copies += [self._remote(place, place, part, 0, 3, distance) for distance in (1, 3)]
        if end == self.spread:
            self._begin(copies, 3)
            self._pass((0,))
        else:
            for copy in copies:
                copy.start()

    def gather_turn(self):
        self._arrive(3)
        copies = []
        for part in range(3):
            for way, distance in enumerate((1, 3)):
                place = self._full(part, self._place(part, 0, 4 - distance), pl.ds(2 * way, 2))
                copies.append(self._remote(place, place, part, 0, BACK, distance))
        self._begin(copies, BACK)
        self._pass((1, 3))

    def gather_done(self):
        self._arrive(BACK if self.ring else 3)
        self._pass((2,) if self.ring else (1, 2, 3))

    def _pass(self, distances):
        sems = self.s.sems
        for part in range(3):
            for distance in distances:
                place = self._full(part, self._place(part, 0, distance))
                remote(place, place, sems.at[6, 0], sems.at[6, 1], self.at.partner()).start()
        if 2 in distances:
            self.at.coming[(self.kind, 6)] = lambda: self._whole(6).wait_recv()
            self.at.sending.append(lambda: self._whole(6).wait_send())


def vmem(**shapes):
    return {name: pltpu.VMEM(shape, kind) for name, (shape, kind) in shapes.items()}


def layer_scratch(index, rows):
    length, half = SEQ * rows, padded(rows)
    message = rows + (NOTE if index == 0 else 0)
    shapes = vmem(
        kv_out=((8, message, 128), BF16), kv_in=((SEQ, message, 128), BF16),
        q_out=((8, half, 128), BF16), q_in=((8, half, 128), BF16),
        dm_out=((8, half, 128), BF16), dm_in=((8, half, 128), BF16),
        mix_out=((8, half, 128), BF16), mix_in=((8, half, 128), BF16),
        dq_out=((8, half, 128), BF16), dq_in=((8, half, 128), BF16),
        dkv_out=((16 if index else 8, rows, 128), BF16), dkv_in=((2, 8, rows, 128) if index else (8, rows, 128), BF16),
        query=((8, rows, 128), BF16), key=((length, 128), BF16), value=((length, 128), BF16),
        expo=((rows, sum(COUNTS)) if index == 0 else (8 * rows, length), BF16), part=((8, rows, 128) if index else (rows, 128), F32),
        normal=((2, rows, D), F32), scale=((2, rows, 128), F32),
        dfirst=((rows, D), F32),
        n1=((rows, D), BF16), n2=((rows, D), BF16), mixed=((rows, D), BF16), glow=((rows, D), BF16),
        act=((2, rows, FF // 2), BF16), dhid=((2, rows, FF // 2), BF16),
        dv1=((2, rows, 256), BF16), dproj=((2, rows, 768), BF16),
        n1_in=((rows, D), BF16), n2_in=((rows, D), BF16), mixed_in=((rows, D), BF16), glow_in=((rows, D), BF16),
        act_in=((rows, FF // 2), BF16), dhid_in=((rows, FF // 2), BF16),
        dv1_in=((rows, 256), BF16), dproj_in=((rows, 768), BF16),
        column=((8, rows, 128) if index else (rows, 128), F32), line=((8, length), F32),
    )
    if not index:
        shapes.update(vmem(dkv_part=((2, 8, rows, 128), BF16), dkv_other=((8, rows, 128), BF16)))
    shapes.update(sems=pltpu.SemaphoreType.DMA((28 if index else 44,)))
    return shapes


def total_scratch(units, rows):
    ways = 2 if units > 1 else 3
    shapes = vmem(
        grads=((3, units, 4, 4, 4, 16, 128), BF16), part0=((3, ways, units, 4, 4, 16, 128), BF16),
        part1=((3, 3, units, 4, 16, 128), BF16), part2=((3, 3, units, 16, 128), BF16),
    )
    if units > 1:
        shapes.update(vmem(hop=((3, 2, units, 2, 4, 16, 128), BF16)))
    shapes.update(sems=pltpu.SemaphoreType.DMA((rows, 2)))
    return shapes


def common_scratch():
    shapes = vmem(
        tokens=((LONG, D), BF16), cot=((LONG, D), BF16), seg=((1, LONG), jnp.int32), gains=((2, 2, D), BF16),
        offsets=((2, LONG, 128), F32), firsts=((2, 2 * SEQ, 128), F32),
        wqkv=((2, D, 3 * D), BF16), wout=((2, D, D), BF16),
        wup=((2, D, FF), BF16), wdown=((2, FF, D), BF16),
        dkey=((SEQ * LONG, 128), F32), dvalue=((SEQ * LONG, 128), F32),
        second=((4, LONG + 8, 128), F32), share=((4, SHORT + 8, 128), F32),
        work=((4, LONG, 128), F32),
        ahead=((4, 8, 128), F32), before=((EXTRA, D), BF16),
        tail_out=((8, EXTRA, 128), BF16), tail_in=((8, EXTRA, 128), BF16),
        output=((LONG, D), BF16), result=((LONG, D), F32),
        gsum=((8, D), F32), gain_in=((4, 4, 8, D), F32), gain_out=((3, 8, D), F32),
    )
    shapes.update(more=pltpu.SemaphoreType.DMA((29,)))
    return shapes


SPACES = (
    common_scratch(), layer_scratch(0, LONG), layer_scratch(1, SHORT),
    *(total_scratch(units, rows) for units, rows in zip(UNITS, (9, 9, 3, 7))),
)


def body(*refs):
    spaces, place = [], 14
    for part in SPACES:
        spaces.append(types.SimpleNamespace(**dict(zip(part, refs[place : place + len(part)]))))
        place += len(part)
    at = Place()
    steps(at, spaces, *refs[:14])
    for wait in at.coming.values():
        wait()
    for wait in at.sending:
        wait()


def steps(
    at, spaces, tokens, seg, wqkv, wout, wup, wdown, gains, cot, offsets, firsts,
    output, tokens_grad, sums, gain_sum,
):
    ref = spaces[0]
    more = ref.more
    full, short = Layer(at, ref, spaces[1], 0, LONG), Layer(at, ref, spaces[2], 1, SHORT)
    for kind in range(4):
        spaces[3 + kind].first = sum(UNITS[:kind])
    early, middle, minor, late = (Total(at, spaces[3 + kind], 20 + kind, sums) for kind in range(4))

    pairs = [
        (tokens, ref.tokens), (gains, ref.gains), (wqkv.at[0], ref.wqkv.at[0]),
        (offsets, ref.offsets), (firsts, ref.firsts), (seg, ref.seg),
        (wout.at[0], ref.wout.at[0]), (wup.at[0], ref.wup.at[0]), (wdown.at[0], ref.wdown.at[0]),
        (wqkv.at[1], ref.wqkv.at[1]), (cot, ref.cot),
        (wout.at[1], ref.wout.at[1]), (wup.at[1], ref.wup.at[1]), (wdown.at[1], ref.wdown.at[1]),
    ]
    loads = [pltpu.make_async_copy(src, dst, more.at[step]) for step, (src, dst) in enumerate(pairs)]
    for load in loads:
        load.start()
    waiting = list(range(len(loads)))

    def loaded(count):
        while waiting and waiting[0] < count:
            loads[waiting.pop(0)].wait()

    at.sending.append(lambda: loaded(len(loads)))
    barrier = pltpu.get_barrier_semaphore()
    greeted = at.greet(barrier)

    loaded(6)
    inputs = ref.tokens[...].astype(F32)
    def ready():
        line = ref.seg[...].astype(F32)
        high = jnp.floor(line * (1.0 / 64.0))
        rows = jnp.concatenate([high, line - 64.0 * high, jnp.zeros((6, LONG), F32)], 0)
        third = jnp.where(sublanes((LONG, 128)) == 3 * lanes((LONG, 128)), 1.0, 0.0)
        picked = dot(rows, third)
        wide = jnp.concatenate([rows[:, 128:], jnp.zeros((8, 112), F32)], 1)
        note = jnp.concatenate([rows[0:2, :128], wide[0:2], picked[0:2], jnp.zeros((10, 128), F32)], 0)
        for head in range(8):
            full.s.kv_out[head, LONG:] = note.astype(BF16)
        pl.semaphore_wait(barrier, greeted)
        at.start(
            remote(ref.tokens.at[pl.ds(LONG - EXTRA, EXTRA)], ref.before, more.at[17], more.at[18], at.along(1)), (3, 0)
        )

    full.project(inputs, ready)

    def segments():
        notes = [full.s.kv_in[block, LONG:, :].astype(F32) for block in range(SEQ)]
        for block, code in enumerate(notes):
            long = jnp.concatenate([64.0 * code[0:1] + code[1:2], 64.0 * code[2:3, :16] + code[3:4, :16]], 1)
            full.s.line[0:1, LONG * block : LONG * block + LONG] = long
            short.s.line[0:1, SHORT * block : SHORT * block + SHORT] = (64.0 * code[4:5] + code[5:6])[:, :SHORT]
        for layer in (full, short):
            rows = layer.rows
            equal = lanes((rows, rows)) == sublanes((rows, rows))
            for pair in range(8):
                code = full.s.kv_in[2 * pair + at.core, LONG:, :].astype(F32)
                if layer is full:
                    line = jnp.concatenate([64.0 * code[0:1] + code[1:2], 64.0 * code[2:3, :16] + code[3:4, :16]], 1)
                else:
                    line = (64.0 * code[4:5] + code[5:6])[:, :SHORT]
                column = jnp.sum(jnp.where(equal, line, 0.0), 1, keepdims=True)
                if layer is full:
                    layer.s.column[:, pair : pair + 1] = column
                else:
                    layer.s.column[pair] = jnp.broadcast_to(column, (rows, 128))

    def attention(layer):
        layer.receive_keys()
        if layer is full:
            segments()
        layer.split_heads()
        layer.receive(Q)
        layer.attend()
        layer.receive(MIX)
        if layer is full:
            layer.receive(TAIL)

    attention(full)
    loaded(9)
    second = ref.second
    at.coming.pop((3, 0))()
    wide = full.feed_forward(jnp.concatenate([inputs, ref.before[...].astype(F32)], 0))
    spill(second, 8, wide[:LONG])
    spill(second, 0, jnp.where(at.seq == 0, 0.0, wide[LONG + EXTRA - 8 :]))
    full.swap(AHEAD)
    loaded(11)
    pooled = jnp.concatenate(
        [
            (every_third(second, 6, g) + every_third(second, 7, g) + every_third(second, 8, g)) / 3.0
            for g in range(GROUPS)
        ],
        1,
    )
    short.project(pooled)
    loaded(14)
    work = ref.work
    spill(work, 0, ref.cot[...].astype(F32))
    grad_short = jnp.concatenate(
        [every_third(work, 0, g) + every_third(work, 1, g) + every_third(work, 2, g) for g in range(GROUPS)], 1
    )
    attention(short)
    result = short.feed_forward(pooled)
    short.swap(AHEAD)

    def backward(layer, total, grad, between):
        layer.feed_back(grad)
        between(0)
        layer.swapped(AHEAD)
        for which in BEHIND:
            layer.swapped((which,))
        layer.grads_feed(total)
        between(1)
        layer.receive(DM)
        layer.attend_back(between)
        if layer is full:
            layer.merge(0)
            layer.send_rest(DKV)
        else:
            layer.send(DKV)
        between(4)
        layer.receive(DQ)
        layer.receive(DKV)
        between(6)
        back = layer.project_back()
        layer.swap((7,))
        return back

    def finish_output():
        for group in range(GROUPS):
            at_lanes = slice(128 * group, 128 * group + 128)
            for step in range(3):
                second[group, pl.ds(8 + step, SHORT, 3), :] = every_third(second, 8 + step, group) + result[:, at_lanes]
            ref.output[:, at_lanes] = second[group, 8:, :].astype(BF16)
        store = pltpu.make_async_copy(ref.output, output, more.at[14])
        store.start()
        at.sending.append(store.wait)

    def between_short(point):
        if point == 0:
            finish_output()
        elif point == 1:
            early.scatter()
        elif point == 4:
            early.turn()

    share = ref.share
    spill(share, 0, backward(short, early, grad_short, between_short) * (1.0 / 3.0))

    def halo_back():
        return remote(share.at[:, pl.ds(0, 8), :], ref.ahead, more.at[19], more.at[20], at.along(SEQ - 1))

    at.start(halo_back(), (3, 1))
    short.swapped((7,))
    short.grads_attention(minor, 0)
    at.finish(halo_back(), (3, 1))
    share[:, SHORT:, :] = jnp.where(at.seq == SEQ - 1, 0.0, ref.ahead[...])
    for group in range(GROUPS):
        own, following = share[group, 0:SHORT, :], share[group, 1 : SHORT + 1, :]
        for step, piece in enumerate((own, following, following)):
            work[group, pl.ds(step, SHORT, 3), :] = every_third(work, step, group) + piece
    grad_full = jnp.concatenate([work[group] for group in range(GROUPS)], 1)

    def between_full(point):
        if point == 0:
            early.scattered(0)
        elif point == 1:
            middle.scatter()
            minor.scatter()
        elif point == 17:
            early.scattered(1)
        elif point == 14:
            middle.turn()
        elif point == 13:
            early.scattered(2)
        elif point == 11:
            minor.scattered(0)
        elif point == 4:
            middle.scattered(0)
            early.gathered(2)
            minor.scattered(1)

    ref.result[...] = backward(full, middle, grad_full, between_full)
    store = pltpu.make_async_copy(ref.result, tokens_grad, more.at[15])
    store.start()
    at.sending.append(store.wait)
    full.swapped((7,))
    full.grads_attention(late, 0)
    late.scatter()
    gsum, gain_in, gain_out = ref.gsum, ref.gain_in, ref.gain_out

    def gain_copy(axis, distance):
        src = gsum if axis == 0 else gain_out.at[axis - 1]
        return remote(src, gain_in.at[axis, at.at[axis]], more.at[23 + axis], more.at[26 + axis], at.peer(axis, distance))

    def gain_step(axis):
        for distance in (1, 2, 3):
            gain_copy(axis, distance).start()
        gain_in[axis, at.at[axis]] = gsum[...] if axis == 0 else gain_out[axis - 1]
        three = gain_in.at[axis, pl.ds(0, 3)]
        copies = remote(three, three, more.at[23 + axis], more.at[26 + axis], at.partner())
        at.coming[(4, axis)] = copies.wait_recv
        at.sending.append(copies.wait_send)

    def gain_done(axis):
        at.coming.pop((4, axis))()
        return (gain_in[axis, 0] + gain_in[axis, 1]) + (gain_in[axis, 2] + gain_in[axis, 3])

    gsum[4:, :] = jnp.zeros((4, D), F32)
    gain_step(0)
    middle.scattered(1)
    minor.scattered(2)
    early.gathered(1)
    late.scattered(0)
    middle.scattered(2)
    late.scattered(1)
    middle.gathered(2)
    gain_out[0] = gain_done(0)
    gain_step(1)
    late.scattered(2)
    early.gather_turn()
    middle.gathered(1, True)
    middle.gather_some(0, 2)
    late.gathered(2)
    gain_out[1] = gain_done(1)
    gain_step(2)
    middle.gather_some(2, 4)
    late.gathered(1)
    early.gather_done()
    middle.gather_turn()
    gain_in[3, 0] = gain_done(2)
    gain_swap = remote(gain_in.at[3, 0], gain_in.at[3, 1], more.at[21], more.at[22], at.partner())
    at.start(gain_swap, (4, 3, 0))
    late.gather_done()
    middle.gather_done()
    at.finish(gain_swap, (4, 3, 0))
    gain_out[2] = gain_in[3, 0] + gain_in[3, 1]
    store = pltpu.make_async_copy(gain_out.at[2], gain_sum, more.at[16])
    store.start()
    at.sending.append(store.wait)


def tables():
    freq = 10000.0 ** (-np.arange(32) / 32.0)
    freq = np.tile(freq, 4)[None, :]
    offset = np.arange(LONG)[:, None] * freq
    first = np.concatenate([np.arange(SEQ) * LONG, np.arange(SEQ) * SHORT])[:, None] * freq
    return (
        np.stack([np.cos(offset), np.sin(offset)]).astype(np.float32),
        np.stack([np.cos(first), np.sin(first)]).astype(np.float32),
    )


def widen_body(
    sums, gain, output, grad, qkv, out, up, down, gains, output_too, grad_too,
    gain_in, gain_out, output_in, grad_in, down_out, up_out, out_out, qkv_out, sems,
):
    small = [
        pltpu.make_async_copy(gain, gain_in, sems.at[0, 0]),
        pltpu.make_async_copy(output, output_in, sems.at[0, 1]),
        pltpu.make_async_copy(grad, grad_in, sems.at[0, 2]),
    ]
    stores = []
    for copy in small:
        copy.start()

    def put(dst, src, slot):
        copy = pltpu.make_async_copy(src, dst, sems.at[1 + slot // 8, slot % 8])
        copy.start()
        stores.append(copy)

    def tiles(kind, half, unit):
        return sums.at[half, unit // UNITS[kind], sum(UNITS[:kind]) + unit % UNITS[kind]]

    def rows_of(kind, half, unit, dst, first_row):
        ref = tiles(kind, half, unit)
        for group in range(4):
            values = ref[group].reshape(256, 128).astype(F32)
            dst[first_row : first_row + 256, 128 * group : 128 * group + 128] = values

    def columns_of(kind, half, unit, dst, column):
        ref = tiles(kind, half, unit)
        for group in range(2):
            values = ref[2 * group : 2 * group + 2].reshape(512, 128).astype(F32)
            dst[:, column + 128 * group : column + 128 * group + 128] = values

    def feed(kind, half, block):
        at = 2 * block + half
        for unit in range(4):
            rows_of(kind, half, unit, down_out.at[at], 256 * unit)
        put(down.at[block, pl.ds(1024 * half, 1024), :], down_out.at[at], at)

    def rest(kind, block, kind_heads, unit):
        for half in range(2):
            for part in range(4):
                columns_of(kind, half, 4 + part, up_out.at[block], 1024 * half + 256 * part)
        put(up.at[block], up_out.at[block], 4 + block)
        for half in range(2):
            columns_of(kind, half, 8, out_out.at[block], 256 * half)
        put(out.at[block], out_out.at[block], 6 + block)
        for half in range(2):
            for part in range(3):
                columns_of(kind_heads, half, unit + part, qkv_out.at[block], 768 * half + 256 * part)
        put(qkv.at[block], qkv_out.at[block], 8 + block)

    def through():
        for copy in small:
            copy.wait()
        gain_out[...] = gain_in[0:4, :].reshape(2, 2, D)
        put(gains, gain_out, 10)
        put(output_too.at[0], output_in, 11)
        put(grad_too.at[0], grad_in, 12)

    for kind, block, kind_heads, unit in ((0, 1, 2, 0), (1, 0, 3, 0)):
        for half in range(2):
            feed(kind, half, block)
        rest(kind, block, kind_heads, unit)
        if kind == 0:
            through()
    for copy in stores:
        copy.wait()


def widen(sums, gain, output, grad):
    anywhere, inside = pl.BlockSpec(memory_space=pl.ANY), pl.BlockSpec(memory_space=pltpu.VMEM)
    return pl.pallas_call(
        widen_body,
        out_shape=(
            jax.ShapeDtypeStruct((2, D, 3 * D), F32),
            jax.ShapeDtypeStruct((2, D, D), F32),
            jax.ShapeDtypeStruct((2, D, FF), F32),
            jax.ShapeDtypeStruct((2, FF, D), F32),
            jax.ShapeDtypeStruct((2, 2, D), F32),
            jax.ShapeDtypeStruct((1, LONG, D), BF16),
            jax.ShapeDtypeStruct((1, LONG, D), F32),
        ),
        in_specs=[inside] + [anywhere] * 3,
        out_specs=(anywhere,) * 7,
        scratch_shapes=[
            pltpu.VMEM((8, D), F32),
            pltpu.VMEM((2, 2, D), F32),
            pltpu.VMEM((LONG, D), BF16),
            pltpu.VMEM((LONG, D), F32),
            pltpu.VMEM((4, 1024, 512), F32),
            pltpu.VMEM((2, 512, 2048), F32),
            pltpu.VMEM((2, 512, 512), F32),
            pltpu.VMEM((2, 512, 1536), F32),
            pltpu.SemaphoreType.DMA((3, 8)),
        ],
        compiler_params=pltpu.CompilerParams(vmem_limit_bytes=40 * 2**20),
        name="widen",
    )(
        pltpu.with_memory_space_constraint(sums, pltpu.VMEM),
        *(pltpu.with_memory_space_constraint(array, pltpu.HBM) for array in (gain, output, grad)),
    )


def per_device(tokens, segment, w_qkv, w_out, w_up, w_down, gains, cotangent):
    offsets, firsts = tables()
    anywhere, inside = pl.BlockSpec(memory_space=pl.ANY), pl.BlockSpec(memory_space=pltpu.VMEM)
    output, tokens_grad, sums, gain = pl.pallas_call(
        body,
        out_shape=(
            jax.ShapeDtypeStruct((LONG, D), BF16),
            jax.ShapeDtypeStruct((LONG, D), F32),
            pltpu.VMEM((2, 3, sum(UNITS), 4, 4, 4, 16, 128), BF16),
            jax.ShapeDtypeStruct((8, D), F32),
        ),
        in_specs=[anywhere] * 10,
        out_specs=(anywhere, anywhere, inside, anywhere),
        scratch_shapes=[shape for part in SPACES for shape in part.values()],
        compiler_params=pltpu.CompilerParams(
            collective_id=0, has_side_effects=True, vmem_limit_bytes=51 * 2**20
        ),
        name="layers",
    )(
        tokens[0], segment, w_qkv, w_out, w_up, w_down, gains, cotangent[0],
        jnp.asarray(offsets), jnp.asarray(firsts),
    )
    qkv, out, up, down, gain, output, tokens_grad = widen(sums, gain, output, tokens_grad)
    return output, tokens_grad, qkv, out, up, down, gain


def solution(mesh):
    return jax.shard_map(
        per_device,
        mesh=mesh,
        in_specs=(
            P("row", "seq", None),
            P("row", "seq"),
            P(),
            P(),
            P(),
            P(),
            P(),
            P("row", "seq", None),
        ),
        out_specs=(P("row", "seq", None), P("row", "seq", None), P(), P(), P(), P(), P()),
        check_vma=False,
    )
```

```python
import types

import jax
import jax.numpy as jnp
import numpy as np
from jax import lax
from jax.experimental import pallas as pl
from jax.experimental.pallas import tpu as pltpu
from jax.sharding import PartitionSpec as P

MESH = pl.DeviceIdType.MESH
F32 = jnp.float32
BF16 = jnp.bfloat16

SEQ = 16
LONG = 144
SHORT = 48
D = 512
FF = 2048
GROUPS = 4
NOTE = 16
KV, Q, DM, MIX, DKV, DQ, RELAY, TAIL, MERGE = range(9)
AHEAD, BEHIND = (1, 2, 4, 6), (0, 3, 5)
EXTRA = 16
UNITS = (3, 3, 1, 1)
HOP, BACK = 7, 8
X, Y, Z = range(3)
ORDERS = ((X, Y, Z), (Y, Z, X), (Z, X, Y))


def dot(left, right):
    return jnp.dot(left, right, preferred_element_type=F32)


def dot_nt(left, right):
    return lax.dot_general(left, right, (((1,), (1,)), ((), ())), preferred_element_type=F32)


def dot_tn(left, right):
    return lax.dot_general(left, right, (((0,), (0,)), ((), ())), preferred_element_type=F32)


def lanes(shape):
    return lax.broadcasted_iota(jnp.int32, shape, len(shape) - 1)


def sublanes(shape):
    return lax.broadcasted_iota(jnp.int32, shape, len(shape) - 2)


def normalize(values):
    center = values - jnp.mean(values, -1, keepdims=True)
    scale = lax.rsqrt(jnp.mean(center * center, -1, keepdims=True) + 1e-05)
    return center * scale, scale


def normalize_back(grad, normal, scale, gain):
    inner = grad * gain
    return scale * (
        inner
        - jnp.mean(inner, -1, keepdims=True)
        - normal * jnp.mean(inner * normal, -1, keepdims=True)
    )


def half_turn(tensor):
    up = pltpu.roll(tensor, 96, 1)
    down = pltpu.roll(tensor, 32, 1)
    return jnp.where(lanes(tensor.shape) % 64 < 32, -up, down)


def padded(rows):
    return -(-rows // 32) * 16


def seal(packed):
    rows = packed.shape[0]
    return jnp.concatenate([packed, jnp.zeros((padded(2 * rows) - rows, 128), F32)], 0).astype(BF16)


def pack_pair(pair):
    rows = pair.shape[0] // 2
    top, bottom = pair[:rows], pltpu.roll(pair[rows:], 64, 1)
    low = lanes(top.shape) < 64
    return seal(jnp.where(low, top, bottom)), seal(jnp.where(low, bottom, top))


def unpack_pair(even, odd, rows):
    even, odd = even.astype(F32)[: rows // 2], odd.astype(F32)[: rows // 2]
    low = lanes(even.shape) < 64
    return jnp.concatenate([jnp.where(low, even, odd), pltpu.roll(jnp.where(low, odd, even), 64, 1)], 0)


def unpack_one(packed, rows):
    packed = packed.astype(F32)[: rows // 2]
    return jnp.concatenate([packed, pltpu.roll(packed, 64, 1)], 0)


def spill(ref, first, values):
    for group in range(GROUPS):
        ref[group, first : first + values.shape[0], :] = values[:, 128 * group : 128 * group + 128]


def every_third(ref, first, group):
    return ref[group, pl.ds(first, SHORT, 3), :]


def remote(src, dst, send, recv, device):
    return pltpu.make_async_remote_copy(
        src_ref=src, dst_ref=dst, send_sem=send, recv_sem=recv, device_id=device, device_id_type=MESH
    )


class Place:
    def __init__(self):
        self.row = lax.axis_index("row")
        self.seq = lax.axis_index("seq")
        self.core = lax.rem(self.row, 2)
        self.at = (self.row // 2, lax.rem(self.seq, 4), self.seq // 4)
        self.head = lax.rem(self.seq, 8)
        self.near = self.seq // 8 == self.core
        odd = lax.rem(self.seq, 2)
        self.same, self.next = self.near & (odd == self.core), self.near & (odd != self.core)
        self.sending, self.coming = [], {}

    def peer(self, axis, distance):
        to = lax.rem(self.at[axis] + distance, 4)
        if axis == X:
            return (to * 2 + self.core, self.seq)
        if axis == Y:
            return (self.row, self.at[Z] * 4 + to)
        return (self.row, to * 4 + self.at[Y])

    def partner(self):
        return (self.row + 1 - 2 * self.core, self.seq)

    def along(self, distance):
        return (self.row, lax.rem(self.seq + distance, SEQ))

    def _with_same(self, row, seq):
        return (row, seq), (row == self.row) & (seq == self.seq)

    def holder(self, head, core):
        return self._with_same(2 * self.at[X] + core, 8 * self.core + head)

    def owner(self, stretch):
        return self._with_same(2 * self.at[X] + self.seq // 8, stretch)

    def start(self, copy, key):
        copy.start()
        self.sending.append(copy.wait_send)
        self.coming[key] = copy.wait_recv

    def finish(self, copy, key):
        self.coming.pop(key)
        copy.wait_recv()

    def greet(self, barrier):
        def one(index, carry):
            for device, same in (self.holder(index // 2, lax.rem(index, 2)), self.owner(index)):

                @pl.when(jnp.logical_not(same))
                def _():
                    pl.semaphore_signal(barrier, inc=1, device_id=device, device_id_type=MESH)

            return carry

        lax.fori_loop(0, 16, one, 0)
        others = [self.partner(), self.along(1), self.along(SEQ - 1)]
        others += [self.peer(axis, distance) for axis in (X, Y, Z) for distance in (1, 2, 3)]
        for device in others:
            pl.semaphore_signal(barrier, inc=1, device_id=device, device_id_type=MESH)
        return 32 + len(others) - 2 * self.near.astype(jnp.int32)


COUNTS = [-(-2 * LONG * (pair + 1) // 128) * 128 for pair in range(8)]
FIRSTS = [sum(COUNTS[:pair]) for pair in range(8)]


class Layer:
    def __init__(self, at, ref, own, index, rows):
        self.at = at
        self.r = ref
        self.s = own
        self.index = index
        self.rows = rows
        self.slope = ref.dvalue if index else ref.dkey

    def _sem(self, row, column):
        rows = (0, 10, 20, 28, 36) if self.index == 0 else (0, 6, None, 12, 20)
        return self.s.sems.at[rows[row] + column]


    def _buffers(self, kind):
        s = self.s
        return {
            KV: (s.kv_out, s.kv_in), Q: (s.q_out, s.q_in), DM: (s.dm_out, s.dm_in), MIX: (s.mix_out, s.mix_in),
            DKV: (s.dkv_out, s.dkv_in), DQ: (s.dq_out, s.dq_in), TAIL: (self.r.tail_out, self.r.tail_in),
        }[kind]

    def _wide(self, kind):
        return self.index == 1 and kind in (KV, DKV)

    def _copy(self, kind, index):
        at = self.at
        out, into = self._buffers(kind)
        source, recv = index, self._sem(1, kind)
        if kind in (KV, Q, DM):
            if self._wide(kind):
                source = index // 2
                device, same = at.holder(source, lax.rem(index, 2))
            else:
                device, same = at.holder(index, lax.rem(at.seq, 2))
            target = at.seq if kind == KV else at.seq // 2
            if kind == KV and not self._wide(kind):
                recv = self._sem(2, at.seq // 2)
            into = into.at[target]
        elif self._wide(kind):
            device, same = at.owner(index)
            into = into.at[at.core, at.head]
        else:
            device, same = at.owner(lax.rem(2 * index + at.core + (1 if kind == TAIL else 0), SEQ))
            into = into.at[at.head]
        return out.at[source], into, self._sem(0, kind), recv, device, same

    def send_one(self, kind, index):
        src, dst, send, recv, device, same = self._copy(kind, index)

        @pl.when(same)
        def _():
            pltpu.make_async_copy(src, dst, recv).start()

        @pl.when(jnp.logical_not(same))
        def _():
            remote(src, dst, send, recv, device).start()

    def send_some(self, kind, first):
        def one(step, carry):
            index = lax.rem(step + self.at.head, 4) + first
            self.send_one(kind, index)
            if kind == MIX:
                self.send_one(TAIL, index)
            return carry

        lax.fori_loop(0, 4, one, 0)

    def send_rest(self, kind):
        self.at.sending.append(lambda: self.sent(kind))
        self.at.coming[(self.index, kind)] = lambda: self.receive(kind)

    def send(self, kind):
        count = 16 if self._wide(kind) else 8
        begin = self.at.seq // 2 if kind in (KV, Q, DM) else self.at.head
        begin = begin * (count // 8)

        def one(step, carry):
            self.send_one(kind, lax.rem(step + begin, count))
            return carry

        lax.fori_loop(0, count, one, 0)
        self.send_rest(kind)

    def _wait(self, place, send, recv):
        return remote(place, place, send, recv, self.at.partner())

    def receive(self, kind):
        self.at.coming.pop((self.index, kind), None)
        self._wait(self._buffers(kind)[1], self._sem(0, kind), self._sem(1, kind)).wait_recv()

    def sent(self, kind):
        count = 16 if self._wide(kind) else 8
        many = self.s.kv_in if kind == KV else self._buffers(kind)[0]
        inside = self.at.near if self._wide(kind) else self.at.next if kind == TAIL else self.at.same
        for number, when in ((count - 1, inside), (count, jnp.logical_not(inside))):

            @pl.when(when)
            def _():
                self._wait(many.at[pl.ds(0, number)], self._sem(0, kind), self._sem(1, kind)).wait_send()

    def _relay(self, index):
        place = self.s.kv_in.at[2 * index + self.at.core]
        return remote(place, place, self._sem(0, RELAY), self._sem(1, RELAY), self.at.partner())

    def receive_keys(self):
        if self._wide(KV):
            self.receive(KV)
            return
        self.at.coming.pop((self.index, KV), None)
        s = self.s

        def one(index, carry):
            self._wait(s.kv_in.at[0], self._sem(0, KV), self._sem(2, index)).wait_recv()
            self._relay(index).start()
            return carry

        lax.fori_loop(0, 8, one, 0)
        relayed = self._wait(s.kv_in.at[pl.ds(0, 8)], self._sem(0, RELAY), self._sem(1, RELAY))
        relayed.wait_recv()
        self.at.sending.append(relayed.wait_send)


    def angles(self):
        table, first = self.r.offsets, self.r.firsts
        place = self.index * SEQ + self.at.seq
        cos_a, sin_a = first[0, pl.ds(place, 1), :], first[1, pl.ds(place, 1), :]
        cos_b, sin_b = table[0, : self.rows, :], table[1, : self.rows, :]
        return cos_a * cos_b - sin_a * sin_b, sin_a * cos_b + cos_a * sin_b

    def gain(self, which):
        return self.r.gains[self.index, which : which + 1, :].astype(F32)

    def project(self, values, ready=None):
        s, rows = self.s, self.rows
        normal, scale = normalize(values)
        s.normal[0] = normal
        s.scale[0] = jnp.broadcast_to(scale, (rows, 128))
        normed = (normal * self.gain(0)).astype(BF16)
        s.n1[...] = normed
        cosine, sine = self.angles()
        low = lanes((rows, 128)) < 64
        weight = self.r.wqkv.at[self.index]
        for group in range(GROUPS):
            key = dot(normed, weight[:, 512 + 128 * group : 640 + 128 * group])
            value = dot(normed, weight[:, 1024 + 128 * group : 1152 + 128 * group])
            key = key * cosine + half_turn(key) * sine
            value = pltpu.roll(value, 64, 1)
            s.kv_out[2 * group, :rows] = jnp.where(low, key, value).astype(BF16)
            s.kv_out[2 * group + 1, :rows] = jnp.where(low, value, key).astype(BF16)
            query = dot(normed, weight[:, 128 * group : 128 * group + 128])
            query = (query * cosine + half_turn(query) * sine) * 0.125
            s.q_out[2 * group], s.q_out[2 * group + 1] = pack_pair(query)
        if ready is not None:
            ready()
        self.send(KV)
        self.send(Q)

    def native(self, shape):
        return (lanes(shape) // 64) == lax.rem(self.at.seq, 2)

    def pack_one(self, values):
        rows = self.rows // 2
        return seal(jnp.where(self.native((rows, 128)), values[:rows], pltpu.roll(values[rows:], 64, 1)))

    def split_heads(self):
        s, length = self.s, SEQ * self.rows
        both = s.kv_in[:, : self.rows, :].reshape(length, 128).astype(F32)
        own = self.native((length, 128))
        s.key[...] = jnp.where(own, both, 0.0).astype(BF16)
        s.value[...] = jnp.where(own, pltpu.roll(both, 64, 1), 0.0).astype(BF16)

    def attend(self):
        s, core = self.s, self.at.core
        for index in range(8):
            s.query[index] = unpack_one(s.q_in[index], self.rows).astype(BF16)
        if self.index == 0:
            for pair in reversed(range(8)):
                count = COUNTS[pair]
                score = dot_nt(s.query[pair], s.key[:count])
                first = (288 * pair) // 128 * 128
                column = s.column[:, pair : pair + 1]
                allowed = s.line[0:1, :count] == column
                position = sublanes((LONG, count - first)) + (2 * pair + core) * LONG
                causal = lanes((LONG, count - first)) + first <= position
                if first:
                    head = jnp.where(allowed[:, :first], score[:, :first], -1e9)
                    tail = jnp.where(allowed[:, first:] & causal, score[:, first:], -1e9)
                    score = jnp.concatenate([head, tail], 1)
                else:
                    score = jnp.where(allowed & causal, score, -1e9)
                top = jnp.max(score, -1, keepdims=True)
                expo = jnp.exp(score - top)
                share = 1.0 / jnp.sum(expo, -1, keepdims=True)
                expo = expo.astype(BF16)
                s.expo[:, FIRSTS[pair] : FIRSTS[pair] + count] = expo
                s.part[:, pair : pair + 1] = share
                mixed = dot(expo, s.value[:count]) * share
                s.mix_out[pair] = self.pack_one(mixed)
                tail = mixed[LONG - EXTRA :]
                self.r.tail_out[pair] = jnp.where(self.native(tail.shape), tail, 0.0).astype(BF16)
                if pair == 4:
                    self.send_some(MIX, 4)
            self.send_some(MIX, 0)
            self.send_rest(MIX)
            self.send_rest(TAIL)
        else:
            count, length = 8 * SHORT, SEQ * SHORT
            score = dot_nt(s.query[...].reshape(count, 128), s.key[...])
            column = s.column[...].reshape(count, 128)[:, :1]
            row = lax.broadcasted_iota(jnp.int32, (8, SHORT, length), 1)
            block = lax.broadcasted_iota(jnp.int32, (8, SHORT, length), 0)
            position = (row + (2 * block + core) * SHORT).reshape(count, length)
            causal = lanes((count, length)) <= position
            score = jnp.where((s.line[0:1, :] == column) & causal, score, -1e9)
            top = jnp.max(score, -1, keepdims=True)
            expo = jnp.exp(score - top)
            share = 1.0 / jnp.sum(expo, -1, keepdims=True)
            expo = expo.astype(BF16)
            s.expo[...] = expo
            s.part[...] = jnp.broadcast_to(share, (count, 128)).reshape(8, SHORT, 128)
            mixed = (dot(expo, s.value[...]) * share).reshape(8, SHORT, 128)
            for index in range(8):
                s.mix_out[index] = self.pack_one(mixed[index])
            self.send(MIX)

    def feed_forward(self, values):
        i, s, rows = self.index, self.s, self.rows
        parts = [unpack_pair(s.mix_in[2 * g], s.mix_in[2 * g + 1], rows) for g in range(GROUPS)]
        mixed = jnp.concatenate(parts, 1).astype(BF16)
        s.mixed[...] = mixed
        if i == 0:
            tails = [self.r.tail_in[2 * g] + self.r.tail_in[2 * g + 1] for g in range(GROUPS)]
            mixed = jnp.concatenate([mixed, jnp.concatenate(tails, 1)], 0)
        first = values + dot(mixed, self.r.wout[i])
        normal, scale = normalize(first)
        s.normal[1] = normal[:rows]
        s.scale[1] = jnp.broadcast_to(scale[:rows], (rows, 128))
        normed = (normal * self.gain(1)).astype(BF16)
        s.n2[...] = normed[:rows]
        result = first
        for part in range(4):
            at = slice(512 * part, 512 * part + 512)
            hidden = dot(normed, self.r.wup[i, :, at])
            inner = 0.7978845608028654 * (hidden + 0.044715 * hidden * hidden * hidden)
            bend = jnp.tanh(inner)
            active = (0.5 * hidden * (1.0 + bend)).astype(BF16)
            result = result + dot(active, self.r.wdown[i, at, :])
            s.act[part // 2, :, 512 * (part % 2) : 512 * (part % 2) + 512] = active[:rows]
            hidden, bend = hidden[:rows], bend[:rows]
            slope = 0.5 * (1.0 + bend) + 0.5 * hidden * (1.0 - bend * bend) * (
                0.7978845608028654 * (1.0 + 3.0 * 0.044715 * hidden * hidden)
            )
            for column in range(4):
                place = rows * (4 * part + column)
                self.slope[place : place + rows, :] = slope[:, 128 * column : 128 * column + 128]
        return result


    def feed_back(self, grad):
        i, s = self.index, self.s
        low = grad.astype(BF16)
        s.glow[...] = low
        self.swap((0,))
        back = jnp.zeros((self.rows, D), F32)
        for part in range(4):
            at = slice(512 * part, 512 * part + 512)
            active = dot_nt(low, self.r.wdown[i, at, :])
            places = [self.rows * (4 * part + column) for column in range(4)]
            slope = jnp.concatenate([self.slope[place : place + self.rows, :] for place in places], 1)
            hidden = (slope * active).astype(BF16)
            s.dhid[part // 2, :, 512 * (part % 2) : 512 * (part % 2) + 512] = hidden
            back = back + dot_nt(hidden, self.r.wup[i, :, at])
        self.swap((3,))
        normal, scale = s.normal[1], s.scale[1][:, :1]
        self.r.gsum[2 * i + 1 : 2 * i + 2, :] = jnp.sum(back * normal, 0, keepdims=True)
        first = grad + normalize_back(back, normal, scale, self.gain(1))
        s.dfirst[...] = first
        first_low = first.astype(BF16)
        s.dv1[0] = first_low[:, :256]
        s.dv1[1] = first_low[:, 256:]
        self.swap((5,))
        for group in range(GROUPS):
            weight = self.r.wout[i, 128 * group : 128 * group + 128, :]
            s.dm_out[2 * group], s.dm_out[2 * group + 1] = pack_pair(dot_nt(first_low, weight))
        self.send(DM)

    def attend_back(self, between):
        s, length = self.s, SEQ * self.rows
        own = self.native((length, 128))
        if self.index == 0:
            for pair in reversed(range(8)):
                count = COUNTS[pair]
                share = s.part[:, pair : pair + 1]
                grad = (unpack_one(s.dm_in[pair], self.rows) * share).astype(BF16)
                expo = s.expo[:, FIRSTS[pair] : FIRSTS[pair] + count]
                weighted = expo * dot_nt(grad, s.value[:count])
                inner = jnp.sum(weighted, -1, keepdims=True) * share
                draw = (weighted - expo * inner).astype(BF16)
                s.dq_out[pair] = self.pack_one(dot(draw, s.key[:count]) * 0.125)
                for total, left, right in ((self.r.dkey, draw, s.query[pair]), (self.r.dvalue, expo, grad)):
                    if pair == 7:
                        total[...] = dot_tn(left, right)
                    else:
                        total[:count] += dot_tn(left, right)
                if pair == 4:
                    self.part_done(1)
                    self.send_some(DQ, 4)
                if pair == 1:
                    self.merge(1)
                between(10 + pair)
            self.part_done(0)
            self.send_some(DQ, 0)
            self.send_rest(DQ)
            return
        else:
            count = 8 * SHORT
            share = s.part[...].reshape(count, 128)
            grad = jnp.concatenate([unpack_one(s.dm_in[index], self.rows) for index in range(8)], 0)
            grad = (grad * share).astype(BF16)
            expo = s.expo[...]
            weighted = expo * dot_nt(grad, s.value[...])
            inner = jnp.sum(weighted, -1, keepdims=True) * share[:, :1]
            draw = (weighted - expo * inner).astype(BF16)
            dq = (dot(draw, s.key[...]) * 0.125).reshape(8, SHORT, 128)
            for index in range(8):
                s.dq_out[index] = self.pack_one(dq[index])
            dkey = dot_tn(draw, s.query[...].reshape(count, 128))
            dvalue = dot_tn(expo, grad)
        self.send(DQ)
        both = jnp.where(own, dkey, pltpu.roll(dvalue, 64, 1)).astype(BF16)
        s.dkv_out[...] = both.reshape(SEQ, self.rows, 128)

    def part_done(self, half):
        s, rows = self.s, SEQ * self.rows // 2
        place = slice(rows * half, rows * half + rows)
        value = pltpu.roll(self.r.dvalue[place], 64, 1)
        both = jnp.where(self.native((rows, 128)), self.r.dkey[place], value).astype(BF16)
        both = both.reshape(4, 2, self.rows, 128)
        for which in range(2):
            s.dkv_part[which, 4 * half : 4 * half + 4] = both[:, which]
        self.at.start(self._merge(half), (self.index, 14, half))

    def _merge(self, half):
        s, four = self.s, pl.ds(4 * half, 4)
        send, recv = self._sem(0, MERGE + half), self._sem(1, MERGE + half)
        return remote(s.dkv_part.at[1 - self.at.core, four], s.dkv_other.at[four], send, recv, self.at.partner())

    def merge(self, half):
        s, four = self.s, slice(4 * half, 4 * half + 4)
        self.at.finish(self._merge(half), (self.index, 14, half))
        s.dkv_out[four] = (s.dkv_part[self.at.core, four].astype(F32) + s.dkv_other[four].astype(F32)).astype(BF16)
        self.send_some(DKV, 4 * half)

    def project_back(self):
        i, s, rows = self.index, self.s, self.rows
        cosine, sine = self.angles()
        low = lanes((rows, 128)) < 64
        back = jnp.zeros((rows, D), F32)
        for group in range(GROUPS):
            if i:
                even, odd = (
                    s.dkv_in[0, head].astype(F32) + s.dkv_in[1, head].astype(F32)
                    for head in (2 * group, 2 * group + 1)
                )
            else:
                even, odd = s.dkv_in[2 * group].astype(F32), s.dkv_in[2 * group + 1].astype(F32)
            key = jnp.where(low, even, odd)
            key = key * cosine - half_turn(key) * sine
            value = pltpu.roll(jnp.where(low, odd, even), 64, 1)
            query = unpack_pair(s.dq_in[2 * group], s.dq_in[2 * group + 1], rows)
            query = query * cosine - half_turn(query) * sine
            for which, piece in enumerate((query, key, value)):
                place = 4 * which + group
                column = 128 * (place % 6)
                s.dproj[place // 6, :, column : column + 128] = piece.astype(BF16)
        for part in range(2):
            back = back + dot_nt(s.dproj[part], self.r.wqkv[i, :, 768 * part : 768 * part + 768])
        normal, scale = s.normal[0], s.scale[0][:, :1]
        self.r.gsum[2 * i : 2 * i + 1, :] = jnp.sum(back * normal, 0, keepdims=True)
        return s.dfirst[...] + normalize_back(back, normal, scale, self.gain(0))


    def _swap(self, which):
        s, other = self.s, 1 - self.at.core
        src, dst = (
            (s.glow, s.glow_in), (s.n2, s.n2_in), (s.act.at[other], s.act_in), (s.dhid.at[other], s.dhid_in),
            (s.mixed, s.mixed_in), (s.dv1.at[other], s.dv1_in), (s.n1, s.n1_in), (s.dproj.at[other], s.dproj_in),
        )[which]
        return remote(src, dst, self._sem(3, which), self._sem(4, which), self.at.partner())

    def swap(self, steps):
        copies = [self._swap(which) for which in steps]
        for copy in copies:
            copy.start()
        self.at.sending += [copy.wait_send for copy in copies]
        self.at.coming[(self.index, 10, steps)] = lambda: [copy.wait_recv() for copy in copies]

    def swapped(self, steps):
        self.at.coming.pop((self.index, 10, steps))()

    def grads_feed(self, total):
        s, core = self.s, self.at.core
        for part in range(4):
            at = slice(256 * part, 256 * part + 256)
            total.put_rows(
                part, dot_tn(s.act[core, :, at], s.glow[...]) + dot_tn(s.act_in[:, at], s.glow_in[...])
            )
        for part in range(2):
            at = slice(512 * part, 512 * part + 512)
            up = dot_tn(s.n2[...], s.dhid[core, :, at]) + dot_tn(s.n2_in[...], s.dhid_in[:, at])
            total.put_columns(4 + 2 * part, up[:, :256])
            total.put_columns(5 + 2 * part, up[:, 256:])
        total.put_columns(8, dot_tn(s.mixed[...], s.dv1[core]) + dot_tn(s.mixed_in[...], s.dv1_in[...]))

    def grads_attention(self, total, first):
        s, core = self.s, self.at.core
        grad = dot_tn(s.n1[...], s.dproj[core]) + dot_tn(s.n1_in[...], s.dproj_in[...])
        for part in range(3):
            total.put_columns(first + part, grad[:, 256 * part : 256 * part + 256])


class Total:
    def __init__(self, at, own, kind, result):
        self.at, self.s, self.kind, self.result = at, own, kind, result
        self.first, self.units = own.first, own.grads.shape[1]
        self.ring = self.units > 1
        self.spread = (self.units, self.units + 1, 0, self.units)[kind - 20]

    def put_rows(self, unit, values):
        values = values.astype(BF16)
        for group in range(4):
            self.s.grads[unit // self.units, unit % self.units, group] = values[
                :, 128 * group : 128 * group + 128
            ].reshape(4, 4, 16, 128)

    def put_columns(self, unit, values):
        values = values.astype(BF16)
        for group in range(2):
            self.s.grads[unit // self.units, unit % self.units, 2 * group : 2 * group + 2] = values[
                :, 128 * group : 128 * group + 128
            ].reshape(2, 4, 4, 16, 128)

    def _full(self, *places):
        if not places:
            places = (slice(None),)
        return self.result.at[(self.at.core, places[0], pl.ds(self.first, self.spread), *places[1:])]

    def _place(self, part, stage, distance=0):
        return lax.rem(self.at.at[ORDERS[part][stage]] + distance, 4)

    def _mine(self, part, count):
        return [self._place(part, before) for before in range(count)]

    def _remote(self, src, dst, part, stage, row, distance):
        sems = self.s.sems
        return remote(src, dst, sems.at[row, 0], sems.at[row, 1], self.at.peer(ORDERS[part][stage], distance))

    def _scatter(self, part, stage, distance):
        s = self.s
        src = s.grads.at[(part, slice(None), *self._mine(part, stage), self._place(part, stage, distance))]
        dst = (s.part0, s.part1, s.part2)[stage].at[part, distance - 1]
        return self._remote(src, dst, part, stage, stage, distance)

    def _gather(self, part, stage, distance):
        place = self._full(part, *[self._place(part, before) for before in range(stage + 1)])
        return self._remote(place, place, part, stage, 3 + stage, distance)

    def _whole(self, row):
        s, sems, every = self.s, self.s.sems, slice(None)
        if row in (0, 1, 2, HOP):
            place = s.hop if row == HOP else (s.part0, s.part1, s.part2)[row]
        else:
            three = pl.ds(0, 3)
            places = {
                3: (pl.ds(0, 2) if self.ring else three,), 4: (0, three), 5: (0, 0, three), 6: (), BACK: (0,),
            }[row]
            place = self._full(every, *places)
        return remote(place, place, sems.at[row, 0], sems.at[row, 1], self.at.partner())

    def _begin(self, copies, row):
        for copy in copies:
            copy.start()
        self.at.coming[(self.kind, row)] = lambda: self._whole(row).wait_recv()
        self.at.sending.append(lambda: self._whole(row).wait_send())

    def _arrive(self, row):
        self.at.coming.pop((self.kind, row))()

    def _direct(self, make, stage, row):
        self._begin([make(part, stage, distance) for part in range(3) for distance in (1, 3, 2)], row)

    def scatter(self):
        s = self.s
        if not self.ring:
            self._direct(self._scatter, 0, 0)
            return
        copies = []
        for part in range(3):
            opposite = s.grads.at[part, :, self._place(part, 0, 2)]
            copies += [
                self._remote(opposite.at[:, pl.ds(2 * way, 2)], s.hop.at[part, way], part, 0, HOP, distance)
                for way, distance in enumerate((1, 3))
            ]
        self._begin(copies, HOP)

    def turn(self):
        s = self.s
        self._arrive(HOP)
        copies = []
        for part in range(3):
            for way, distance in enumerate((1, 3)):
                place = self._place(part, 0, distance)
                half = pl.ds(2 * way, 2)
                total = s.grads[part, :, place, half].astype(F32) + s.hop[part, way].astype(F32)
                s.grads[part, :, place, half] = total.astype(BF16)
                copies.append(self._remote(s.grads.at[part, :, place], s.part0.at[part, way], part, 0, 0, distance))
        self._begin(copies, 0)

    def scattered(self, stage):
        s = self.s
        self._arrive(stage)
        got = (s.part0, s.part1, s.part2)[stage]
        for part in range(3):
            mine = self._mine(part, stage + 1)
            total = s.grads[(part, slice(None), *mine)].astype(F32)
            for index in range(got.shape[1]):
                total = total + got[part, index].astype(F32)
            total = total.astype(BF16)
            if stage < 2:
                s.grads[(part, slice(None), *mine)] = total
            else:
                self.result[(self.at.core, part, pl.ds(self.first, self.units), *mine)] = total
        if stage < 2:
            self._direct(self._scatter, stage + 1, stage + 1)
        elif self.spread:
            self._direct(self._gather, 2, 5)

    def gathered(self, stage, hold=False):
        self._arrive(3 + stage)
        if stage == 2:
            self._direct(self._gather, 1, 4)
        elif not hold:
            self.gather_last()

    def gather_last(self):
        if self.ring:
            self.gather_some(0, self.spread)
        else:
            self._direct(self._gather, 0, 3)
            self._pass((0,))

    def gather_some(self, begin, end):
        copies = []
        for part in range(3):
            units = pl.ds(self.first + begin, end - begin)
            place = self.result.at[self.at.core, part, units, self._place(part, 0)]
            copies += [self._remote(place, place, part, 0, 3, distance) for distance in (1, 3)]
        if end == self.spread:
            self._begin(copies, 3)
            self._pass((0,))
        else:
            for copy in copies:
                copy.start()

    def gather_turn(self):
        self._arrive(3)
        copies = []
        for part in range(3):
            for way, distance in enumerate((1, 3)):
                place = self._full(part, self._place(part, 0, 4 - distance), pl.ds(2 * way, 2))
                copies.append(self._remote(place, place, part, 0, BACK, distance))
        self._begin(copies, BACK)
        self._pass((1, 3))

    def gather_done(self):
        self._arrive(BACK if self.ring else 3)
        self._pass((2,) if self.ring else (1, 2, 3))

    def _pass(self, distances):
        sems = self.s.sems
        for part in range(3):
            for distance in distances:
                place = self._full(part, self._place(part, 0, distance))
                remote(place, place, sems.at[6, 0], sems.at[6, 1], self.at.partner()).start()
        if 2 in distances:
            self.at.coming[(self.kind, 6)] = lambda: self._whole(6).wait_recv()
            self.at.sending.append(lambda: self._whole(6).wait_send())


def vmem(**shapes):
    return {name: pltpu.VMEM(shape, kind) for name, (shape, kind) in shapes.items()}


def layer_scratch(index, rows):
    length, half = SEQ * rows, padded(rows)
    message = rows + (NOTE if index == 0 else 0)
    shapes = vmem(
        kv_out=((8, message, 128), BF16), kv_in=((SEQ, message, 128), BF16),
        q_out=((8, half, 128), BF16), q_in=((8, half, 128), BF16),
        dm_out=((8, half, 128), BF16), dm_in=((8, half, 128), BF16),
        mix_out=((8, half, 128), BF16), mix_in=((8, half, 128), BF16),
        dq_out=((8, half, 128), BF16), dq_in=((8, half, 128), BF16),
        dkv_out=((16 if index else 8, rows, 128), BF16), dkv_in=((2, 8, rows, 128) if index else (8, rows, 128), BF16),
        query=((8, rows, 128), BF16), key=((length, 128), BF16), value=((length, 128), BF16),
        expo=((rows, sum(COUNTS)) if index == 0 else (8 * rows, length), BF16), part=((8, rows, 128) if index else (rows, 128), F32),
        normal=((2, rows, D), F32), scale=((2, rows, 128), F32),
        dfirst=((rows, D), F32),
        n1=((rows, D), BF16), n2=((rows, D), BF16), mixed=((rows, D), BF16), glow=((rows, D), BF16),
        act=((2, rows, FF // 2), BF16), dhid=((2, rows, FF // 2), BF16),
        dv1=((2, rows, 256), BF16), dproj=((2, rows, 768), BF16),
        n1_in=((rows, D), BF16), n2_in=((rows, D), BF16), mixed_in=((rows, D), BF16), glow_in=((rows, D), BF16),
        act_in=((rows, FF // 2), BF16), dhid_in=((rows, FF // 2), BF16),
        dv1_in=((rows, 256), BF16), dproj_in=((rows, 768), BF16),
        column=((8, rows, 128) if index else (rows, 128), F32), line=((8, length), F32),
    )
    if not index:
        shapes.update(vmem(dkv_part=((2, 8, rows, 128), BF16), dkv_other=((8, rows, 128), BF16)))
    shapes.update(sems=pltpu.SemaphoreType.DMA((28 if index else 44,)))
    return shapes


def total_scratch(units, rows):
    ways = 2 if units > 1 else 3
    shapes = vmem(
        grads=((3, units, 4, 4, 4, 16, 128), BF16), part0=((3, ways, units, 4, 4, 16, 128), BF16),
        part1=((3, 3, units, 4, 16, 128), BF16), part2=((3, 3, units, 16, 128), BF16),
    )
    if units > 1:
        shapes.update(vmem(hop=((3, 2, units, 2, 4, 16, 128), BF16)))
    shapes.update(sems=pltpu.SemaphoreType.DMA((rows, 2)))
    return shapes


def common_scratch():
    shapes = vmem(
        tokens=((LONG, D), BF16), cot=((LONG, D), BF16), seg=((1, LONG), jnp.int32), gains=((2, 2, D), BF16),
        offsets=((2, LONG, 128), F32), firsts=((2, 2 * SEQ, 128), F32),
        wqkv=((2, D, 3 * D), BF16), wout=((2, D, D), BF16),
        wup=((2, D, FF), BF16), wdown=((2, FF, D), BF16),
        dkey=((SEQ * LONG, 128), F32), dvalue=((SEQ * LONG, 128), F32),
        second=((4, LONG + 16, 128), F32), share=((4, SHORT + 8, 128), F32),
        work=((4, LONG + 8, 128), F32),
        ahead=((4, 8, 128), F32), before=((EXTRA, D), BF16),
        tail_out=((8, EXTRA, 128), BF16), tail_in=((8, EXTRA, 128), BF16),
        output=((LONG, D), BF16), result=((LONG, D), F32),
        gsum=((8, D), F32), gain_in=((4, 4, 8, D), F32), gain_out=((3, 8, D), F32),
    )
    shapes.update(more=pltpu.SemaphoreType.DMA((29,)))
    return shapes


SPACES = (
    common_scratch(), layer_scratch(0, LONG), layer_scratch(1, SHORT),
    *(total_scratch(units, rows) for units, rows in zip(UNITS, (9, 9, 3, 7))),
)


def body(*refs):
    spaces, place = [], 14
    for part in SPACES:
        spaces.append(types.SimpleNamespace(**dict(zip(part, refs[place : place + len(part)]))))
        place += len(part)
    at = Place()
    steps(at, spaces, *refs[:14])
    for wait in at.coming.values():
        wait()
    for wait in at.sending:
        wait()


def steps(
    at, spaces, tokens, seg, wqkv, wout, wup, wdown, gains, cot, offsets, firsts,
    output, tokens_grad, sums, gain_sum,
):
    ref = spaces[0]
    more = ref.more
    full, short = Layer(at, ref, spaces[1], 0, LONG), Layer(at, ref, spaces[2], 1, SHORT)
    for kind in range(4):
        spaces[3 + kind].first = sum(UNITS[:kind])
    early, middle, minor, late = (Total(at, spaces[3 + kind], 20 + kind, sums) for kind in range(4))

    pairs = [
        (tokens, ref.tokens), (gains, ref.gains), (wqkv.at[0], ref.wqkv.at[0]),
        (offsets, ref.offsets), (firsts, ref.firsts), (seg, ref.seg),
        (wout.at[0], ref.wout.at[0]), (wup.at[0], ref.wup.at[0]), (wdown.at[0], ref.wdown.at[0]),
        (wqkv.at[1], ref.wqkv.at[1]), (cot, ref.cot),
        (wout.at[1], ref.wout.at[1]), (wup.at[1], ref.wup.at[1]), (wdown.at[1], ref.wdown.at[1]),
    ]
    loads = [pltpu.make_async_copy(src, dst, more.at[step]) for step, (src, dst) in enumerate(pairs)]
    for load in loads:
        load.start()
    waiting = list(range(len(loads)))

    def loaded(count):
        while waiting and waiting[0] < count:
            loads[waiting.pop(0)].wait()

    at.sending.append(lambda: loaded(len(loads)))
    barrier = pltpu.get_barrier_semaphore()
    greeted = at.greet(barrier)

    loaded(6)
    inputs = ref.tokens[...].astype(F32)
    def ready():
        line = ref.seg[...].astype(F32)
        high = jnp.floor(line * (1.0 / 64.0))
        rows = jnp.concatenate([high, line - 64.0 * high, jnp.zeros((6, LONG), F32)], 0)
        third = jnp.where(sublanes((LONG, 128)) == 3 * lanes((LONG, 128)), 1.0, 0.0)
        picked = dot(rows, third)
        wide = jnp.concatenate([rows[:, 128:], jnp.zeros((8, 112), F32)], 1)
        note = jnp.concatenate([rows[0:2, :128], wide[0:2], picked[0:2], jnp.zeros((10, 128), F32)], 0)
        for head in range(8):
            full.s.kv_out[head, LONG:] = note.astype(BF16)
        pl.semaphore_wait(barrier, greeted)
        at.start(
            remote(ref.tokens.at[pl.ds(LONG - EXTRA, EXTRA)], ref.before, more.at[17], more.at[18], at.along(1)), (3, 0)
        )

    full.project(inputs, ready)

    def segments():
        notes = [full.s.kv_in[block, LONG:, :].astype(F32) for block in range(SEQ)]
        for block, code in enumerate(notes):
            long = jnp.concatenate([64.0 * code[0:1] + code[1:2], 64.0 * code[2:3, :16] + code[3:4, :16]], 1)
            full.s.line[0:1, LONG * block : LONG * block + LONG] = long
            short.s.line[0:1, SHORT * block : SHORT * block + SHORT] = (64.0 * code[4:5] + code[5:6])[:, :SHORT]
        for layer in (full, short):
            rows = layer.rows
            equal = lanes((rows, rows)) == sublanes((rows, rows))
            for pair in range(8):
                code = full.s.kv_in[2 * pair + at.core, LONG:, :].astype(F32)
                if layer is full:
                    line = jnp.concatenate([64.0 * code[0:1] + code[1:2], 64.0 * code[2:3, :16] + code[3:4, :16]], 1)
                else:
                    line = (64.0 * code[4:5] + code[5:6])[:, :SHORT]
                column = jnp.sum(jnp.where(equal, line, 0.0), 1, keepdims=True)
                if layer is full:
                    layer.s.column[:, pair : pair + 1] = column
                else:
                    layer.s.column[pair] = jnp.broadcast_to(column, (rows, 128))

    def attention(layer):
        layer.receive_keys()
        if layer is full:
            segments()
        layer.split_heads()
        layer.receive(Q)
        layer.attend()
        layer.receive(MIX)
        if layer is full:
            layer.receive(TAIL)

    attention(full)
    loaded(9)
    second = ref.second
    at.coming.pop((3, 0))()
    wide = full.feed_forward(jnp.concatenate([inputs, ref.before[...].astype(F32)], 0))
    spill(second, 8, wide[:LONG])
    spill(second, 0, jnp.where(at.seq == 0, 0.0, wide[LONG + EXTRA - 8 :]))
    full.swap(AHEAD)
    loaded(11)
    pooled = jnp.concatenate(
        [
            (every_third(second, 6, g) + every_third(second, 7, g) + every_third(second, 8, g)) / 3.0
            for g in range(GROUPS)
        ],
        1,
    )
    short.project(pooled)
    loaded(14)
    work = ref.work
    spill(work, 0, ref.cot[...].astype(F32))
    grad_short = jnp.concatenate(
        [every_third(work, 0, g) + every_third(work, 1, g) + every_third(work, 2, g) for g in range(GROUPS)], 1
    )
    attention(short)
    result = short.feed_forward(pooled)
    short.swap(AHEAD)

    def backward(layer, total, grad, between):
        layer.feed_back(grad)
        between(0)
        layer.swapped(AHEAD)
        for which in BEHIND:
            layer.swapped((which,))
        layer.grads_feed(total)
        between(1)
        layer.receive(DM)
        layer.attend_back(between)
        if layer is full:
            layer.merge(0)
            layer.send_rest(DKV)
        else:
            layer.send(DKV)
        between(4)
        layer.receive(DQ)
        layer.receive(DKV)
        between(6)
        back = layer.project_back()
        layer.swap((7,))
        return back

    def finish_output():
        for group in range(GROUPS):
            at_lanes = slice(128 * group, 128 * group + 128)
            for step in range(3):
                second[group, pl.ds(8 + step, SHORT, 3), :] = every_third(second, 8 + step, group) + result[:, at_lanes]
            ref.output[:, at_lanes] = second[group, 8 : 8 + LONG, :].astype(BF16)
        store = pltpu.make_async_copy(ref.output, output, more.at[14])
        store.start()
        at.sending.append(store.wait)

    def between_short(point):
        if point == 0:
            finish_output()
        elif point == 1:
            early.scatter()
        elif point == 4:
            early.turn()

    share = ref.share
    spill(share, 0, backward(short, early, grad_short, between_short) * (1.0 / 3.0))

    def halo_back():
        return remote(share.at[:, pl.ds(0, 8), :], ref.ahead, more.at[19], more.at[20], at.along(SEQ - 1))

    at.start(halo_back(), (3, 1))
    short.swapped((7,))
    short.grads_attention(minor, 0)
    at.finish(halo_back(), (3, 1))
    share[:, SHORT:, :] = jnp.where(at.seq == SEQ - 1, 0.0, ref.ahead[...])
    for group in range(GROUPS):
        own, following = share[group, 0:SHORT, :], share[group, 1 : SHORT + 1, :]
        for step, piece in enumerate((own, following, following)):
            work[group, pl.ds(step, SHORT, 3), :] = every_third(work, step, group) + piece
    grad_full = jnp.concatenate([work[group, :LONG, :] for group in range(GROUPS)], 1)

    def between_full(point):
        if point == 0:
            early.scattered(0)
        elif point == 1:
            middle.scatter()
            minor.scatter()
        elif point == 17:
            early.scattered(1)
        elif point == 14:
            middle.turn()
        elif point == 13:
            early.scattered(2)
        elif point == 11:
            minor.scattered(0)
        elif point == 4:
            middle.scattered(0)
            early.gathered(2)
            minor.scattered(1)

    ref.result[...] = backward(full, middle, grad_full, between_full)
    store = pltpu.make_async_copy(ref.result, tokens_grad, more.at[15])
    store.start()
    at.sending.append(store.wait)
    full.swapped((7,))
    full.grads_attention(late, 0)
    late.scatter()
    gsum, gain_in, gain_out = ref.gsum, ref.gain_in, ref.gain_out

    def gain_copy(axis, distance):
        src = gsum if axis == 0 else gain_out.at[axis - 1]
        return remote(src, gain_in.at[axis, at.at[axis]], more.at[23 + axis], more.at[26 + axis], at.peer(axis, distance))

    def gain_step(axis):
        for distance in (1, 2, 3):
            gain_copy(axis, distance).start()
        gain_in[axis, at.at[axis]] = gsum[...] if axis == 0 else gain_out[axis - 1]
        three = gain_in.at[axis, pl.ds(0, 3)]
        copies = remote(three, three, more.at[23 + axis], more.at[26 + axis], at.partner())
        at.coming[(4, axis)] = copies.wait_recv
        at.sending.append(copies.wait_send)

    def gain_done(axis):
        at.coming.pop((4, axis))()
        return (gain_in[axis, 0] + gain_in[axis, 1]) + (gain_in[axis, 2] + gain_in[axis, 3])

    gsum[4:, :] = jnp.zeros((4, D), F32)
    gain_step(0)
    middle.scattered(1)
    minor.scattered(2)
    early.gathered(1)
    late.scattered(0)
    middle.scattered(2)
    late.scattered(1)
    middle.gathered(2)
    gain_out[0] = gain_done(0)
    gain_step(1)
    late.scattered(2)
    early.gather_turn()
    middle.gathered(1, True)
    middle.gather_some(0, 2)
    late.gathered(2)
    gain_out[1] = gain_done(1)
    gain_step(2)
    middle.gather_some(2, 4)
    late.gathered(1)
    early.gather_done()
    middle.gather_turn()
    gain_in[3, 0] = gain_done(2)
    gain_swap = remote(gain_in.at[3, 0], gain_in.at[3, 1], more.at[21], more.at[22], at.partner())
    at.start(gain_swap, (4, 3, 0))
    late.gather_done()
    middle.gather_done()
    at.finish(gain_swap, (4, 3, 0))
    gain_out[2] = gain_in[3, 0] + gain_in[3, 1]
    store = pltpu.make_async_copy(gain_out.at[2], gain_sum, more.at[16])
    store.start()
    at.sending.append(store.wait)


def tables():
    freq = 10000.0 ** (-np.arange(32) / 32.0)
    freq = np.tile(freq, 4)[None, :]
    offset = np.arange(LONG)[:, None] * freq
    first = np.concatenate([np.arange(SEQ) * LONG, np.arange(SEQ) * SHORT])[:, None] * freq
    return (
        np.stack([np.cos(offset), np.sin(offset)]).astype(np.float32),
        np.stack([np.cos(first), np.sin(first)]).astype(np.float32),
    )


def widen_body(
    sums, gain, output, grad, qkv, out, up, down, gains, output_too, grad_too,
    gain_in, gain_out, output_in, grad_in, down_out, up_out, out_out, qkv_out, sems,
):
    small = [
        pltpu.make_async_copy(gain, gain_in, sems.at[0, 0]),
        pltpu.make_async_copy(output, output_in, sems.at[0, 1]),
        pltpu.make_async_copy(grad, grad_in, sems.at[0, 2]),
    ]
    stores = []
    for copy in small:
        copy.start()

    def put(dst, src, slot):
        copy = pltpu.make_async_copy(src, dst, sems.at[1 + slot // 8, slot % 8])
        copy.start()
        stores.append(copy)

    def tiles(kind, half, unit):
        return sums.at[half, unit // UNITS[kind], sum(UNITS[:kind]) + unit % UNITS[kind]]

    def rows_of(kind, half, unit, dst, first_row):
        ref = tiles(kind, half, unit)
        for group in range(4):
            values = ref[group].reshape(256, 128).astype(F32)
            dst[first_row : first_row + 256, 128 * group : 128 * group + 128] = values

    def columns_of(kind, half, unit, dst, column):
        ref = tiles(kind, half, unit)
        for group in range(2):
            values = ref[2 * group : 2 * group + 2].reshape(512, 128).astype(F32)
            dst[:, column + 128 * group : column + 128 * group + 128] = values

    def feed(kind, half, block):
        at = 2 * block + half
        for unit in range(4):
            rows_of(kind, half, unit, down_out.at[at], 256 * unit)
        put(down.at[block, pl.ds(1024 * half, 1024), :], down_out.at[at], at)

    def rest(kind, block, kind_heads, unit):
        for half in range(2):
            for part in range(4):
                columns_of(kind, half, 4 + part, up_out.at[block], 1024 * half + 256 * part)
        put(up.at[block], up_out.at[block], 4 + block)
        for half in range(2):
            columns_of(kind, half, 8, out_out.at[block], 256 * half)
        put(out.at[block], out_out.at[block], 6 + block)
        for half in range(2):
            for part in range(3):
                columns_of(kind_heads, half, unit + part, qkv_out.at[block], 768 * half + 256 * part)
        put(qkv.at[block], qkv_out.at[block], 8 + block)

    def through():
        for copy in small:
            copy.wait()
        gain_out[...] = gain_in[0:4, :].reshape(2, 2, D)
        put(gains, gain_out, 10)
        put(output_too.at[0], output_in, 11)
        put(grad_too.at[0], grad_in, 12)

    for kind, block, kind_heads, unit in ((0, 1, 2, 0), (1, 0, 3, 0)):
        for half in range(2):
            feed(kind, half, block)
        rest(kind, block, kind_heads, unit)
        if kind == 0:
            through()
    for copy in stores:
        copy.wait()


def widen(sums, gain, output, grad):
    anywhere, inside = pl.BlockSpec(memory_space=pl.ANY), pl.BlockSpec(memory_space=pltpu.VMEM)
    return pl.pallas_call(
        widen_body,
        out_shape=(
            jax.ShapeDtypeStruct((2, D, 3 * D), F32),
            jax.ShapeDtypeStruct((2, D, D), F32),
            jax.ShapeDtypeStruct((2, D, FF), F32),
            jax.ShapeDtypeStruct((2, FF, D), F32),
            jax.ShapeDtypeStruct((2, 2, D), F32),
            jax.ShapeDtypeStruct((1, LONG, D), BF16),
            jax.ShapeDtypeStruct((1, LONG, D), F32),
        ),
        in_specs=[inside] + [anywhere] * 3,
        out_specs=(anywhere,) * 7,
        scratch_shapes=[
            pltpu.VMEM((8, D), F32),
            pltpu.VMEM((2, 2, D), F32),
            pltpu.VMEM((LONG, D), BF16),
            pltpu.VMEM((LONG, D), F32),
            pltpu.VMEM((4, 1024, 512), F32),
            pltpu.VMEM((2, 512, 2048), F32),
            pltpu.VMEM((2, 512, 512), F32),
            pltpu.VMEM((2, 512, 1536), F32),
            pltpu.SemaphoreType.DMA((3, 8)),
        ],
        compiler_params=pltpu.CompilerParams(vmem_limit_bytes=40 * 2**20),
        name="widen",
    )(
        pltpu.with_memory_space_constraint(sums, pltpu.VMEM),
        *(pltpu.with_memory_space_constraint(array, pltpu.HBM) for array in (gain, output, grad)),
    )


def per_device(tokens, segment, w_qkv, w_out, w_up, w_down, gains, cotangent):
    offsets, firsts = tables()
    anywhere, inside = pl.BlockSpec(memory_space=pl.ANY), pl.BlockSpec(memory_space=pltpu.VMEM)
    output, tokens_grad, sums, gain = pl.pallas_call(
        body,
        out_shape=(
            jax.ShapeDtypeStruct((LONG, D), BF16),
            jax.ShapeDtypeStruct((LONG, D), F32),
            pltpu.VMEM((2, 3, sum(UNITS), 4, 4, 4, 16, 128), BF16),
            jax.ShapeDtypeStruct((8, D), F32),
        ),
        in_specs=[anywhere] * 10,
        out_specs=(anywhere, anywhere, inside, anywhere),
        scratch_shapes=[shape for part in SPACES for shape in part.values()],
        compiler_params=pltpu.CompilerParams(
            collective_id=0, has_side_effects=True, vmem_limit_bytes=51 * 2**20
        ),
        name="layers",
    )(
        tokens[0], segment, w_qkv, w_out, w_up, w_down, gains, cotangent[0],
        jnp.asarray(offsets), jnp.asarray(firsts),
    )
    qkv, out, up, down, gain, output, tokens_grad = widen(sums, gain, output, tokens_grad)
    return output, tokens_grad, qkv, out, up, down, gain


def solution(mesh):
    return jax.shard_map(
        per_device,
        mesh=mesh,
        in_specs=(
            P("row", "seq", None),
            P("row", "seq"),
            P(),
            P(),
            P(),
            P(),
            P(),
            P("row", "seq", None),
        ),
        out_specs=(P("row", "seq", None), P("row", "seq", None), P(), P(), P(), P(), P()),
        check_vma=False,
    )
```
